32 devices in a mesh: stream: 2 (over y), seq: 8 (over z, core), tensor: 2 (over x).
Axes of the slice: x: 2, y: 2, z: 4, core: 2. Of those that a mesh axis runs over, the one named last changes fastest.
Arguments:
- hidden: bfloat16 [2, 1, 4096, 4096], P('stream', None, 'seq', 'tensor'), may hold values from -32 to 32
- norm_gain: float32 [4096], replicated, may hold values from 0.1 to 1.9
- query_weight: bfloat16 [4096, 4096], P('seq', 'tensor'), may hold values from -1 to 1
- key_weight: bfloat16 [4096, 1024], P('seq', 'tensor'), may hold values from -24 to 24
- value_projection_weight: bfloat16 [4096, 1024], P('seq', 'tensor'), may hold values from -0.09375 to 0.09375
- out_weight: bfloat16 [4096, 4096], P('tensor', 'seq'), may hold values from -0.125 to 0.125
Outputs:
- cross_out: bfloat16 [2, 1, 4096, 4096], P('stream', None, 'seq', 'tensor')
The draws below stay inside these ranges and needn't reach their ends.
All inputs are finite; a program needn't handle non-finite values.
Results may differ from the reference program's by a relative error of at most 0.014.
The reference program's roundings to bfloat16 on the way count: a program that leaves them out, or rounds other values in their place, can miss the bound.
Values may be sent and summed in bfloat16 or wider, within the bound.
A program may use at most 256 MiB of HBM per device.

```python
import math
import jax
import jax.numpy as jnp
from jax import lax

MODEL_DIM = 4096
QUERY_HEAD_COUNT = 32
KV_HEAD_COUNT = 8
HEAD_DIM = 128
WINDOW_BATCH = 1
FRAME_LENGTH = 4096
N_TENSOR = 2


def draw_hidden(key, part):
    random_subkeys = jax.random.split(jax.random.fold_in(key, 3), 4)
    full_shape = (2, WINDOW_BATCH, FRAME_LENGTH, MODEL_DIM)
    raw_field = jnp.clip(jax.random.normal(random_subkeys[0], full_shape, jnp.float32), -4.0, 4.0)
    lower_log = math.log(0.5)
    upper_log = math.log(2.0)
    feature = jnp.exp(jax.random.uniform(random_subkeys[2], (MODEL_DIM,), jnp.float32, lower_log, upper_log))
    row_scale = jnp.exp(jax.random.uniform(random_subkeys[3], (2, WINDOW_BATCH, FRAME_LENGTH, 1), jnp.float32, lower_log, upper_log))
    hidden_field = raw_field * feature * row_scale
    return hidden_field.astype(jnp.bfloat16)


def weight_pair(key):
    random_subkeys = jax.random.split(jax.random.fold_in(key, 17), 3)
    query_projection_matrix = jnp.clip(jax.random.normal(random_subkeys[0], (MODEL_DIM, QUERY_HEAD_COUNT * HEAD_DIM), jnp.float32), -6.0, 6.0) * MODEL_DIM ** (-0.5)
    cross_scale = jnp.exp(jax.random.uniform(random_subkeys[2], (KV_HEAD_COUNT,), jnp.float32, math.log(1.5), math.log(4.0)))
    unnormed_keys = jnp.clip(jax.random.normal(random_subkeys[1], (MODEL_DIM, KV_HEAD_COUNT, HEAD_DIM), jnp.float32), -6.0, 6.0) * MODEL_DIM ** (-0.5)
    key_projection_matrix = (unnormed_keys * cross_scale[None, :, None]).reshape(MODEL_DIM, KV_HEAD_COUNT * HEAD_DIM)
    return (query_projection_matrix, key_projection_matrix)


def draw_query_weight(key, part):
    return weight_pair(key)[0].astype(jnp.bfloat16)


def draw_key_weight(key, part):
    return weight_pair(key)[1].astype(jnp.bfloat16)


def spiked(array, rng, source, target, shards_of, factor):
    owner, partner = [(jnp.arange(array.shape[axis_at]) // (array.shape[axis_at] // shards_of)).reshape([-1 if axis == axis_at else 1 for axis in range(array.ndim)]) for axis_at in (source, target)]
    chosen = jax.random.permutation(rng, shards_of)[partner]
    strong = (owner == chosen) | (owner == (partner + shards_of // 2) % shards_of)
    return jnp.where(strong, factor * array, array)


def block_levels(rng, dims, cuts, smallest, high):
    factor_of = 1.0
    for position, blocks in cuts:
        steps = jax.random.uniform(jax.random.fold_in(jax.random.fold_in(rng, 6), position), (blocks,), jnp.float32, smallest / len(cuts), high / len(cuts))
        factor_of = factor_of * jnp.repeat(jnp.exp(steps), dims[position] // blocks).reshape((-1,) + (1,) * (len(dims) - 1 - position))
    return factor_of


def normal_values(rng, extent, spread, reach, cuts=(), kind=jnp.bfloat16):
    entries = jax.random.normal(rng, extent, jnp.float32) * spread
    if len(cuts) > 0:
        entries = block_levels(rng, extent, cuts, -0.22, 0.18) * entries
    return jnp.clip(entries, min=-reach, max=reach).astype(kind)


def heavy_noise(key, dims, deviation, bound, shards, heavy, held_as=jnp.bfloat16):
    values = deviation * jax.random.normal(key, dims, jnp.float32)
    if shards:
        values = values * block_levels(key, dims, shards, -0.22, 0.18)
    return jnp.clip(spiked(values, jax.random.fold_in(key, 3), *heavy), -bound, bound).astype(held_as)


def setup_inputs(seed: int = 0) -> dict:
    streams_of = jax.random.split(jax.random.key(seed), 7)
    return {
        "hidden": draw_hidden(jax.random.fold_in(streams_of[6], 71), 0),
        "norm_gain": jnp.clip(1.0 + 0.18 * jax.random.normal(streams_of[1], (MODEL_DIM,), jnp.float32), 0.1, 1.9),
        "query_weight": draw_query_weight(jax.random.fold_in(streams_of[6], 71), 0),
        "key_weight": draw_key_weight(jax.random.fold_in(streams_of[6], 71), 0),
        "value_projection_weight": normal_values(streams_of[4], (MODEL_DIM, KV_HEAD_COUNT * HEAD_DIM), MODEL_DIM ** -0.5, 0.09375, ((0, 8), (1, 2))),
        "out_weight": heavy_noise(streams_of[5], (QUERY_HEAD_COUNT * HEAD_DIM, MODEL_DIM), (QUERY_HEAD_COUNT * HEAD_DIM) ** -0.5, 0.125, ((0, 2), (1, 8)), (0, 1, 8, 2.0)),
    }


def reference(hidden, norm_gain, query_weight, key_weight, value_projection_weight, out_weight):
    group_repeat = QUERY_HEAD_COUNT // KV_HEAD_COUNT
    widened = hidden.astype(jnp.float32)
    inverse_rms = lax.rsqrt(lax.optimization_barrier(jnp.mean(widened * widened, axis=-1, keepdims=True)) + 1e-05)
    normed = (widened * inverse_rms * norm_gain).astype(jnp.bfloat16)
    flattened = normed.reshape(-1, MODEL_DIM)
    query_rows = jnp.dot(flattened, query_weight, preferred_element_type=jnp.float32).astype(jnp.bfloat16)
    self_key_rows = jnp.dot(flattened, key_weight, preferred_element_type=jnp.float32).astype(jnp.bfloat16)
    self_value_rows = jnp.dot(flattened, value_projection_weight, preferred_element_type=jnp.float32).astype(jnp.bfloat16)
    query_rows = query_rows.reshape(2, WINDOW_BATCH, FRAME_LENGTH, KV_HEAD_COUNT, group_repeat, HEAD_DIM)
    self_key_rows = self_key_rows.reshape(2, WINDOW_BATCH, FRAME_LENGTH, KV_HEAD_COUNT, HEAD_DIM)[::-1]
    self_value_rows = self_value_rows.reshape(2, WINDOW_BATCH, FRAME_LENGTH, KV_HEAD_COUNT, HEAD_DIM)[::-1]
    query_groups = query_rows.transpose(0, 1, 3, 2, 4, 5).reshape(-1, FRAME_LENGTH, group_repeat, HEAD_DIM)
    key_groups = self_key_rows.transpose(0, 1, 3, 2, 4).reshape(-1, FRAME_LENGTH, HEAD_DIM)
    value_groups = self_value_rows.transpose(0, 1, 3, 2, 4).reshape(-1, FRAME_LENGTH, HEAD_DIM)
    positions = jnp.arange(FRAME_LENGTH, dtype=jnp.int32)
    allowed = positions[None, :] <= positions[:, None]

    def one_group(operands):
        query_tile, key_tile, value_tile = operands
        scores = jnp.einsum('frd,gd->rfg', query_tile.astype(jnp.float32), key_tile.astype(jnp.float32)) * HEAD_DIM ** (-0.5)
        scores = jnp.where(allowed[None], scores, -1e+30)
        row_max = lax.optimization_barrier(jnp.max(scores, axis=-1, keepdims=True))
        expo = jnp.where(allowed[None], jnp.exp(scores - row_max), 0.0)
        totals = lax.optimization_barrier(jnp.sum(expo, axis=-1, keepdims=True))
        weights = lax.optimization_barrier(expo.astype(jnp.bfloat16))
        attended_output = jnp.einsum('rfg,gd->rfd', weights.astype(jnp.float32), value_tile.astype(jnp.float32)) / totals
        return attended_output.astype(jnp.bfloat16)
    attended_output = lax.map(one_group, (query_groups, key_groups, value_groups))
    attended_output = attended_output.reshape(2, WINDOW_BATCH, KV_HEAD_COUNT, group_repeat, FRAME_LENGTH, HEAD_DIM).transpose(0, 1, 4, 2, 3, 5)
    attended_output = attended_output.reshape(2 * WINDOW_BATCH * FRAME_LENGTH, QUERY_HEAD_COUNT * HEAD_DIM)
    group_width = QUERY_HEAD_COUNT * HEAD_DIM // N_TENSOR

    def add_share(index, total):
        start = (index * group_width).astype(jnp.int32)
        columns = lax.dynamic_slice_in_dim(attended_output, start, group_width, 1)
        rows = lax.dynamic_slice_in_dim(out_weight, start, group_width, 0)
        share = jnp.dot(columns, rows, preferred_element_type=jnp.float32).astype(jnp.bfloat16)
        share = lax.optimization_barrier(share)
        return total + share.astype(jnp.float32)
    initial = jnp.zeros((2 * WINDOW_BATCH * FRAME_LENGTH, MODEL_DIM), jnp.float32)
    summed = lax.fori_loop(jnp.int32(0), jnp.int32(N_TENSOR), add_share, initial)
    return summed.astype(jnp.bfloat16).reshape(2, WINDOW_BATCH, FRAME_LENGTH, MODEL_DIM)
```

```python
import functools

import jax
import jax.numpy as jnp
from jax import lax
from jax.experimental import pallas as pl
from jax.experimental.pallas import tpu as pltpu
from jax.sharding import PartitionSpec as P

HEAD_DIM = 128
ROW_CHUNKS = 2
KEY_BLOCK = 1024
LOG2E = 1.4426950408889634


def swap_pairs(block, axis):
    count = lax.axis_size(axis)
    return lax.ppermute(block, axis, [(i, i ^ 1) for i in range(count)])


def attend_kernel(repeat, start_ref, q_ref, k_ref, v_ref, o_ref, m_ref, l_ref, acc_ref):
    step = pl.program_id(1)
    rows = q_ref.shape[0]
    keys = k_ref.shape[0]
    start = start_ref[0]
    last = (start + rows - 1) // keys
    scale = LOG2E * HEAD_DIM ** (-0.5)

    @pl.when(step == 0)
    def _():
        m_ref[...] = jnp.full_like(m_ref, -1e30)
        l_ref[...] = jnp.zeros_like(l_ref)
        acc_ref[...] = jnp.zeros_like(acc_ref)

    def update(masked):
        k = k_ref[...]
        v = v_ref[...]
        if masked:
            frame = start + lax.broadcasted_iota(jnp.int32, (keys, rows), 1)
            key = step * keys + lax.broadcasted_iota(jnp.int32, (keys, rows), 0)
            allowed = key <= frame

        def scored(r):
            q = q_ref[:, r * HEAD_DIM:(r + 1) * HEAD_DIM]
            return lax.dot_general(k, q, (((1,), (1,)), ((), ())), preferred_element_type=jnp.float32)

        following = scored(0)
        for r in range(repeat):
            s = following
            if r + 1 < repeat:
                following = scored(r + 1)
            if masked:
                s = jnp.where(allowed, s, -1e30)
            top = jnp.max(s, axis=0, keepdims=True) * scale
            before = m_ref[r]
            fresh = jnp.maximum(before, top)
            m_ref[r] = fresh
            alpha = jnp.exp2(before - fresh)
            p = jnp.exp2(s * scale - fresh)
            l_ref[r] = alpha * l_ref[r] + jnp.sum(p, axis=0, keepdims=True)
            acc_ref[r] = alpha * acc_ref[r] + lax.dot_general(
                v, p.astype(jnp.bfloat16), (((0,), (0,)), ((), ())), preferred_element_type=jnp.float32
            )

    @pl.when(step < last)
    def _():
        update(False)

    @pl.when(step == last)
    def _():
        update(True)
        for r in range(repeat):
            attended = (acc_ref[r] / l_ref[r]).T
            o_ref[:, r * HEAD_DIM:(r + 1) * HEAD_DIM] = attended.astype(o_ref.dtype)


def attend(start, queries, keys_values, repeat):
    rows, width = queries.shape
    count = keys_values.shape[0]
    groups = width // (repeat * HEAD_DIM)
    block = min(KEY_BLOCK, count)

    def at(step, start_ref):
        return jnp.minimum(step, (start_ref[0] + rows - 1) // block)

    return pl.pallas_call(
        functools.partial(attend_kernel, repeat),
        out_shape=jax.ShapeDtypeStruct((rows, width), jnp.bfloat16),
        grid_spec=pltpu.PrefetchScalarGridSpec(
            num_scalar_prefetch=1,
            grid=(groups, count // block),
            in_specs=[
                pl.BlockSpec((rows, repeat * HEAD_DIM), lambda g, i, s: (0, g)),
                pl.BlockSpec((block, HEAD_DIM), lambda g, i, s: (at(i, s), g)),
                pl.BlockSpec((block, HEAD_DIM), lambda g, i, s: (at(i, s), groups + g)),
            ],
            out_specs=pl.BlockSpec((rows, repeat * HEAD_DIM), lambda g, i, s: (0, g)),
            scratch_shapes=[
                pltpu.VMEM((repeat, 1, rows), jnp.float32),
                pltpu.VMEM((repeat, 1, rows), jnp.float32),
                pltpu.VMEM((repeat, HEAD_DIM, rows), jnp.float32),
            ],
        ),
        compiler_params=pltpu.CompilerParams(
            dimension_semantics=("arbitrary", "arbitrary"), vmem_limit_bytes=32 * 1024 * 1024
        ),
        cost_estimate=pl.CostEstimate(
            flops=8 * rows * count * width,
            bytes_accessed=2 * (2 * rows * width + keys_values.size),
            transcendentals=rows * count * width // HEAD_DIM,
        ),
    )(start.reshape(1), queries, keys_values, keys_values)


SUBS = 4


def line_order(z):
    first = z - 1 + 2 * ((3 - z) // 3)
    third = 3 * (1 - z // 2)
    return (z, first, 6 - z - first - third, third)


def remote(src, dst, send, recv, device):
    return pltpu.make_async_remote_copy(
        src_ref=src, dst_ref=dst, send_sem=send, recv_sem=recv, device_id=device, device_id_type=pl.DeviceIdType.MESH
    )


def greet(z, last, devices, up, down):
    barrier = pltpu.get_barrier_semaphore()

    def hello(device):
        pl.semaphore_signal(barrier, inc=1, device_id=device, device_id_type=pl.DeviceIdType.MESH)

    for device in devices:
        hello(device)

    @pl.when(z < last)
    def _():
        hello(up)

    @pl.when(z > 0)
    def _():
        hello(down)

    inner = jnp.where((z > 0) & (z < last), 1, 0)
    pl.semaphore_wait(barrier, len(devices) + 1 + inner)


def project_kernel(
    gain_ref, hidden_ref, wq_ref, wk_ref, wv_ref, q_ref, kv_ref,
    w, hid, normed, acc,
    local_sem, x_s, x_r, z_s, z_r, y_s, y_r, c_s, c_r, own_s, own_r,
):
    last = 3
    c = lax.axis_index("stream")
    s = lax.axis_index("seq")
    t = lax.axis_index("tensor")
    z, k = s // 2, s % 2
    depth = wq_ref.shape[0]
    half = depth // 2
    rows = half // SUBS
    q_width, kv_width = wq_ref.shape[1], wk_ref.shape[1]
    frames = hid.shape[1]
    step = frames // SUBS
    at = {"stream": c, "seq": s, "tensor": t}
    up, down = {**at, "seq": s + 2}, {**at, "seq": s - 2}
    beside, mate, across = {**at, "stream": 1 - c}, {**at, "seq": 2 * z + 1 - k}, {**at, "tensor": 1 - t}
    greet(z, last, (beside, mate, across), up, down)

    own = pl.multiple_of(s * depth, depth)
    fills = [
        pltpu.make_async_copy(wq_ref, w.at[pl.ds(own, depth), pl.ds(0, q_width)], local_sem.at[0]),
        pltpu.make_async_copy(wk_ref, w.at[pl.ds(own, depth), pl.ds(q_width, kv_width)], local_sem.at[1]),
        pltpu.make_async_copy(wv_ref, w.at[pl.ds(own, depth), pl.ds(q_width + kv_width, kv_width)], local_sem.at[2]),
    ]
    mine = pltpu.make_async_copy(hidden_ref, hid.at[t], local_sem.at[3])
    for copy in fills:
        copy.start()
    mine.start()

    def crossing(piece):
        start = pl.multiple_of(piece * step, step)
        return remote(
            hidden_ref.at[pl.ds(start, step)], hid.at[t, pl.ds(start, step)], x_s.at[piece], x_r.at[piece], across
        )

    for piece in range(SUBS):
        crossing(piece).start()
    for copy in fills:
        copy.wait()

    def part(source, core, side, sub):
        start = pl.multiple_of(source * (2 * depth) + core * depth + side * half + sub * rows, rows)
        return w.at[pl.ds(start, rows)]

    def source(way, hop):
        return z - hop if way == 0 else z + hop

    def along(way, hop, sub):
        view = part(source(way, hop), k, c, sub)
        return remote(view, view, z_s.at[way, hop, sub], z_r.at[way, hop, sub], up if way == 0 else down)

    def sideways(way, hop, sub):
        view = part(source(way, hop), k, c, sub)
        return remote(view, view, y_s.at[way, hop - 1, sub], y_r.at[way, hop - 1, sub], beside)

    def inward(way, kind, hop, sub):
        view = part(source(way, hop), k, c if kind == 0 else 1 - c, sub)
        return remote(view, view, c_s.at[way, kind, hop - 1, sub], c_r.at[way, kind, hop - 1, sub], mate)

    sends = (z < last, z > 0)

    def arrives(way, hop):
        return z >= hop if way == 0 else z + hop <= last

    def each_sub(action):
        @pl.loop(0, SUBS)
        def _(sub):
            action(sub)

    def leave(sub):
        for way in range(2):
            @pl.when(sends[way])
            def _():
                along(way, 0, sub).start()

    each_sub(leave)
    block = w.at[pl.ds(own, depth)]
    share = remote(block, block, own_s, own_r, mate)
    share.start()

    def pass_on(hop, sub):
        for way in range(2):
            @pl.when(arrives(way, hop))
            def _():
                along(way, hop - 1, sub).wait_recv()
                if hop < last:
                    @pl.when(sends[way])
                    def _():
                        along(way, hop, sub).start()
                sideways(way, hop, sub).start()
                inward(way, 0, hop, sub).start()

    def pass_in(hop, sub):
        for way in range(2):
            @pl.when(arrives(way, hop))
            def _():
                sideways(way, hop, sub).wait_recv()
                inward(way, 1, hop, sub).start()

    def gathered(hop):
        def action(sub):
            for way in range(2):
                @pl.when(arrives(way, hop))
                def _():
                    inward(way, 0, hop, sub).wait_recv()
                    inward(way, 1, hop, sub).wait_recv()

        each_sub(action)

    tall = 16

    def norm(sub):
        crossing(sub).wait_recv()

        @pl.loop(0, step // tall)
        def _(i):
            at_rows = pl.ds(pl.multiple_of(sub * step + i * tall, tall), tall)
            low = hid[0, at_rows, :].astype(jnp.float32)
            high = hid[1, at_rows, :].astype(jnp.float32)
            total = jnp.sum(low * low, axis=1, keepdims=True) + jnp.sum(high * high, axis=1, keepdims=True)
            inverse_rms = lax.rsqrt(total / (2 * low.shape[1]) + 1e-05)
            wide = normed.shape[2]
            for group in range(4):
                x = (low if group < 2 else high)[:, (group % 2) * wide:(group % 2 + 1) * wide]
                gain = gain_ref[:, group * wide:(group + 1) * wide]
                normed[group, at_rows, :] = (x * inverse_rms * gain).astype(jnp.bfloat16)

    order = line_order(z)
    tile = min(512, kv_width)

    def dot(place, index):
        group = order[place]
        columns = pl.ds(pl.multiple_of(index * tile, tile), tile)
        return jnp.dot(
            normed[group],
            w[pl.ds(pl.multiple_of(group * 2 * depth, 2 * depth), 2 * depth), columns],
            preferred_element_type=jnp.float32,
        ), columns

    def project(place, low, high):
        @pl.loop(low, high)
        def _(index):
            value, columns = dot(place, index)
            if place == 0:
                acc[:, columns] = value
            else:
                acc[:, columns] += value

    tiles = (q_width + 2 * kv_width) // tile

    each_sub(lambda sub: pass_on(1, sub))
    mine.wait()

    def second(sub):
        pass_on(2, sub)
        pass_in(1, sub)
        norm(sub)

    each_sub(second)
    share.wait_recv()
    gathered(1)
    cut = tiles // 2
    for sub in range(SUBS):
        pass_on(3, sub)
        pass_in(2, sub)
        low = (sub % 2) * cut
        project(sub // 2, low, low + cut if sub % 2 == 0 else tiles)
    each_sub(lambda sub: pass_in(3, sub))
    gathered(2)
    project(2, 0, tiles)
    gathered(3)

    @pl.loop(0, q_width // tile)
    def _(index):
        value, columns = dot(3, index)
        q_ref[:, columns] = (acc[:, columns] + value).astype(jnp.bfloat16)

    for index in range(2 * kv_width // tile):
        value, columns = dot(3, q_width // tile + index)
        kv_ref[:, index * tile:(index + 1) * tile] = (acc[:, columns] + value).astype(jnp.bfloat16)

    share.wait_send()

    def settle(sub):
        crossing(sub).wait_send()
        for way in range(2):
            for hop in range(last):
                @pl.when(sends[way] & (arrives(way, hop) if hop else True))
                def _():
                    along(way, hop, sub).wait_send()
            for hop in range(1, last + 1):
                @pl.when(arrives(way, hop))
                def _():
                    sideways(way, hop, sub).wait_send()
                    inward(way, 0, hop, sub).wait_send()
                    inward(way, 1, hop, sub).wait_send()

    each_sub(settle)


def projected(hidden, norm_gain, query_weight, key_weight, value_weight):
    frames, features = hidden.shape
    depth, q_width = query_weight.shape
    kv_width = key_weight.shape[1]
    total = q_width + 2 * kv_width
    dma = pltpu.SemaphoreType.DMA
    anywhere = pl.BlockSpec(memory_space=pl.ANY)
    vmem = pl.BlockSpec(memory_space=pltpu.VMEM)
    return pl.pallas_call(
        project_kernel,
        out_shape=(
            jax.ShapeDtypeStruct((frames, q_width), jnp.bfloat16),
            jax.ShapeDtypeStruct((frames, 2 * kv_width), jnp.bfloat16),
        ),
        in_specs=[vmem] + [anywhere] * 4,
        out_specs=(vmem, vmem),
        scratch_shapes=[
            pltpu.VMEM((8 * depth, total), jnp.bfloat16),
            pltpu.VMEM((2, frames, features), jnp.bfloat16),
            pltpu.VMEM((4, frames, features // 2), jnp.bfloat16),
            pltpu.VMEM((frames, total), jnp.float32),
            dma((4,)), dma((SUBS,)), dma((SUBS,)),
            dma((2, 3, SUBS)), dma((2, 3, SUBS)),
            dma((2, 3, SUBS)), dma((2, 3, SUBS)),
            dma((2, 2, 3, SUBS)), dma((2, 2, 3, SUBS)),
            dma, dma,
        ],
        compiler_params=pltpu.CompilerParams(
            collective_id=0, has_side_effects=True, vmem_limit_bytes=58 * 1024 * 1024
        ),
        cost_estimate=pl.CostEstimate(
            flops=2 * frames * 8 * depth * total, bytes_accessed=4 * hidden.size, transcendentals=frames
        ),
    )(norm_gain.reshape(1, -1), hidden, query_weight, key_weight, value_weight)


def y_share(mine, core, after=None):
    depth = mine.shape[0] // 2
    part = lax.dynamic_slice_in_dim(mine, core * depth, depth, 0)
    near = lax.ppermute(part, "stream", [(0, 1), (1, 0)])
    if after is None:
        return near, swap_pairs(near, "seq")
    near, after = lax.optimization_barrier((near, after))
    return near, swap_pairs(near, "seq"), after


def fits(hidden, query_weight, key_weight):
    meshes = (lax.axis_size("stream"), lax.axis_size("seq"), lax.axis_size("tensor"))
    rows = hidden.shape[1] * hidden.shape[2]
    return (
        meshes == (2, 8, 2)
        and hidden.shape[1] == 1
        and rows == 512
        and query_weight.shape == (512, 2048)
        and key_weight.shape == (512, 512)
    )


def body(hidden, norm_gain, query_weight, key_weight, value_projection_weight, out_weight):
    windows, frame_count = hidden.shape[1], hidden.shape[2]
    n_tensor = lax.axis_size("tensor")
    n_seq = lax.axis_size("seq")
    stream = lax.axis_index("stream")
    tensor = lax.axis_index("tensor")
    seq = lax.axis_index("seq")
    core = seq % 2
    rows = windows * frame_count
    depth = query_weight.shape[0] // 2
    out_half = out_weight.shape[1] // 2

    fast = fits(hidden, query_weight, key_weight)
    kv_weight = jnp.concatenate([key_weight, value_projection_weight], axis=1)
    kv_mine = lax.all_gather(
        lax.dynamic_slice_in_dim(kv_weight, stream * depth, depth, 0), "seq", axis=0, tiled=True
    )
    query_mine = lax.all_gather(
        lax.dynamic_slice_in_dim(query_weight, stream * depth, depth, 0), "seq", axis=0, tiled=True
    )
    out_mine = lax.all_gather(
        lax.dynamic_slice_in_dim(out_weight, stream * out_half, out_half, 1), "seq", axis=1, tiled=True
    )

    local = hidden.reshape(rows, hidden.shape[3])
    if n_tensor == 2:
        other = lax.ppermute(local, "tensor", [(0, 1), (1, 0)])
        gathered = jnp.where(
            tensor == 0,
            jnp.concatenate([local, other], axis=1),
            jnp.concatenate([other, local], axis=1),
        )
    else:
        gathered = lax.all_gather(local, "tensor", axis=1, tiled=True)
    flat = gathered.astype(jnp.float32)
    inverse_rms = lax.rsqrt(jnp.mean(flat * flat, axis=1, keepdims=True) + 1e-05)
    normed = (flat * inverse_rms * norm_gain).astype(jnp.bfloat16)
    split = normed.reshape(rows, n_seq, 2, depth)

    def features(half):
        return lax.dynamic_index_in_dim(split, half, 2, keepdims=False).reshape(rows, n_seq * depth)

    normed_mine = features(stream)
    normed_other = features(1 - stream)
    span = n_seq * depth // 2
    normed_near = lax.dynamic_slice_in_dim(normed_other, core * span, span, 1)
    normed_far = lax.dynamic_slice_in_dim(normed_other, (1 - core) * span, span, 1)

    def project(mine, near, far):
        total = jnp.dot(normed_mine, mine, preferred_element_type=jnp.float32)
        total += jnp.dot(normed_near, near, preferred_element_type=jnp.float32)
        total += jnp.dot(normed_far, far, preferred_element_type=jnp.float32)
        return total.astype(jnp.bfloat16)

    if fast:
        queries, keys_values = projected(
            local, norm_gain, query_weight, key_weight, value_projection_weight
        )
        queries = queries.reshape(windows, frame_count, -1)
    else:
        keys_values = project(kv_mine, *y_share(kv_mine, core))
    partner = lax.ppermute(keys_values, "stream", [(0, 1), (1, 0)])
    kv_width = key_weight.shape[1]
    parts = 2 if kv_width % (2 * HEAD_DIM) == 0 else 1
    step = kv_width // parts
    pieces = []
    for part in range(parts):
        columns = jnp.concatenate(
            [partner[:, part * step:(part + 1) * step],
             partner[:, kv_width + part * step:kv_width + (part + 1) * step]],
            axis=1,
        )
        pieces.append(
            lax.all_gather(columns.reshape(windows, frame_count, 2 * step), "seq", axis=1, tiled=True)
        )
    if not fast:
        queries = project(query_mine, *y_share(query_mine, core)).reshape(windows, frame_count, -1)
    out_near = out_far = None
    width = out_weight.shape[0] // 2

    repeat = query_weight.shape[1] // key_weight.shape[1]
    chunk = frame_count // ROW_CHUNKS

    def scattered(share):
        if n_tensor == 2:
            wide = share.shape[1] // 2
            away = lax.dynamic_slice_in_dim(share, (1 - tensor) * wide, wide, 1)
            kept = lax.dynamic_slice_in_dim(share, tensor * wide, wide, 1)
            came = lax.ppermute(away, "tensor", [(0, 1), (1, 0)])
            return (kept.astype(jnp.float32) + came.astype(jnp.float32)).astype(jnp.bfloat16)
        return lax.psum_scatter(share, "tensor", scatter_dimension=1, tiled=True)

    outs = []
    q_step = step * repeat
    for window in range(windows):
        early = [
            attend(
                seq * frame_count,
                queries[window][:, part * q_step:(part + 1) * q_step],
                pieces[part][window],
                repeat,
            )
            for part in range(parts - 1)
        ]
        for index in range(ROW_CHUNKS):
            low, high = index * chunk, (index + 1) * chunk
            final = attend(
                seq * frame_count + low,
                queries[window][low:high, (parts - 1) * q_step:],
                pieces[-1][window],
                repeat,
            )
            attended = jnp.concatenate([done[low:high] for done in early] + [final], axis=1)
            share_mine = jnp.dot(attended, out_mine, preferred_element_type=jnp.float32)
            if out_near is None:
                out_near, out_far, attended = y_share(out_mine, core, attended)
            attended_near = lax.dynamic_slice_in_dim(attended, core * width, width, 1)
            attended_far = lax.dynamic_slice_in_dim(attended, (1 - core) * width, width, 1)
            share_other = jnp.dot(attended_near, out_near, preferred_element_type=jnp.float32)
            share_other += jnp.dot(attended_far, out_far, preferred_element_type=jnp.float32)
            mine = scattered(share_mine.astype(jnp.bfloat16)).reshape(chunk, -1, out_half)
            other = scattered(share_other.astype(jnp.bfloat16)).reshape(chunk, -1, out_half)
            outs.append(
                jnp.where(
                    stream == 0, jnp.stack([mine, other], axis=2), jnp.stack([other, mine], axis=2)
                ).reshape(chunk, -1)
            )
    return jnp.concatenate(outs, axis=0).reshape(1, windows, frame_count, -1)


def solution(mesh):
    in_specs = (
        P("stream", None, "seq", "tensor"),
        P(),
        P("seq", "tensor"),
        P("seq", "tensor"),
        P("seq", "tensor"),
        P("tensor", "seq"),
    )
    out_specs = P("stream", None, "seq", "tensor")
    return jax.shard_map(body, mesh=mesh, in_specs=in_specs, out_specs=out_specs, check_vma=False)
```

```python
import functools

import jax
import jax.numpy as jnp
from jax import lax
from jax.experimental import pallas as pl
from jax.experimental.pallas import tpu as pltpu
from jax.sharding import PartitionSpec as P

HEAD_DIM = 128
ROW_CHUNKS = 2
KEY_BLOCK = 1024
LOG2E = 1.4426950408889634


def swap_pairs(block, axis):
    count = lax.axis_size(axis)
    return lax.ppermute(block, axis, [(i, i ^ 1) for i in range(count)])


def attend_kernel(repeat, start_ref, q_ref, k_ref, v_ref, o_ref, m_ref, l_ref, acc_ref):
    step = pl.program_id(1)
    rows = q_ref.shape[0]
    keys = k_ref.shape[0]
    start = start_ref[0]
    last = (start + rows - 1) // keys
    scale = LOG2E * HEAD_DIM ** (-0.5)

    @pl.when(step == 0)
    def _():
        m_ref[...] = jnp.full_like(m_ref, -1e30)
        l_ref[...] = jnp.zeros_like(l_ref)
        acc_ref[...] = jnp.zeros_like(acc_ref)

    def update(masked):
        k = k_ref[...]
        v = v_ref[...]
        if masked:
            frame = start + lax.broadcasted_iota(jnp.int32, (keys, rows), 1)
            key = step * keys + lax.broadcasted_iota(jnp.int32, (keys, rows), 0)
            allowed = key <= frame

        def scored(r):
            q = q_ref[:, r * HEAD_DIM:(r + 1) * HEAD_DIM]
            return lax.dot_general(k, q, (((1,), (1,)), ((), ())), preferred_element_type=jnp.float32)

        following = scored(0)
        for r in range(repeat):
            s = following
            if r + 1 < repeat:
                following = scored(r + 1)
            if masked:
                s = jnp.where(allowed, s, -1e30)
            top = jnp.max(s, axis=0, keepdims=True) * scale
            before = m_ref[r]
            fresh = jnp.maximum(before, top)
            m_ref[r] = fresh
            alpha = jnp.exp2(before - fresh)
            p = jnp.exp2(s * scale - fresh)
            l_ref[r] = alpha * l_ref[r] + jnp.sum(p, axis=0, keepdims=True)
            acc_ref[r] = alpha * acc_ref[r] + lax.dot_general(
                v, p.astype(jnp.bfloat16), (((0,), (0,)), ((), ())), preferred_element_type=jnp.float32
            )

    @pl.when(step < last)
    def _():
        update(False)

    @pl.when(step == last)
    def _():
        update(True)
        for r in range(repeat):
            attended = (acc_ref[r] / l_ref[r]).T
            o_ref[:, r * HEAD_DIM:(r + 1) * HEAD_DIM] = attended.astype(o_ref.dtype)


def attend(start, queries, keys_values, repeat):
    rows, width = queries.shape
    count = keys_values.shape[0]
    groups = width // (repeat * HEAD_DIM)
    block = min(KEY_BLOCK, count)

    def at(step, start_ref):
        return jnp.minimum(step, (start_ref[0] + rows - 1) // block)

    return pl.pallas_call(
        functools.partial(attend_kernel, repeat),
        out_shape=jax.ShapeDtypeStruct((rows, width), jnp.bfloat16),
        grid_spec=pltpu.PrefetchScalarGridSpec(
            num_scalar_prefetch=1,
            grid=(groups, count // block),
            in_specs=[
                pl.BlockSpec((rows, repeat * HEAD_DIM), lambda g, i, s: (0, g)),
                pl.BlockSpec((block, HEAD_DIM), lambda g, i, s: (at(i, s), g)),
                pl.BlockSpec((block, HEAD_DIM), lambda g, i, s: (at(i, s), groups + g)),
            ],
            out_specs=pl.BlockSpec((rows, repeat * HEAD_DIM), lambda g, i, s: (0, g)),
            scratch_shapes=[
                pltpu.VMEM((repeat, 1, rows), jnp.float32),
                pltpu.VMEM((repeat, 1, rows), jnp.float32),
                pltpu.VMEM((repeat, HEAD_DIM, rows), jnp.float32),
            ],
        ),
        compiler_params=pltpu.CompilerParams(
            dimension_semantics=("arbitrary", "arbitrary"), vmem_limit_bytes=32 * 1024 * 1024
        ),
        cost_estimate=pl.CostEstimate(
            flops=8 * rows * count * width,
            bytes_accessed=2 * (2 * rows * width + keys_values.size),
            transcendentals=rows * count * width // HEAD_DIM,
        ),
    )(start.reshape(1), queries, keys_values, keys_values)


SUBS = 4


def line_order(z):
    first = z - 1 + 2 * ((3 - z) // 3)
    third = 3 * (1 - z // 2)
    return (z, first, 6 - z - first - third, third)


def remote(src, dst, send, recv, device):
    return pltpu.make_async_remote_copy(
        src_ref=src, dst_ref=dst, send_sem=send, recv_sem=recv, device_id=device, device_id_type=pl.DeviceIdType.MESH
    )


def greet(z, last, devices, up, down):
    barrier = pltpu.get_barrier_semaphore()

    def hello(device):
        pl.semaphore_signal(barrier, inc=1, device_id=device, device_id_type=pl.DeviceIdType.MESH)

    for device in devices:
        hello(device)

    @pl.when(z < last)
    def _():
        hello(up)

    @pl.when(z > 0)
    def _():
        hello(down)

    inner = jnp.where((z > 0) & (z < last), 1, 0)
    pl.semaphore_wait(barrier, len(devices) + 1 + inner)


def project_kernel(
    gain_ref, hidden_ref, wq_ref, wk_ref, wv_ref, q_ref, kv_ref,
    w, hid, normed, acc,
    local_sem, x_s, x_r, z_s, z_r, y_s, y_r, c_s, c_r, own_s, own_r,
):
    last = 3
    c = lax.axis_index("stream")
    s = lax.axis_index("seq")
    t = lax.axis_index("tensor")
    z, k = s // 2, s % 2
    depth = wq_ref.shape[0]
    half = depth // 2
    rows = half // SUBS
    q_width, kv_width = wq_ref.shape[1], wk_ref.shape[1]
    frames = hid.shape[1]
    step = frames // SUBS
    at = {"stream": c, "seq": s, "tensor": t}
    up, down = {**at, "seq": s + 2}, {**at, "seq": s - 2}
    beside, mate, across = {**at, "stream": 1 - c}, {**at, "seq": 2 * z + 1 - k}, {**at, "tensor": 1 - t}
    greet(z, last, (beside, mate, across), up, down)

    own = pl.multiple_of(s * depth, depth)
    fills = [
        pltpu.make_async_copy(wq_ref, w.at[pl.ds(own, depth), pl.ds(0, q_width)], local_sem.at[0]),
        pltpu.make_async_copy(wk_ref, w.at[pl.ds(own, depth), pl.ds(q_width, kv_width)], local_sem.at[1]),
        pltpu.make_async_copy(wv_ref, w.at[pl.ds(own, depth), pl.ds(q_width + kv_width, kv_width)], local_sem.at[2]),
    ]
    mine = pltpu.make_async_copy(hidden_ref, hid.at[t], local_sem.at[3])
    for copy in fills:
        copy.start()
    mine.start()

    def crossing(piece):
        start = pl.multiple_of(piece * step, step)
        return remote(
            hidden_ref.at[pl.ds(start, step)], hid.at[t, pl.ds(start, step)], x_s.at[piece], x_r.at[piece], across
        )

    for piece in range(SUBS):
        crossing(piece).start()
    for copy in fills:
        copy.wait()

    def part(source, core, side, sub):
        start = pl.multiple_of(source * (2 * depth) + core * depth + side * half + sub * rows, rows)
        return w.at[pl.ds(start, rows)]

    def source(way, hop):
        return z - hop if way == 0 else z + hop

    def along(way, hop, sub):
        view = part(source(way, hop), k, c, sub)
        return remote(view, view, z_s.at[way, hop, sub], z_r.at[way, hop, sub], up if way == 0 else down)

    def sideways(way, hop, sub):
        view = part(source(way, hop), k, c, sub)
        return remote(view, view, y_s.at[way, hop - 1, sub], y_r.at[way, hop - 1, sub], beside)

    def inward(way, kind, hop, sub):
        view = part(source(way, hop), k, c if kind == 0 else 1 - c, sub)
        return remote(view, view, c_s.at[way, kind, hop - 1, sub], c_r.at[way, kind, hop - 1, sub], mate)

    sends = (z < last, z > 0)

    def arrives(way, hop):
        return z >= hop if way == 0 else z + hop <= last

    def each_sub(action):
        @pl.loop(0, SUBS)
        def _(sub):
            action(sub)

    def leave(sub):
        for way in range(2):
            @pl.when(sends[way])
            def _():
                along(way, 0, sub).start()

    each_sub(leave)
    block = w.at[pl.ds(own, depth)]
    share = remote(block, block, own_s, own_r, mate)
    share.start()

    def pass_on(hop, sub):
        for way in range(2):
            @pl.when(arrives(way, hop))
            def _():
                along(way, hop - 1, sub).wait_recv()
                if hop < last:
                    @pl.when(sends[way])
                    def _():
                        along(way, hop, sub).start()
                sideways(way, hop, sub).start()
                inward(way, 0, hop, sub).start()

    def pass_in(hop, sub):
        for way in range(2):
            @pl.when(arrives(way, hop))
            def _():
                sideways(way, hop, sub).wait_recv()
                inward(way, 1, hop, sub).start()

    def gathered(hop):
        def action(sub):
            for way in range(2):
                @pl.when(arrives(way, hop))
                def _():
                    inward(way, 0, hop, sub).wait_recv()
                    inward(way, 1, hop, sub).wait_recv()

        each_sub(action)

    tall = 16

    def norm(sub):
        crossing(sub).wait_recv()

        @pl.loop(0, step // tall)
        def _(i):
            at_rows = pl.ds(pl.multiple_of(sub * step + i * tall, tall), tall)
            low = hid[0, at_rows, :].astype(jnp.float32)
            high = hid[1, at_rows, :].astype(jnp.float32)
            total = jnp.sum(low * low, axis=1, keepdims=True) + jnp.sum(high * high, axis=1, keepdims=True)
            inverse_rms = lax.rsqrt(total / (2 * low.shape[1]) + 1e-05)
            wide = normed.shape[2]
            for group in range(4):
                x = (low if group < 2 else high)[:, (group % 2) * wide:(group % 2 + 1) * wide]
                gain = gain_ref[:, group * wide:(group + 1) * wide]
                normed[group, at_rows, :] = (x * inverse_rms * gain).astype(jnp.bfloat16)

    order = line_order(z)
    tile = min(512, kv_width)

    def dot(place, index):
        group = order[place]
        columns = pl.ds(pl.multiple_of(index * tile, tile), tile)
        return jnp.dot(
            normed[group],
            w[pl.ds(pl.multiple_of(group * 2 * depth, 2 * depth), 2 * depth), columns],
            preferred_element_type=jnp.float32,
        ), columns

    def project(place, low, high):
        @pl.loop(low, high)
        def _(index):
            value, columns = dot(place, index)
            if place == 0:
                acc[:, columns] = value
            else:
                acc[:, columns] += value

    tiles = (q_width + 2 * kv_width) // tile

    each_sub(lambda sub: pass_on(1, sub))
    mine.wait()

    def second(sub):
        pass_on(2, sub)
        pass_in(1, sub)
        norm(sub)

    each_sub(second)
    share.wait_recv()
    gathered(1)
    cut = tiles // 2
    for sub in range(SUBS):
        pass_on(3, sub)
        pass_in(2, sub)
        low = (sub % 2) * cut
        project(sub // 2, low, low + cut if sub % 2 == 0 else tiles)
    each_sub(lambda sub: pass_in(3, sub))
    gathered(2)
    project(2, 0, tiles)
    gathered(3)

    @pl.loop(0, q_width // tile)
    def _(index):
        value, columns = dot(3, index)
        q_ref[:, columns] = (acc[:, columns] + value).astype(jnp.bfloat16)

    for index in range(2 * kv_width // tile):
        value, columns = dot(3, q_width // tile + index)
        kv_ref[:, index * tile:(index + 1) * tile] = (acc[:, columns] + value).astype(jnp.bfloat16)

    share.wait_send()

    def settle(sub):
        crossing(sub).wait_send()
        for way in range(2):
            for hop in range(last):
                @pl.when(sends[way] & (arrives(way, hop) if hop else True))
                def _():
                    along(way, hop, sub).wait_send()
            for hop in range(1, last + 1):
                @pl.when(arrives(way, hop))
                def _():
                    sideways(way, hop, sub).wait_send()
                    inward(way, 0, hop, sub).wait_send()
                    inward(way, 1, hop, sub).wait_send()

    each_sub(settle)


def projected(hidden, norm_gain, query_weight, key_weight, value_weight):
    frames, features = hidden.shape
    depth, q_width = query_weight.shape
    kv_width = key_weight.shape[1]
    total = q_width + 2 * kv_width
    dma = pltpu.SemaphoreType.DMA
    anywhere = pl.BlockSpec(memory_space=pl.ANY)
    vmem = pl.BlockSpec(memory_space=pltpu.VMEM)
    return pl.pallas_call(
        project_kernel,
        out_shape=(
            jax.ShapeDtypeStruct((frames, q_width), jnp.bfloat16),
            jax.ShapeDtypeStruct((frames, 2 * kv_width), jnp.bfloat16),
        ),
        in_specs=[vmem] + [anywhere] * 4,
        out_specs=(vmem, vmem),
        scratch_shapes=[
            pltpu.VMEM((8 * depth, total), jnp.bfloat16),
            pltpu.VMEM((2, frames, features), jnp.bfloat16),
            pltpu.VMEM((4, frames, features // 2), jnp.bfloat16),
            pltpu.VMEM((frames, total), jnp.float32),
            dma((4,)), dma((SUBS,)), dma((SUBS,)),
            dma((2, 3, SUBS)), dma((2, 3, SUBS)),
            dma((2, 3, SUBS)), dma((2, 3, SUBS)),
            dma((2, 2, 3, SUBS)), dma((2, 2, 3, SUBS)),
            dma, dma,
        ],
        compiler_params=pltpu.CompilerParams(
            collective_id=0, has_side_effects=True, vmem_limit_bytes=58 * 1024 * 1024
        ),
        cost_estimate=pl.CostEstimate(
            flops=2 * frames * 8 * depth * total, bytes_accessed=4 * hidden.size, transcendentals=frames
        ),
    )(norm_gain.reshape(1, -1), hidden, query_weight, key_weight, value_weight)


def cross_kernel(
    repeat, q_ref, kv_ref, wo_ref, out_ref,
    kv, wo, m_ref, l_ref, acc_ref, attended, kept, leaving, came,
    local_sem, swap_s, swap_r, k_s, k_r, kc_s, kc_r,
    z_s, z_r, y_s, y_r, c_s, c_r, own_s, own_r, x_s, x_r,
):
    last = 3
    c = lax.axis_index("stream")
    s = lax.axis_index("seq")
    t = lax.axis_index("tensor")
    z, k = s // 2, s % 2
    frames = q_ref.shape[0]
    kv_width = kv_ref.shape[1] // 2
    heads = kv_width // HEAD_DIM
    depth, block = wo_ref.shape
    half = depth // 2
    rows = half // SUBS
    keys = frames // SUBS
    scale = LOG2E * HEAD_DIM ** (-0.5)
    at = {"stream": c, "seq": s, "tensor": t}
    up, down = {**at, "seq": s + 2}, {**at, "seq": s - 2}
    beside, mate, across = {**at, "stream": 1 - c}, {**at, "seq": 2 * z + 1 - k}, {**at, "tensor": 1 - t}
    greet(z, last, (beside, mate, across), up, down)
    sends = (z < last, z > 0)

    def each_sub(action):
        @pl.loop(0, SUBS)
        def _(sub):
            action(sub)

    def key_rows(hop, sub):
        start = pl.multiple_of((2 * (z - hop) + k) * frames + sub * keys, keys)
        return kv.at[pl.ds(start, keys)]

    def swap(sub):
        start = pl.multiple_of(sub * keys, keys)
        return remote(kv_ref.at[pl.ds(start, keys)], key_rows(0, sub), swap_s.at[sub], swap_r.at[sub], beside)

    def climb(hop, sub):
        view = key_rows(hop, sub)
        return remote(view, view, k_s.at[hop, sub], k_r.at[hop, sub], up)

    def hand(hop, sub):
        view = key_rows(hop, sub)
        return remote(view, view, kc_s.at[hop, sub], kc_r.at[hop, sub], mate)

    def source(way, hop):
        return z - hop if way == 0 else z + hop

    def part(origin, core, side, sub):
        start = pl.multiple_of(side * half + sub * rows, rows)
        return wo.at[2 * origin + core, pl.ds(start, rows)]

    def along(way, hop, sub):
        view = part(source(way, hop), k, c, sub)
        return remote(view, view, z_s.at[way, hop, sub], z_r.at[way, hop, sub], up if way == 0 else down)

    def sideways(way, hop, sub):
        view = part(source(way, hop), k, c, sub)
        return remote(view, view, y_s.at[way, hop - 1, sub], y_r.at[way, hop - 1, sub], beside)

    def inward(way, kind, hop, sub):
        view = part(source(way, hop), k, c if kind == 0 else 1 - c, sub)
        return remote(view, view, c_s.at[way, kind, hop - 1, sub], c_r.at[way, kind, hop - 1, sub], mate)

    def arrives(way, hop):
        return z >= hop if way == 0 else z + hop <= last

    def pass_on(way, hop, sub):
        @pl.when(arrives(way, hop))
        def _():
            along(way, hop - 1, sub).wait_recv()
            if hop < last:
                @pl.when(sends[way])
                def _():
                    along(way, hop, sub).start()
            sideways(way, hop, sub).start()
            inward(way, 0, hop, sub).start()

    def pass_in(way, hop, sub):
        @pl.when(arrives(way, hop))
        def _():
            sideways(way, hop, sub).wait_recv()
            inward(way, 1, hop, sub).start()

    def gathered(way, hop):
        @pl.when(arrives(way, hop))
        def _():
            def action(sub):
                inward(way, 0, hop, sub).wait_recv()
                inward(way, 1, hop, sub).wait_recv()

            each_sub(action)

    def pass_keys(hop, sub):
        @pl.when(z >= hop)
        def _():
            climb(hop - 1, sub).wait_recv()
            if hop < last:
                @pl.when(z < last)
                def _():
                    climb(hop, sub).start()
            hand(hop, sub).start()

    def attend_to(head, start, count, masked):
        at_keys = pl.ds(pl.multiple_of(start, count), count)
        keys_here = kv[at_keys, pl.ds(pl.multiple_of(head * HEAD_DIM, HEAD_DIM), HEAD_DIM)]
        values_here = kv[at_keys, pl.ds(pl.multiple_of(kv_width + head * HEAD_DIM, HEAD_DIM), HEAD_DIM)]
        if masked:
            allowed = lax.broadcasted_iota(jnp.int32, (count, frames), 0) <= lax.broadcasted_iota(
                jnp.int32, (count, frames), 1
            )

        def scored(r):
            q = q_ref[:, pl.ds(pl.multiple_of((head * repeat + r) * HEAD_DIM, HEAD_DIM), HEAD_DIM)]
            return lax.dot_general(
                keys_here, q, (((1,), (1,)), ((), ())), preferred_element_type=jnp.float32
            )

        following = scored(0)
        for r in range(repeat):
            index = head * repeat + r
            scores = following
            if r + 1 < repeat:
                following = scored(r + 1)
            if masked:
                scores = jnp.where(allowed, scores, -1e30)
            top = jnp.max(scores, axis=0, keepdims=True) * scale
            before = m_ref[index]
            fresh = jnp.maximum(before, top)
            m_ref[index] = fresh
            alpha = jnp.exp2(before - fresh)
            p = jnp.exp2(scores * scale - fresh)
            l_ref[index] = alpha * l_ref[index] + jnp.sum(p, axis=0, keepdims=True)
            acc_ref[index] = alpha * acc_ref[index] + lax.dot_general(
                values_here, p.astype(jnp.bfloat16), (((0,), (0,)), ((), ())), preferred_element_type=jnp.float32
            )

    def attend_own(head):
        attend_to(head, s * frames, frames, True)

        @pl.when(k == 1)
        def _():
            attend_to(head, (s - 1) * frames, frames, False)

    def attend_hop(hop, head):
        @pl.when(z >= hop)
        def _():
            attend_to(head, (z - hop) * 2 * frames, 2 * frames, False)

    def keys_held(hop):
        @pl.when(z >= hop)
        def _():
            each_sub(lambda sub: hand(hop, sub).wait_recv())

    order = line_order(z)

    def carry(slot):
        return remote(leaving.at[slot], came.at[slot], x_s.at[slot], x_r.at[slot], across)

    def shares(place, core):
        group = order[place]
        share = jnp.dot(attended[...], wo[2 * group + core], preferred_element_type=jnp.float32).astype(jnp.bfloat16)
        slot = (group % 2) * 2 + core

        @pl.when(group // 2 == t)
        def _():
            kept[slot] = share

        @pl.when(group // 2 != t)
        def _():
            leaving[slot] = share
            carry(slot).start()

    each_sub(lambda sub: swap(sub).start())
    fill = pltpu.make_async_copy(wo_ref, wo.at[s], local_sem)
    fill.start()
    fill.wait()

    @pl.when(sends[1])
    def _():
        each_sub(lambda sub: along(1, 0, sub).start())

    whole = remote(wo.at[s], wo.at[s], own_s, own_r, mate)
    whole.start()
    m_ref[...] = jnp.full_like(m_ref, -1e30)
    l_ref[...] = jnp.zeros_like(l_ref)
    acc_ref[...] = jnp.zeros_like(acc_ref)

    def first(sub):
        swap(sub).wait_recv()

        @pl.when(z < last)
        def _():
            climb(0, sub).start()

        hand(0, sub).start()

    each_sub(first)
    keys_held(0)

    for hop in range(1, last + 1):
        def phase(sub):
            pass_keys(hop, sub)
            pass_on(1, hop, sub)
            if hop > 1:
                pass_in(1, hop - 1, sub)
                attend_hop(hop - 1, sub)
            else:
                attend_own(sub)

        each_sub(phase)
        keys_held(hop)
        if hop == last - 1:
            @pl.when(sends[0])
            def _():
                each_sub(lambda sub: along(0, 0, sub).start())

    def fourth(sub):
        pass_on(0, 1, sub)
        pass_in(1, last, sub)
        attend_hop(last, sub)

    each_sub(fourth)

    @pl.loop(0, heads)
    def _(head):
        for r in range(repeat):
            index = head * repeat + r
            out = (acc_ref[index] / l_ref[index]).T.astype(jnp.bfloat16)
            attended[:, pl.ds(pl.multiple_of(index * HEAD_DIM, HEAD_DIM), HEAD_DIM)] = out

    whole.wait_recv()
    for hop in range(1, last + 1):
        gathered(1, hop)
    split = SUBS // 2

    def fifth(sub):
        pass_on(0, 2, sub)
        pass_in(0, 1, sub)

        @pl.when(sub % split == 0)
        def _():
            shares(0, sub // split)

    each_sub(fifth)
    gathered(0, 1)

    def sixth(sub):
        pass_on(0, 3, sub)
        pass_in(0, 2, sub)

        @pl.when(sub % split == 0)
        def _():
            shares(1, sub // split)

    each_sub(sixth)
    gathered(0, 2)
    shares(2, 0)
    shares(2, 1)
    each_sub(lambda sub: pass_in(0, 3, sub))
    gathered(0, 3)
    shares(3, 0)
    shares(3, 1)

    for place in range(4):
        for core in range(2):
            group = order[place]
            slot = (group % 2) * 2 + core

            @pl.when(group // 2 == t)
            def _():
                carry(slot).wait_recv()
                total = kept[slot].astype(jnp.float32) + came[slot].astype(jnp.float32)
                out_ref[:, pl.ds(pl.multiple_of(slot * block, block), block)] = total.astype(jnp.bfloat16)

    whole.wait_send()
    for slot in range(4):
        carry(slot).wait_send()

    def settle(sub):
        swap(sub).wait_send()
        for hop in range(last + 1):
            @pl.when(z >= hop)
            def _():
                hand(hop, sub).wait_send()
                if hop < last:
                    @pl.when(z < last)
                    def _():
                        climb(hop, sub).wait_send()
        for way in range(2):
            for hop in range(last):
                @pl.when(sends[way] & (arrives(way, hop) if hop else True))
                def _():
                    along(way, hop, sub).wait_send()
            for hop in range(1, last + 1):
                @pl.when(arrives(way, hop))
                def _():
                    sideways(way, hop, sub).wait_send()
                    inward(way, 0, hop, sub).wait_send()
                    inward(way, 1, hop, sub).wait_send()

    each_sub(settle)


def crossed(queries, keys_values, out_weight, repeat):
    frames, width = queries.shape
    kv_width = keys_values.shape[1] // 2
    depth, block = out_weight.shape
    count = width // HEAD_DIM
    dma = pltpu.SemaphoreType.DMA
    anywhere = pl.BlockSpec(memory_space=pl.ANY)
    vmem = pl.BlockSpec(memory_space=pltpu.VMEM)
    bf16, f32 = jnp.bfloat16, jnp.float32
    return pl.pallas_call(
        functools.partial(cross_kernel, repeat),
        out_shape=jax.ShapeDtypeStruct((frames, 4 * block), bf16),
        in_specs=[vmem, vmem, anywhere],
        out_specs=vmem,
        scratch_shapes=[
            pltpu.VMEM((8 * frames, 2 * kv_width), bf16),
            pltpu.VMEM((8, depth, block), bf16),
            pltpu.VMEM((count, 1, frames), f32),
            pltpu.VMEM((count, 1, frames), f32),
            pltpu.VMEM((count, HEAD_DIM, frames), f32),
            pltpu.VMEM((frames, width), bf16),
            pltpu.VMEM((4, frames, block), bf16),
            pltpu.VMEM((4, frames, block), bf16),
            pltpu.VMEM((4, frames, block), bf16),
            dma, dma((SUBS,)), dma((SUBS,)),
            dma((3, SUBS)), dma((3, SUBS)),
            dma((4, SUBS)), dma((4, SUBS)),
            dma((2, 3, SUBS)), dma((2, 3, SUBS)),
            dma((2, 3, SUBS)), dma((2, 3, SUBS)),
            dma((2, 2, 3, SUBS)), dma((2, 2, 3, SUBS)),
            dma, dma, dma((4,)), dma((4,)),
        ],
        compiler_params=pltpu.CompilerParams(
            collective_id=1, has_side_effects=True, vmem_limit_bytes=58 * 1024 * 1024
        ),
        cost_estimate=pl.CostEstimate(
            flops=16 * frames * depth * block, bytes_accessed=4 * queries.size, transcendentals=4 * frames * frames * count
        ),
    )(queries, keys_values, out_weight)


def y_share(mine, core, after=None):
    depth = mine.shape[0] // 2
    part = lax.dynamic_slice_in_dim(mine, core * depth, depth, 0)
    near = lax.ppermute(part, "stream", [(0, 1), (1, 0)])
    if after is None:
        return near, swap_pairs(near, "seq")
    near, after = lax.optimization_barrier((near, after))
    return near, swap_pairs(near, "seq"), after


def fits(hidden, query_weight, key_weight):
    meshes = (lax.axis_size("stream"), lax.axis_size("seq"), lax.axis_size("tensor"))
    return (
        meshes == (2, 8, 2)
        and hidden.shape[1:] == (1, 512, 2048)
        and query_weight.shape == (512, 2048)
        and key_weight.shape == (512, 512)
    )


def body(hidden, norm_gain, query_weight, key_weight, value_projection_weight, out_weight):
    if not fits(hidden, query_weight, key_weight):
        return general_body(hidden, norm_gain, query_weight, key_weight, value_projection_weight, out_weight)
    queries, keys_values = projected(
        hidden.reshape(hidden.shape[2:]), norm_gain, query_weight, key_weight, value_projection_weight
    )
    out = crossed(queries, keys_values, out_weight, query_weight.shape[1] // key_weight.shape[1])
    return out.reshape(hidden.shape)


def general_body(hidden, norm_gain, query_weight, key_weight, value_projection_weight, out_weight):
    windows, frame_count = hidden.shape[1], hidden.shape[2]
    n_tensor = lax.axis_size("tensor")
    n_seq = lax.axis_size("seq")
    stream = lax.axis_index("stream")
    tensor = lax.axis_index("tensor")
    seq = lax.axis_index("seq")
    core = seq % 2
    rows = windows * frame_count
    depth = query_weight.shape[0] // 2
    out_half = out_weight.shape[1] // 2

    kv_weight = jnp.concatenate([key_weight, value_projection_weight], axis=1)
    kv_mine = lax.all_gather(
        lax.dynamic_slice_in_dim(kv_weight, stream * depth, depth, 0), "seq", axis=0, tiled=True
    )
    query_mine = lax.all_gather(
        lax.dynamic_slice_in_dim(query_weight, stream * depth, depth, 0), "seq", axis=0, tiled=True
    )
    out_mine = lax.all_gather(
        lax.dynamic_slice_in_dim(out_weight, stream * out_half, out_half, 1), "seq", axis=1, tiled=True
    )

    local = hidden.reshape(rows, hidden.shape[3])
    if n_tensor == 2:
        other = lax.ppermute(local, "tensor", [(0, 1), (1, 0)])
        gathered = jnp.where(
            tensor == 0,
            jnp.concatenate([local, other], axis=1),
            jnp.concatenate([other, local], axis=1),
        )
    else:
        gathered = lax.all_gather(local, "tensor", axis=1, tiled=True)
    flat = gathered.astype(jnp.float32)
    inverse_rms = lax.rsqrt(jnp.mean(flat * flat, axis=1, keepdims=True) + 1e-05)
    normed = (flat * inverse_rms * norm_gain).astype(jnp.bfloat16)
    split = normed.reshape(rows, n_seq, 2, depth)

    def features(half):
        return lax.dynamic_index_in_dim(split, half, 2, keepdims=False).reshape(rows, n_seq * depth)

    normed_mine = features(stream)
    normed_other = features(1 - stream)
    span = n_seq * depth // 2
    normed_near = lax.dynamic_slice_in_dim(normed_other, core * span, span, 1)
    normed_far = lax.dynamic_slice_in_dim(normed_other, (1 - core) * span, span, 1)

    def project(mine, near, far):
        total = jnp.dot(normed_mine, mine, preferred_element_type=jnp.float32)
        total += jnp.dot(normed_near, near, preferred_element_type=jnp.float32)
        total += jnp.dot(normed_far, far, preferred_element_type=jnp.float32)
        return total.astype(jnp.bfloat16)

    keys_values = project(kv_mine, *y_share(kv_mine, core))
    partner = lax.ppermute(keys_values, "stream", [(0, 1), (1, 0)])
    kv_width = key_weight.shape[1]
    parts = 2 if kv_width % (2 * HEAD_DIM) == 0 else 1
    step = kv_width // parts
    pieces = []
    for part in range(parts):
        columns = jnp.concatenate(
            [partner[:, part * step:(part + 1) * step],
             partner[:, kv_width + part * step:kv_width + (part + 1) * step]],
            axis=1,
        )
        pieces.append(
            lax.all_gather(columns.reshape(windows, frame_count, 2 * step), "seq", axis=1, tiled=True)
        )
    queries = project(query_mine, *y_share(query_mine, core)).reshape(windows, frame_count, -1)
    out_near = out_far = None
    width = out_weight.shape[0] // 2

    repeat = query_weight.shape[1] // key_weight.shape[1]
    chunk = frame_count // ROW_CHUNKS

    def scattered(share):
        if n_tensor == 2:
            wide = share.shape[1] // 2
            away = lax.dynamic_slice_in_dim(share, (1 - tensor) * wide, wide, 1)
            kept = lax.dynamic_slice_in_dim(share, tensor * wide, wide, 1)
            came = lax.ppermute(away, "tensor", [(0, 1), (1, 0)])
            return (kept.astype(jnp.float32) + came.astype(jnp.float32)).astype(jnp.bfloat16)
        return lax.psum_scatter(share, "tensor", scatter_dimension=1, tiled=True)

    outs = []
    q_step = step * repeat
    for window in range(windows):
        early = [
            attend(
                seq * frame_count,
                queries[window][:, part * q_step:(part + 1) * q_step],
                pieces[part][window],
                repeat,
            )
            for part in range(parts - 1)
        ]
        for index in range(ROW_CHUNKS):
            low, high = index * chunk, (index + 1) * chunk
            final = attend(
                seq * frame_count + low,
                queries[window][low:high, (parts - 1) * q_step:],
                pieces[-1][window],
                repeat,
            )
            attended = jnp.concatenate([done[low:high] for done in early] + [final], axis=1)
            share_mine = jnp.dot(attended, out_mine, preferred_element_type=jnp.float32)
            if out_near is None:
                out_near, out_far, attended = y_share(out_mine, core, attended)
            attended_near = lax.dynamic_slice_in_dim(attended, core * width, width, 1)
            attended_far = lax.dynamic_slice_in_dim(attended, (1 - core) * width, width, 1)
            share_other = jnp.dot(attended_near, out_near, preferred_element_type=jnp.float32)
            share_other += jnp.dot(attended_far, out_far, preferred_element_type=jnp.float32)
            mine = scattered(share_mine.astype(jnp.bfloat16)).reshape(chunk, -1, out_half)
            other = scattered(share_other.astype(jnp.bfloat16)).reshape(chunk, -1, out_half)
            outs.append(
                jnp.where(
                    stream == 0, jnp.stack([mine, other], axis=2), jnp.stack([other, mine], axis=2)
                ).reshape(chunk, -1)
            )
    return jnp.concatenate(outs, axis=0).reshape(1, windows, frame_count, -1)


def solution(mesh):
    in_specs = (
        P("stream", None, "seq", "tensor"),
        P(),
        P("seq", "tensor"),
        P("seq", "tensor"),
        P("seq", "tensor"),
        P("tensor", "seq"),
    )
    out_specs = P("stream", None, "seq", "tensor")
    return jax.shard_map(body, mesh=mesh, in_specs=in_specs, out_specs=out_specs, check_vma=False)
```

```python
import functools

import jax
import jax.numpy as jnp
from jax import lax
from jax.experimental import pallas as pl
from jax.experimental.pallas import tpu as pltpu
from jax.sharding import PartitionSpec as P

HEAD_DIM = 128
ROW_CHUNKS = 2
KEY_BLOCK = 1024
LOG2E = 1.4426950408889634


def swap_pairs(block, axis):
    count = lax.axis_size(axis)
    return lax.ppermute(block, axis, [(i, i ^ 1) for i in range(count)])


def attend_kernel(repeat, start_ref, q_ref, k_ref, v_ref, o_ref, m_ref, l_ref, acc_ref):
    step = pl.program_id(1)
    rows = q_ref.shape[0]
    keys = k_ref.shape[0]
    start = start_ref[0]
    last = (start + rows - 1) // keys
    scale = LOG2E * HEAD_DIM ** (-0.5)

    @pl.when(step == 0)
    def _():
        m_ref[...] = jnp.full_like(m_ref, -1e30)
        l_ref[...] = jnp.zeros_like(l_ref)
        acc_ref[...] = jnp.zeros_like(acc_ref)

    def update(masked):
        k = k_ref[...]
        v = v_ref[...]
        if masked:
            frame = start + lax.broadcasted_iota(jnp.int32, (keys, rows), 1)
            key = step * keys + lax.broadcasted_iota(jnp.int32, (keys, rows), 0)
            allowed = key <= frame

        def scored(r):
            q = q_ref[:, r * HEAD_DIM:(r + 1) * HEAD_DIM]
            return lax.dot_general(k, q, (((1,), (1,)), ((), ())), preferred_element_type=jnp.float32)

        following = scored(0)
        for r in range(repeat):
            s = following
            if r + 1 < repeat:
                following = scored(r + 1)
            if masked:
                s = jnp.where(allowed, s, -1e30)
            top = jnp.max(s, axis=0, keepdims=True) * scale
            before = m_ref[r]
            fresh = jnp.maximum(before, top)
            m_ref[r] = fresh
            alpha = jnp.exp2(before - fresh)
            p = jnp.exp2(s * scale - fresh)
            l_ref[r] = alpha * l_ref[r] + jnp.sum(p, axis=0, keepdims=True)
            acc_ref[r] = alpha * acc_ref[r] + lax.dot_general(
                v, p.astype(jnp.bfloat16), (((0,), (0,)), ((), ())), preferred_element_type=jnp.float32
            )

    @pl.when(step < last)
    def _():
        update(False)

    @pl.when(step == last)
    def _():
        update(True)
        for r in range(repeat):
            attended = (acc_ref[r] / l_ref[r]).T
            o_ref[:, r * HEAD_DIM:(r + 1) * HEAD_DIM] = attended.astype(o_ref.dtype)


def attend(start, queries, keys_values, repeat):
    rows, width = queries.shape
    count = keys_values.shape[0]
    groups = width // (repeat * HEAD_DIM)
    block = min(KEY_BLOCK, count)

    def at(step, start_ref):
        return jnp.minimum(step, (start_ref[0] + rows - 1) // block)

    return pl.pallas_call(
        functools.partial(attend_kernel, repeat),
        out_shape=jax.ShapeDtypeStruct((rows, width), jnp.bfloat16),
        grid_spec=pltpu.PrefetchScalarGridSpec(
            num_scalar_prefetch=1,
            grid=(groups, count // block),
            in_specs=[
                pl.BlockSpec((rows, repeat * HEAD_DIM), lambda g, i, s: (0, g)),
                pl.BlockSpec((block, HEAD_DIM), lambda g, i, s: (at(i, s), g)),
                pl.BlockSpec((block, HEAD_DIM), lambda g, i, s: (at(i, s), groups + g)),
            ],
            out_specs=pl.BlockSpec((rows, repeat * HEAD_DIM), lambda g, i, s: (0, g)),
            scratch_shapes=[
                pltpu.VMEM((repeat, 1, rows), jnp.float32),
                pltpu.VMEM((repeat, 1, rows), jnp.float32),
                pltpu.VMEM((repeat, HEAD_DIM, rows), jnp.float32),
            ],
        ),
        compiler_params=pltpu.CompilerParams(
            dimension_semantics=("arbitrary", "arbitrary"), vmem_limit_bytes=32 * 1024 * 1024
        ),
        cost_estimate=pl.CostEstimate(
            flops=8 * rows * count * width,
            bytes_accessed=2 * (2 * rows * width + keys_values.size),
            transcendentals=rows * count * width // HEAD_DIM,
        ),
    )(start.reshape(1), queries, keys_values, keys_values)


SUBS = 4
WINDOW = 2


def line_order(z):
    first = z - 1 + 2 * ((3 - z) // 3)
    third = 3 * (1 - z // 2)
    return (z, first, 6 - z - first - third, third)


def remote(src, dst, send, recv, device):
    return pltpu.make_async_remote_copy(
        src_ref=src, dst_ref=dst, send_sem=send, recv_sem=recv, device_id=device, device_id_type=pl.DeviceIdType.MESH
    )


def greet(z, last, devices, up, down):
    barrier = pltpu.get_barrier_semaphore()

    def hello(device):
        pl.semaphore_signal(barrier, inc=1, device_id=device, device_id_type=pl.DeviceIdType.MESH)

    for device in devices:
        hello(device)

    @pl.when(z < last)
    def _():
        hello(up)

    @pl.when(z > 0)
    def _():
        hello(down)

    inner = jnp.where((z > 0) & (z < last), 1, 0)
    pl.semaphore_wait(barrier, len(devices) + 1 + inner)


def project_kernel(
    gain_ref, hidden_ref, wq_ref, wk_ref, wv_ref, q_ref, kv_ref,
    w, hid, normed, acc,
    local_sem, x_s, x_r, z_s, z_r, y_s, y_r, c_s, c_r, own_s, own_r,
):
    last = 3
    c = lax.axis_index("stream")
    s = lax.axis_index("seq")
    t = lax.axis_index("tensor")
    z, k = s // 2, s % 2
    depth = wq_ref.shape[0]
    half = depth // 2
    rows = half // SUBS
    q_width, kv_width = wq_ref.shape[1], wk_ref.shape[1]
    frames = hid.shape[1]
    step = frames // SUBS
    at = {"stream": c, "seq": s, "tensor": t}
    up, down = {**at, "seq": s + 2}, {**at, "seq": s - 2}
    beside, mate, across = {**at, "stream": 1 - c}, {**at, "seq": 2 * z + 1 - k}, {**at, "tensor": 1 - t}
    greet(z, last, (beside, mate, across), up, down)

    own = pl.multiple_of(s * depth, depth)
    fills = [
        pltpu.make_async_copy(wq_ref, w.at[pl.ds(own, depth), pl.ds(0, q_width)], local_sem.at[0]),
        pltpu.make_async_copy(wk_ref, w.at[pl.ds(own, depth), pl.ds(q_width, kv_width)], local_sem.at[1]),
        pltpu.make_async_copy(wv_ref, w.at[pl.ds(own, depth), pl.ds(q_width + kv_width, kv_width)], local_sem.at[2]),
    ]
    mine = pltpu.make_async_copy(hidden_ref, hid.at[t], local_sem.at[3])
    for copy in fills:
        copy.start()
    mine.start()

    def crossing(piece):
        start = pl.multiple_of(piece * step, step)
        return remote(
            hidden_ref.at[pl.ds(start, step)], hid.at[t, pl.ds(start, step)], x_s.at[piece], x_r.at[piece], across
        )

    for piece in range(SUBS):
        crossing(piece).start()
    for copy in fills:
        copy.wait()

    def part(source, core, side, sub):
        start = pl.multiple_of(source * (2 * depth) + core * depth + side * half + sub * rows, rows)
        return w.at[pl.ds(start, rows)]

    def source(way, hop):
        return z - hop if way == 0 else z + hop

    def along(way, hop, sub):
        view = part(source(way, hop), k, c, sub)
        return remote(view, view, z_s.at[way, hop, sub], z_r.at[way, hop, sub], up if way == 0 else down)

    def sideways(way, hop, sub):
        view = part(source(way, hop), k, c, sub)
        return remote(view, view, y_s.at[way, hop - 1, sub], y_r.at[way, hop - 1, sub], beside)

    def inward(way, kind, hop, sub):
        view = part(source(way, hop), k, c if kind == 0 else 1 - c, sub)
        return remote(view, view, c_s.at[way, kind, hop - 1, sub], c_r.at[way, kind, hop - 1, sub], mate)

    sends = (z < last, z > 0)

    def arrives(way, hop):
        return z >= hop if way == 0 else z + hop <= last

    def each_sub(action):
        @pl.loop(0, SUBS)
        def _(sub):
            action(sub)

    def leave(way, number):
        if number < last * SUBS:
            hop, sub = number // SUBS, number % SUBS

            @pl.when(sends[way] & arrives(way, hop))
            def _():
                along(way, hop, sub).start()

    def left(way, number):
        hop, sub = number // SUBS, number % SUBS

        @pl.when(sends[way] & arrives(way, hop))
        def _():
            along(way, hop, sub).wait_send()

    for number in range(WINDOW):
        for way in range(2):
            leave(way, number)
    block = w.at[pl.ds(own, depth)]
    share = remote(block, block, own_s, own_r, mate)
    share.start()

    def pass_on(hop, sub):
        for way in range(2):
            @pl.when(arrives(way, hop))
            def _():
                along(way, hop - 1, sub).wait_recv()
                sideways(way, hop, sub).start()
                inward(way, 0, hop, sub).start()

            number = (hop - 1) * SUBS + sub
            left(way, number)
            leave(way, number + WINDOW)

    def pass_in(hop, sub):
        for way in range(2):
            @pl.when(arrives(way, hop))
            def _():
                sideways(way, hop, sub).wait_recv()
                inward(way, 1, hop, sub).start()

    def gathered(hop):
        def action(sub):
            for way in range(2):
                @pl.when(arrives(way, hop))
                def _():
                    inward(way, 0, hop, sub).wait_recv()
                    inward(way, 1, hop, sub).wait_recv()

        each_sub(action)

    tall = 16

    def norm(sub):
        crossing(sub).wait_recv()

        @pl.loop(0, step // tall)
        def _(i):
            at_rows = pl.ds(pl.multiple_of(sub * step + i * tall, tall), tall)
            low = hid[0, at_rows, :].astype(jnp.float32)
            high = hid[1, at_rows, :].astype(jnp.float32)
            total = jnp.sum(low * low, axis=1, keepdims=True) + jnp.sum(high * high, axis=1, keepdims=True)
            inverse_rms = lax.rsqrt(total / (2 * low.shape[1]) + 1e-05)
            wide = normed.shape[2]
            for group in range(4):
                x = (low if group < 2 else high)[:, (group % 2) * wide:(group % 2 + 1) * wide]
                gain = gain_ref[:, group * wide:(group + 1) * wide]
                normed[group, at_rows, :] = (x * inverse_rms * gain).astype(jnp.bfloat16)

    order = line_order(z)
    tile = min(512, kv_width)

    def dot(place, index):
        group = order[place]
        columns = pl.ds(pl.multiple_of(index * tile, tile), tile)
        return jnp.dot(
            normed[group],
            w[pl.ds(pl.multiple_of(group * 2 * depth, 2 * depth), 2 * depth), columns],
            preferred_element_type=jnp.float32,
        ), columns

    def project(place, low, high):
        @pl.loop(low, high)
        def _(index):
            value, columns = dot(place, index)
            if place == 0:
                acc[:, columns] = value
            else:
                acc[:, columns] += value

    tiles = (q_width + 2 * kv_width) // tile

    for sub in range(SUBS):
        pass_on(1, sub)
    mine.wait()

    def second(sub):
        pass_on(2, sub)
        pass_in(1, sub)
        norm(sub)

    for sub in range(SUBS):
        second(sub)
    share.wait_recv()
    gathered(1)
    for sub in range(SUBS):
        pass_on(3, sub)
        pass_in(2, sub)
        low, high = sub * 2 * tiles // SUBS, (sub + 1) * 2 * tiles // SUBS
        for place in range(2):
            first, end = max(low - place * tiles, 0), min(high - place * tiles, tiles)
            if first < end:
                project(place, first, end)
    for sub in range(SUBS - 1):
        pass_in(3, sub)
    gathered(2)
    project(2, 0, tiles)
    pass_in(3, SUBS - 1)
    gathered(3)

    @pl.loop(0, q_width // tile)
    def _(index):
        value, columns = dot(3, index)
        q_ref[:, columns] = (acc[:, columns] + value).astype(jnp.bfloat16)

    for index in range(2 * kv_width // tile):
        value, columns = dot(3, q_width // tile + index)
        kv_ref[:, index * tile:(index + 1) * tile] = (acc[:, columns] + value).astype(jnp.bfloat16)

    share.wait_send()

    def settle(sub):
        crossing(sub).wait_send()
        for way in range(2):
            for hop in range(1, last + 1):
                @pl.when(arrives(way, hop))
                def _():
                    sideways(way, hop, sub).wait_send()
                    inward(way, 0, hop, sub).wait_send()
                    inward(way, 1, hop, sub).wait_send()

    each_sub(settle)


def projected(hidden, norm_gain, query_weight, key_weight, value_weight):
    frames, features = hidden.shape
    depth, q_width = query_weight.shape
    kv_width = key_weight.shape[1]
    total = q_width + 2 * kv_width
    dma = pltpu.SemaphoreType.DMA
    anywhere = pl.BlockSpec(memory_space=pl.ANY)
    vmem = pl.BlockSpec(memory_space=pltpu.VMEM)
    return pl.pallas_call(
        project_kernel,
        out_shape=(
            jax.ShapeDtypeStruct((frames, q_width), jnp.bfloat16),
            jax.ShapeDtypeStruct((frames, 2 * kv_width), jnp.bfloat16),
        ),
        in_specs=[vmem] + [anywhere] * 4,
        out_specs=(vmem, vmem),
        scratch_shapes=[
            pltpu.VMEM((8 * depth, total), jnp.bfloat16),
            pltpu.VMEM((2, frames, features), jnp.bfloat16),
            pltpu.VMEM((4, frames, features // 2), jnp.bfloat16),
            pltpu.VMEM((frames, total), jnp.float32),
            dma((4,)), dma((SUBS,)), dma((SUBS,)),
            dma((2, 3, SUBS)), dma((2, 3, SUBS)),
            dma((2, 3, SUBS)), dma((2, 3, SUBS)),
            dma((2, 2, 3, SUBS)), dma((2, 2, 3, SUBS)),
            dma, dma,
        ],
        compiler_params=pltpu.CompilerParams(
            collective_id=0, has_side_effects=True, vmem_limit_bytes=58 * 1024 * 1024
        ),
        cost_estimate=pl.CostEstimate(
            flops=2 * frames * 8 * depth * total, bytes_accessed=4 * hidden.size, transcendentals=frames
        ),
    )(norm_gain.reshape(1, -1), hidden, query_weight, key_weight, value_weight)


def cross_kernel(
    repeat, q_ref, kv_ref, wo_ref, out_ref,
    kv, wo, m_ref, l_ref, acc_ref, attended, kept, leaving, came,
    local_sem, swap_s, swap_r, k_s, k_r, kc_s, kc_r,
    z_s, z_r, y_s, y_r, c_s, c_r, own_s, own_r, x_s, x_r,
):
    last = 3
    c = lax.axis_index("stream")
    s = lax.axis_index("seq")
    t = lax.axis_index("tensor")
    z, k = s // 2, s % 2
    frames = q_ref.shape[0]
    kv_width = kv_ref.shape[1] // 2
    heads = kv_width // HEAD_DIM
    depth, block = wo_ref.shape
    half = depth // 2
    wide = block // SUBS
    keys = frames // SUBS
    scale = LOG2E * HEAD_DIM ** (-0.5)
    at = {"stream": c, "seq": s, "tensor": t}
    up, down = {**at, "seq": s + 2}, {**at, "seq": s - 2}
    beside, mate, across = {**at, "stream": 1 - c}, {**at, "seq": 2 * z + 1 - k}, {**at, "tensor": 1 - t}
    greet(z, last, (beside, mate, across), up, down)
    sends = (z < last, z > 0)

    def each_sub(action):
        @pl.loop(0, SUBS)
        def _(sub):
            action(sub)

    def key_rows(hop, sub):
        start = pl.multiple_of((2 * (z - hop) + k) * frames + sub * keys, keys)
        return kv.at[pl.ds(start, keys)]

    def swap(sub):
        start = pl.multiple_of(sub * keys, keys)
        return remote(kv_ref.at[pl.ds(start, keys)], key_rows(0, sub), swap_s.at[sub], swap_r.at[sub], beside)

    def climb(hop, sub):
        view = key_rows(hop, sub)
        return remote(view, view, k_s.at[hop, sub], k_r.at[hop, sub], up)

    def hand(hop, sub):
        view = key_rows(hop, sub)
        return remote(view, view, kc_s.at[hop, sub], kc_r.at[hop, sub], mate)

    def source(way, hop):
        return z - hop if way == 0 else z + hop

    def part(origin, core, side, sub):
        return wo.at[2 * origin + core, sub, pl.ds(pl.multiple_of(side * half, half), half)]

    def along(way, hop, sub):
        view = part(source(way, hop), k, c, sub)
        return remote(view, view, z_s.at[way, hop, sub], z_r.at[way, hop, sub], up if way == 0 else down)

    def sideways(way, hop, sub):
        view = part(source(way, hop), k, c, sub)
        return remote(view, view, y_s.at[way, hop - 1, sub], y_r.at[way, hop - 1, sub], beside)

    def inward(way, kind, hop, sub):
        view = part(source(way, hop), k, c if kind == 0 else 1 - c, sub)
        return remote(view, view, c_s.at[way, kind, hop - 1, sub], c_r.at[way, kind, hop - 1, sub], mate)

    def arrives(way, hop):
        return z >= hop if way == 0 else z + hop <= last

    def pass_on(way, hop, sub):
        @pl.when(arrives(way, hop))
        def _():
            along(way, hop - 1, sub).wait_recv()
            if hop < last:
                @pl.when(sends[way])
                def _():
                    along(way, hop, sub).start()
            sideways(way, hop, sub).start()
            inward(way, 0, hop, sub).start()

    def pass_in(way, hop, sub):
        @pl.when(arrives(way, hop))
        def _():
            sideways(way, hop, sub).wait_recv()
            inward(way, 1, hop, sub).start()

    def gathered(way, hop):
        @pl.when(arrives(way, hop))
        def _():
            def action(sub):
                inward(way, 0, hop, sub).wait_recv()
                inward(way, 1, hop, sub).wait_recv()

            each_sub(action)

    def pass_keys(hop, sub):
        @pl.when(z >= hop)
        def _():
            climb(hop - 1, sub).wait_recv()
            if hop < last:
                @pl.when(z < last)
                def _():
                    climb(hop, sub).start()
            hand(hop, sub).start()

    def attend_to(head, start, count, masked):
        at_keys = pl.ds(pl.multiple_of(start, count), count)
        keys_here = kv[at_keys, pl.ds(pl.multiple_of(head * HEAD_DIM, HEAD_DIM), HEAD_DIM)]
        values_here = kv[at_keys, pl.ds(pl.multiple_of(kv_width + head * HEAD_DIM, HEAD_DIM), HEAD_DIM)]
        if masked:
            allowed = lax.broadcasted_iota(jnp.int32, (count, frames), 0) <= lax.broadcasted_iota(
                jnp.int32, (count, frames), 1
            )

        def scored(r):
            q = q_ref[:, pl.ds(pl.multiple_of((head * repeat + r) * HEAD_DIM, HEAD_DIM), HEAD_DIM)]
            return lax.dot_general(
                keys_here, q, (((1,), (1,)), ((), ())), preferred_element_type=jnp.float32
            )

        following = scored(0)
        for r in range(repeat):
            index = head * repeat + r
            scores = following
            if r + 1 < repeat:
                following = scored(r + 1)
            if masked:
                scores = jnp.where(allowed, scores, -1e30)
            top = jnp.max(scores, axis=0, keepdims=True) * scale
            before = m_ref[index]
            fresh = jnp.maximum(before, top)
            m_ref[index] = fresh
            alpha = jnp.exp2(before - fresh)
            p = jnp.exp2(scores * scale - fresh)
            l_ref[index] = alpha * l_ref[index] + jnp.sum(p, axis=0, keepdims=True)
            acc_ref[index] = alpha * acc_ref[index] + lax.dot_general(
                values_here, p.astype(jnp.bfloat16), (((0,), (0,)), ((), ())), preferred_element_type=jnp.float32
            )

    def attend_own(head):
        attend_to(head, s * frames, frames, True)

        @pl.when(k == 1)
        def _():
            attend_to(head, (s - 1) * frames, frames, False)

    def attend_hop(hop, head):
        @pl.when(z >= hop)
        def _():
            attend_to(head, (z - hop) * 2 * frames, 2 * frames, False)

    def keys_held(hop):
        @pl.when(z >= hop)
        def _():
            each_sub(lambda sub: hand(hop, sub).wait_recv())

    def carry(slot):
        return remote(leaving.at[slot], came.at[slot], x_s.at[slot], x_r.at[slot], across)

    def shares(group, sub):
        weights = jnp.concatenate([wo[2 * group, sub], wo[2 * group + 1, sub]], axis=1)
        share = jnp.dot(attended[...], weights, preferred_element_type=jnp.float32).astype(jnp.bfloat16)
        slot = (group % 2) * SUBS + sub

        @pl.when(group // 2 == t)
        def _():
            kept[slot] = share

        @pl.when(group // 2 != t)
        def _():
            leaving[slot] = share
            carry(slot).start()

    each_sub(lambda sub: swap(sub).start())
    fills = [
        pltpu.make_async_copy(wo_ref.at[:, pl.ds(sub * wide, wide)], wo.at[s, sub], local_sem.at[sub])
        for sub in range(SUBS)
    ]
    for fill in fills:
        fill.start()
    for fill in fills:
        fill.wait()

    @pl.when(sends[1])
    def _():
        each_sub(lambda sub: along(1, 0, sub).start())

    whole = remote(wo.at[s], wo.at[s], own_s, own_r, mate)
    whole.start()
    m_ref[...] = jnp.full_like(m_ref, -1e30)
    l_ref[...] = jnp.zeros_like(l_ref)
    acc_ref[...] = jnp.zeros_like(acc_ref)

    def first(sub):
        swap(sub).wait_recv()

        @pl.when(z < last)
        def _():
            climb(0, sub).start()

        hand(0, sub).start()

    def climb_after(hop):
        @pl.when(sends[0] & (z == hop))
        def _():
            each_sub(lambda sub: along(0, 0, sub).start())

    each_sub(first)
    climb_after(0)
    keys_held(0)

    for hop in range(1, last + 1):
        def phase(sub):
            pass_keys(hop, sub)
            pass_on(1, hop, sub)
            if hop > 1:
                pass_in(1, hop - 1, sub)
                attend_hop(hop - 1, sub)
            else:
                attend_own(sub)

        each_sub(phase)
        climb_after(hop)
        keys_held(hop)

    def climbed(number):
        return number // SUBS + 1, number % SUBS

    def arrive(number):
        hop, sub = climbed(number)

        @pl.when(arrives(0, hop))
        def _():
            along(0, hop - 1, sub).wait_recv()

            @pl.when(sends[0] & (hop < last))
            def _():
                along(0, hop, sub).start()

            sideways(0, hop, sub).start()
            inward(0, 0, hop, sub).start()

    def spread(number):
        hop, sub = climbed(number)
        pass_in(0, hop, sub)

    def work(number):
        hop, sub = climbed(number)

        @pl.when(arrives(0, hop))
        def _():
            inward(0, 0, hop, sub).wait_recv()
            inward(0, 1, hop, sub).wait_recv()
            shares(z - hop, sub)

    def fourth(sub):
        arrive(sub)

        @pl.when(sub > 0)
        def _():
            spread(sub - 1)

        pass_in(1, last, sub)
        attend_hop(last, sub)

    each_sub(fourth)

    @pl.loop(0, heads)
    def _(head):
        for r in range(repeat):
            index = head * repeat + r
            out = (acc_ref[index] / l_ref[index]).T.astype(jnp.bfloat16)
            attended[:, pl.ds(pl.multiple_of(index * HEAD_DIM, HEAD_DIM), HEAD_DIM)] = out

    whole.wait_recv()
    each_sub(lambda sub: shares(z, sub))
    for hop in range(1, last + 1):
        gathered(1, hop)

        @pl.when(arrives(1, hop))
        def _():
            each_sub(lambda sub: shares(z + hop, sub))

    each_sub(lambda number: pl.when(number < SUBS - 2)(lambda: work(number)))

    @pl.loop(SUBS, last * SUBS)
    def _(number):
        arrive(number)
        spread(number - 1)
        work(number - 2)

    spread(last * SUBS - 1)
    work(last * SUBS - 2)
    work(last * SUBS - 1)

    high_first = z // 2

    @pl.loop(0, 2 * SUBS)
    def _(number):
        side, sub = number // SUBS, number % SUBS
        side = side + high_first * (1 - 2 * side)
        slot = side * SUBS + sub
        carry(slot).wait_recv()
        total = (kept[slot].astype(jnp.float32) + came[slot].astype(jnp.float32)).astype(jnp.bfloat16)
        for core in range(2):
            start = pl.multiple_of((side * 2 + core) * block + sub * wide, wide)
            out_ref[:, pl.ds(start, wide)] = total[:, core * wide:(core + 1) * wide]

    whole.wait_send()

    @pl.loop(0, 2 * SUBS)
    def _(slot):
        carry(slot).wait_send()

    def settle(sub):
        swap(sub).wait_send()
        for hop in range(last + 1):
            @pl.when(z >= hop)
            def _():
                hand(hop, sub).wait_send()
                if hop < last:
                    @pl.when(z < last)
                    def _():
                        climb(hop, sub).wait_send()
        for way in range(2):
            for hop in range(last):
                @pl.when(sends[way] & (arrives(way, hop) if hop else True))
                def _():
                    along(way, hop, sub).wait_send()
            for hop in range(1, last + 1):
                @pl.when(arrives(way, hop))
                def _():
                    sideways(way, hop, sub).wait_send()
                    inward(way, 0, hop, sub).wait_send()
                    inward(way, 1, hop, sub).wait_send()

    each_sub(settle)


def crossed(queries, keys_values, out_weight, repeat):
    frames, width = queries.shape
    kv_width = keys_values.shape[1] // 2
    depth, block = out_weight.shape
    count = width // HEAD_DIM
    dma = pltpu.SemaphoreType.DMA
    anywhere = pl.BlockSpec(memory_space=pl.ANY)
    vmem = pl.BlockSpec(memory_space=pltpu.VMEM)
    bf16, f32 = jnp.bfloat16, jnp.float32
    return pl.pallas_call(
        functools.partial(cross_kernel, repeat),
        out_shape=jax.ShapeDtypeStruct((frames, 4 * block), bf16),
        in_specs=[vmem, vmem, anywhere],
        out_specs=vmem,
        scratch_shapes=[
            pltpu.VMEM((8 * frames, 2 * kv_width), bf16),
            pltpu.VMEM((8, SUBS, depth, block // SUBS), bf16),
            pltpu.VMEM((count, 1, frames), f32),
            pltpu.VMEM((count, 1, frames), f32),
            pltpu.VMEM((count, HEAD_DIM, frames), f32),
            pltpu.VMEM((frames, width), bf16),
            pltpu.VMEM((2 * SUBS, frames, 2 * block // SUBS), bf16),
            pltpu.VMEM((2 * SUBS, frames, 2 * block // SUBS), bf16),
            pltpu.VMEM((2 * SUBS, frames, 2 * block // SUBS), bf16),
            dma((SUBS,)), dma((SUBS,)), dma((SUBS,)),
            dma((3, SUBS)), dma((3, SUBS)),
            dma((4, SUBS)), dma((4, SUBS)),
            dma((2, 3, SUBS)), dma((2, 3, SUBS)),
            dma((2, 3, SUBS)), dma((2, 3, SUBS)),
            dma((2, 2, 3, SUBS)), dma((2, 2, 3, SUBS)),
            dma, dma, dma((2 * SUBS,)), dma((2 * SUBS,)),
        ],
        compiler_params=pltpu.CompilerParams(
            collective_id=1, has_side_effects=True, vmem_limit_bytes=58 * 1024 * 1024
        ),
        cost_estimate=pl.CostEstimate(
            flops=16 * frames * depth * block, bytes_accessed=4 * queries.size, transcendentals=4 * frames * frames * count
        ),
    )(queries, keys_values, out_weight)


def y_share(mine, core, after=None):
    depth = mine.shape[0] // 2
    part = lax.dynamic_slice_in_dim(mine, core * depth, depth, 0)
    near = lax.ppermute(part, "stream", [(0, 1), (1, 0)])
    if after is None:
        return near, swap_pairs(near, "seq")
    near, after = lax.optimization_barrier((near, after))
    return near, swap_pairs(near, "seq"), after


def fits(hidden, query_weight, key_weight):
    meshes = (lax.axis_size("stream"), lax.axis_size("seq"), lax.axis_size("tensor"))
    return (
        meshes == (2, 8, 2)
        and hidden.shape[1:] == (1, 512, 2048)
        and query_weight.shape == (512, 2048)
        and key_weight.shape == (512, 512)
    )


def body(hidden, norm_gain, query_weight, key_weight, value_projection_weight, out_weight):
    if not fits(hidden, query_weight, key_weight):
        return general_body(hidden, norm_gain, query_weight, key_weight, value_projection_weight, out_weight)
    queries, keys_values = projected(
        hidden.reshape(hidden.shape[2:]), norm_gain, query_weight, key_weight, value_projection_weight
    )
    out = crossed(queries, keys_values, out_weight, query_weight.shape[1] // key_weight.shape[1])
    return out.reshape(hidden.shape)


def general_body(hidden, norm_gain, query_weight, key_weight, value_projection_weight, out_weight):
    windows, frame_count = hidden.shape[1], hidden.shape[2]
    n_tensor = lax.axis_size("tensor")
    n_seq = lax.axis_size("seq")
    stream = lax.axis_index("stream")
    tensor = lax.axis_index("tensor")
    seq = lax.axis_index("seq")
    core = seq % 2
    rows = windows * frame_count
    depth = query_weight.shape[0] // 2
    out_half = out_weight.shape[1] // 2

    kv_weight = jnp.concatenate([key_weight, value_projection_weight], axis=1)
    kv_mine = lax.all_gather(
        lax.dynamic_slice_in_dim(kv_weight, stream * depth, depth, 0), "seq", axis=0, tiled=True
    )
    query_mine = lax.all_gather(
        lax.dynamic_slice_in_dim(query_weight, stream * depth, depth, 0), "seq", axis=0, tiled=True
    )
    out_mine = lax.all_gather(
        lax.dynamic_slice_in_dim(out_weight, stream * out_half, out_half, 1), "seq", axis=1, tiled=True
    )

    local = hidden.reshape(rows, hidden.shape[3])
    if n_tensor == 2:
        other = lax.ppermute(local, "tensor", [(0, 1), (1, 0)])
        gathered = jnp.where(
            tensor == 0,
            jnp.concatenate([local, other], axis=1),
            jnp.concatenate([other, local], axis=1),
        )
    else:
        gathered = lax.all_gather(local, "tensor", axis=1, tiled=True)
    flat = gathered.astype(jnp.float32)
    inverse_rms = lax.rsqrt(jnp.mean(flat * flat, axis=1, keepdims=True) + 1e-05)
    normed = (flat * inverse_rms * norm_gain).astype(jnp.bfloat16)
    split = normed.reshape(rows, n_seq, 2, depth)

    def features(half):
        return lax.dynamic_index_in_dim(split, half, 2, keepdims=False).reshape(rows, n_seq * depth)

    normed_mine = features(stream)
    normed_other = features(1 - stream)
    span = n_seq * depth // 2
    normed_near = lax.dynamic_slice_in_dim(normed_other, core * span, span, 1)
    normed_far = lax.dynamic_slice_in_dim(normed_other, (1 - core) * span, span, 1)

    def project(mine, near, far):
        total = jnp.dot(normed_mine, mine, preferred_element_type=jnp.float32)
        total += jnp.dot(normed_near, near, preferred_element_type=jnp.float32)
        total += jnp.dot(normed_far, far, preferred_element_type=jnp.float32)
        return total.astype(jnp.bfloat16)

    keys_values = project(kv_mine, *y_share(kv_mine, core))
    partner = lax.ppermute(keys_values, "stream", [(0, 1), (1, 0)])
    kv_width = key_weight.shape[1]
    parts = 2 if kv_width % (2 * HEAD_DIM) == 0 else 1
    step = kv_width // parts
    pieces = []
    for part in range(parts):
        columns = jnp.concatenate(
            [partner[:, part * step:(part + 1) * step],
             partner[:, kv_width + part * step:kv_width + (part + 1) * step]],
            axis=1,
        )
        pieces.append(
            lax.all_gather(columns.reshape(windows, frame_count, 2 * step), "seq", axis=1, tiled=True)
        )
    queries = project(query_mine, *y_share(query_mine, core)).reshape(windows, frame_count, -1)
    out_near = out_far = None
    width = out_weight.shape[0] // 2

    repeat = query_weight.shape[1] // key_weight.shape[1]
    chunk = frame_count // ROW_CHUNKS

    def scattered(share):
        if n_tensor == 2:
            wide = share.shape[1] // 2
            away = lax.dynamic_slice_in_dim(share, (1 - tensor) * wide, wide, 1)
            kept = lax.dynamic_slice_in_dim(share, tensor * wide, wide, 1)
            came = lax.ppermute(away, "tensor", [(0, 1), (1, 0)])
            return (kept.astype(jnp.float32) + came.astype(jnp.float32)).astype(jnp.bfloat16)
        return lax.psum_scatter(share, "tensor", scatter_dimension=1, tiled=True)

    outs = []
    q_step = step * repeat
    for window in range(windows):
        early = [
            attend(
                seq * frame_count,
                queries[window][:, part * q_step:(part + 1) * q_step],
                pieces[part][window],
                repeat,
            )
            for part in range(parts - 1)
        ]
        for index in range(ROW_CHUNKS):
            low, high = index * chunk, (index + 1) * chunk
            final = attend(
                seq * frame_count + low,
                queries[window][low:high, (parts - 1) * q_step:],
                pieces[-1][window],
                repeat,
            )
            attended = jnp.concatenate([done[low:high] for done in early] + [final], axis=1)
            share_mine = jnp.dot(attended, out_mine, preferred_element_type=jnp.float32)
            if out_near is None:
                out_near, out_far, attended = y_share(out_mine, core, attended)
            attended_near = lax.dynamic_slice_in_dim(attended, core * width, width, 1)
            attended_far = lax.dynamic_slice_in_dim(attended, (1 - core) * width, width, 1)
            share_other = jnp.dot(attended_near, out_near, preferred_element_type=jnp.float32)
            share_other += jnp.dot(attended_far, out_far, preferred_element_type=jnp.float32)
            mine = scattered(share_mine.astype(jnp.bfloat16)).reshape(chunk, -1, out_half)
            other = scattered(share_other.astype(jnp.bfloat16)).reshape(chunk, -1, out_half)
            outs.append(
                jnp.where(
                    stream == 0, jnp.stack([mine, other], axis=2), jnp.stack([other, mine], axis=2)
                ).reshape(chunk, -1)
            )
    return jnp.concatenate(outs, axis=0).reshape(1, windows, frame_count, -1)


def solution(mesh):
    in_specs = (
        P("stream", None, "seq", "tensor"),
        P(),
        P("seq", "tensor"),
        P("seq", "tensor"),
        P("seq", "tensor"),
        P("tensor", "seq"),
    )
    out_specs = P("stream", None, "seq", "tensor")
    return jax.shard_map(body, mesh=mesh, in_specs=in_specs, out_specs=out_specs, check_vma=False)
```

```python
import functools

import jax
import jax.numpy as jnp
from jax import lax
from jax.experimental import pallas as pl
from jax.experimental.pallas import tpu as pltpu
from jax.sharding import PartitionSpec as P

HEAD_DIM = 128
ROW_CHUNKS = 2
KEY_BLOCK = 1024
SUBS = 4
LOG2E = 1.4426950408889634


def swap_pairs(block, axis):
    count = lax.axis_size(axis)
    return lax.ppermute(block, axis, [(i, i ^ 1) for i in range(count)])


def attend_kernel(repeat, start_ref, q_ref, k_ref, v_ref, o_ref, m_ref, l_ref, acc_ref):
    step = pl.program_id(1)
    rows = q_ref.shape[0]
    keys = k_ref.shape[0]
    start = start_ref[0]
    last = (start + rows - 1) // keys
    scale = LOG2E * HEAD_DIM ** (-0.5)

    @pl.when(step == 0)
    def _():
        m_ref[...] = jnp.full_like(m_ref, -1e30)
        l_ref[...] = jnp.zeros_like(l_ref)
        acc_ref[...] = jnp.zeros_like(acc_ref)

    def update(masked):
        k = k_ref[...]
        v = v_ref[...]
        if masked:
            frame = start + lax.broadcasted_iota(jnp.int32, (keys, rows), 1)
            key = step * keys + lax.broadcasted_iota(jnp.int32, (keys, rows), 0)
            allowed = key <= frame

        def scored(r):
            q = q_ref[:, r * HEAD_DIM:(r + 1) * HEAD_DIM]
            return lax.dot_general(k, q, (((1,), (1,)), ((), ())), preferred_element_type=jnp.float32)

        following = scored(0)
        for r in range(repeat):
            s = following
            if r + 1 < repeat:
                following = scored(r + 1)
            if masked:
                s = jnp.where(allowed, s, -1e30)
            top = jnp.max(s, axis=0, keepdims=True) * scale
            before = m_ref[r]
            fresh = jnp.maximum(before, top)
            m_ref[r] = fresh
            alpha = jnp.exp2(before - fresh)
            p = jnp.exp2(s * scale - fresh)
            l_ref[r] = alpha * l_ref[r] + jnp.sum(p, axis=0, keepdims=True)
            acc_ref[r] = alpha * acc_ref[r] + lax.dot_general(
                v, p.astype(jnp.bfloat16), (((0,), (0,)), ((), ())), preferred_element_type=jnp.float32
            )

    @pl.when(step < last)
    def _():
        update(False)

    @pl.when(step == last)
    def _():
        update(True)
        for r in range(repeat):
            attended = (acc_ref[r] / l_ref[r]).T
            o_ref[:, r * HEAD_DIM:(r + 1) * HEAD_DIM] = attended.astype(o_ref.dtype)


def attend(start, queries, keys_values, repeat):
    rows, width = queries.shape
    count = keys_values.shape[0]
    groups = width // (repeat * HEAD_DIM)
    block = min(KEY_BLOCK, count)

    def at(step, start_ref):
        return jnp.minimum(step, (start_ref[0] + rows - 1) // block)

    return pl.pallas_call(
        functools.partial(attend_kernel, repeat),
        out_shape=jax.ShapeDtypeStruct((rows, width), jnp.bfloat16),
        grid_spec=pltpu.PrefetchScalarGridSpec(
            num_scalar_prefetch=1,
            grid=(groups, count // block),
            in_specs=[
                pl.BlockSpec((rows, repeat * HEAD_DIM), lambda g, i, s: (0, g)),
                pl.BlockSpec((block, HEAD_DIM), lambda g, i, s: (at(i, s), g)),
                pl.BlockSpec((block, HEAD_DIM), lambda g, i, s: (at(i, s), groups + g)),
            ],
            out_specs=pl.BlockSpec((rows, repeat * HEAD_DIM), lambda g, i, s: (0, g)),
            scratch_shapes=[
                pltpu.VMEM((repeat, 1, rows), jnp.float32),
                pltpu.VMEM((repeat, 1, rows), jnp.float32),
                pltpu.VMEM((repeat, HEAD_DIM, rows), jnp.float32),
            ],
        ),
        compiler_params=pltpu.CompilerParams(
            dimension_semantics=("arbitrary", "arbitrary"), vmem_limit_bytes=32 * 1024 * 1024
        ),
        cost_estimate=pl.CostEstimate(
            flops=8 * rows * count * width,
            bytes_accessed=2 * (2 * rows * width + keys_values.size),
            transcendentals=rows * count * width // HEAD_DIM,
        ),
    )(start.reshape(1), queries, keys_values, keys_values)


def line_order(z):
    first = z - 1 + 2 * ((3 - z) // 3)
    third = 3 * (1 - z // 2)
    return (z, first, 6 - z - first - third, third)


def remote(src, dst, send, recv, device):
    return pltpu.make_async_remote_copy(
        src_ref=src, dst_ref=dst, send_sem=send, recv_sem=recv, device_id=device, device_id_type=pl.DeviceIdType.MESH
    )


def greet(z, last, devices, up, down):
    barrier = pltpu.get_barrier_semaphore()

    def hello(device):
        pl.semaphore_signal(barrier, inc=1, device_id=device, device_id_type=pl.DeviceIdType.MESH)

    for device in devices:
        hello(device)

    @pl.when(z < last)
    def _():
        hello(up)

    @pl.when(z > 0)
    def _():
        hello(down)

    inner = jnp.where((z > 0) & (z < last), 1, 0)
    pl.semaphore_wait(barrier, len(devices) + 1 + inner)


def cross_kernel(
    repeat, gain_ref, hidden_ref, wq_ref, wk_ref, wv_ref, wo_ref, out_ref, wo,
    w, hid, normed, acc_ref, kv, m_ref, l_ref, came,
    fill_sem, wo_sem, stage_sem, cross_s, cross_r, swap_s, swap_r, k_s, k_r, kc_s, kc_r,
    wz_s, wz_r, wy_s, wy_r, wc_s, wc_r, w_own_s, w_own_r,
    oz_s, oz_r, oy_s, oy_r, oc_s, oc_r, o_own_s, o_own_r, x_s, x_r,
):
    last = 3
    c = lax.axis_index("stream")
    s = lax.axis_index("seq")
    t = lax.axis_index("tensor")
    z, k = s // 2, s % 2
    depth, q_width = wq_ref.shape
    half = depth // 2
    rows = half // SUBS
    kv_width = wk_ref.shape[1]
    frames = hid.shape[1]
    step = frames // SUBS
    out_depth, block = wo_ref.shape
    out_half = out_depth // 2
    wide = block // SUBS
    keys = frames // SUBS
    heads = kv_width // HEAD_DIM
    scale = LOG2E * HEAD_DIM ** (-0.5)
    at = {"stream": c, "seq": s, "tensor": t}
    up, down = {**at, "seq": s + 2}, {**at, "seq": s - 2}
    beside, mate, across = {**at, "stream": 1 - c}, {**at, "seq": 2 * z + 1 - k}, {**at, "tensor": 1 - t}
    greet(z, last, (beside, mate, across), up, down)
    sends = (z < last, z > 0)

    def each_sub(action):
        @pl.loop(0, SUBS)
        def _(sub):
            action(sub)

    def source(way, hop):
        return z - hop if way == 0 else z + hop

    def arrives(way, hop):
        return z >= hop if way == 0 else z + hop <= last

    def w_part(origin, core, side, sub):
        start = pl.multiple_of(origin * (2 * depth) + core * depth + side * half + sub * rows, rows)
        return w.at[pl.ds(start, rows)]

    def o_part(origin, core, side, sub):
        return wo.at[2 * origin + core, sub, pl.ds(pl.multiple_of(side * out_half, out_half), out_half)]

    def routes(part, z_s, z_r, y_s, y_r, c_s, c_r):
        def along(way, hop, sub):
            view = part(source(way, hop), k, c, sub)
            return remote(view, view, z_s.at[way, hop, sub], z_r.at[way, hop, sub], up if way == 0 else down)

        def sideways(way, hop, sub):
            view = part(source(way, hop), k, c, sub)
            return remote(view, view, y_s.at[way, hop - 1, sub], y_r.at[way, hop - 1, sub], beside)

        def inward(way, kind, hop, sub):
            view = part(source(way, hop), k, c if kind == 0 else 1 - c, sub)
            return remote(view, view, c_s.at[way, kind, hop - 1, sub], c_r.at[way, kind, hop - 1, sub], mate)

        def leave(way):
            @pl.when(sends[way])
            def _():
                each_sub(lambda sub: along(way, 0, sub).start())

        def pass_on(way, hop, sub):
            @pl.when(arrives(way, hop))
            def _():
                along(way, hop - 1, sub).wait_recv()

                @pl.when(sends[way] & (hop < last))
                def _():
                    along(way, hop, sub).start()

                sideways(way, hop, sub).start()
                inward(way, 0, hop, sub).start()

        def pass_in(way, hop, sub):
            @pl.when(arrives(way, hop))
            def _():
                sideways(way, hop, sub).wait_recv()
                inward(way, 1, hop, sub).start()

        def gathered(way, hop):
            @pl.when(arrives(way, hop))
            def _():
                def action(sub):
                    inward(way, 0, hop, sub).wait_recv()
                    inward(way, 1, hop, sub).wait_recv()

                each_sub(action)

        def settle(sub):
            for way in range(2):
                for hop in range(last):
                    @pl.when(sends[way] & arrives(way, hop))
                    def _():
                        along(way, hop, sub).wait_send()
                for hop in range(1, last + 1):
                    @pl.when(arrives(way, hop))
                    def _():
                        sideways(way, hop, sub).wait_send()
                        inward(way, 0, hop, sub).wait_send()
                        inward(way, 1, hop, sub).wait_send()

        return leave, pass_on, pass_in, gathered, settle, inward

    w_leave, w_on, w_in, w_gathered, w_settle, _ = routes(w_part, wz_s, wz_r, wy_s, wy_r, wc_s, wc_r)
    o_leave, o_on, o_in, o_gathered, o_settle, o_inward = routes(o_part, oz_s, oz_r, oy_s, oy_r, oc_s, oc_r)

    own = pl.multiple_of(s * depth, depth)
    fills = [
        pltpu.make_async_copy(wq_ref, w.at[pl.ds(own, depth), pl.ds(0, q_width)], fill_sem.at[0]),
        pltpu.make_async_copy(wk_ref, w.at[pl.ds(own, depth), pl.ds(q_width, kv_width)], fill_sem.at[1]),
        pltpu.make_async_copy(wv_ref, w.at[pl.ds(own, depth), pl.ds(q_width + kv_width, kv_width)], fill_sem.at[2]),
    ]
    mine = pltpu.make_async_copy(hidden_ref, hid.at[t], fill_sem.at[3])
    wo_fills = [
        pltpu.make_async_copy(wo_ref.at[:, pl.ds(sub * wide, wide)], wo.at[s, sub], wo_sem.at[sub])
        for sub in range(SUBS)
    ]

    def crossing(piece):
        start = pl.multiple_of(piece * step, step)
        return remote(
            hidden_ref.at[pl.ds(start, step)], hid.at[t, pl.ds(start, step)],
            cross_s.at[piece], cross_r.at[piece], across,
        )

    for copy in fills:
        copy.start()
    mine.start()
    each_sub(lambda piece: crossing(piece).start())
    for copy in fills:
        copy.wait()
    for way in range(2):
        w_leave(way)
    w_block = w.at[pl.ds(own, depth)]
    w_whole = remote(w_block, w_block, w_own_s, w_own_r, mate)
    w_whole.start()
    for copy in wo_fills:
        copy.start()

    tall = 16

    def norm(sub):
        crossing(sub).wait_recv()

        @pl.loop(0, step // tall)
        def _(i):
            at_rows = pl.ds(pl.multiple_of(sub * step + i * tall, tall), tall)
            low = hid[0, at_rows, :].astype(jnp.float32)
            high = hid[1, at_rows, :].astype(jnp.float32)
            total = jnp.sum(low * low, axis=1, keepdims=True) + jnp.sum(high * high, axis=1, keepdims=True)
            inverse_rms = lax.rsqrt(total / (2 * low.shape[1]) + 1e-05)
            part = normed.shape[2]
            for group in range(4):
                x = (low if group < 2 else high)[:, (group % 2) * part:(group % 2 + 1) * part]
                gain = gain_ref[:, group * part:(group + 1) * part]
                normed[group, at_rows, :] = (x * inverse_rms * gain).astype(jnp.bfloat16)

    order = line_order(z)
    tile = 512
    tiles = (q_width + 2 * kv_width) // tile
    q_tiles = q_width // tile
    folds = frames // HEAD_DIM

    def dot(place, index):
        group = order[place]
        columns = pl.ds(pl.multiple_of(index * tile, tile), tile)
        return jnp.dot(
            normed[group],
            w[pl.ds(pl.multiple_of(group * 2 * depth, 2 * depth), 2 * depth), columns],
            preferred_element_type=jnp.float32,
        )

    def held(index):
        return pl.ds(index * folds, folds)

    def project(place, low, high):
        @pl.loop(low, high)
        def _(index):
            value = dot(place, index).reshape(folds, HEAD_DIM, tile)
            if place == 0:
                acc_ref[held(index)] = value
            else:
                acc_ref[held(index)] += value

    def finish(index):
        total = acc_ref[held(index)].reshape(frames, tile) + dot(3, index)
        return total.astype(jnp.bfloat16)

    def first_hop(sub):
        for way in range(2):
            w_on(way, 1, sub)

    def second_hop(sub):
        for way in range(2):
            w_on(way, 2, sub)
            w_in(way, 1, sub)
        norm(sub)

    each_sub(first_hop)
    mine.wait()
    each_sub(second_hop)
    w_whole.wait_recv()
    for way in range(2):
        w_gathered(way, 1)
    for copy in wo_fills:
        copy.wait()
    for sub in range(SUBS):
        for way in range(2):
            w_on(way, 3, sub)
            w_in(way, 2, sub)
        if sub == SUBS - 1:
            for way in range(2):
                o_leave(way)
            o_whole = remote(wo.at[s], wo.at[s], o_own_s, o_own_r, mate)
            o_whole.start()
        low, high = sub * 2 * tiles // SUBS, (sub + 1) * 2 * tiles // SUBS
        for place in range(2):
            begin, end = max(low - place * tiles, 0), min(high - place * tiles, tiles)
            if begin < end:
                project(place, begin, end)
    for way in range(2):
        w_gathered(way, 2)
    project(2, 0, tiles)
    for way in range(2):
        each_sub(lambda sub: w_in(way, 3, sub))
        w_gathered(way, 3)

    for index in range(2 * kv_width // tile):
        hid[1, :, index * tile:(index + 1) * tile] = finish(q_tiles + index)

    def key_rows(hop, sub):
        start = pl.multiple_of((2 * (z - hop) + k) * frames + sub * keys, keys)
        return kv.at[pl.ds(start, keys)]

    def swap(sub):
        start = pl.multiple_of(sub * keys, keys)
        return remote(
            hid.at[1, pl.ds(start, keys), pl.ds(0, 2 * kv_width)], key_rows(0, sub),
            swap_s.at[sub], swap_r.at[sub], beside,
        )

    def climb(hop, sub):
        view = key_rows(hop, sub)
        return remote(view, view, k_s.at[hop, sub], k_r.at[hop, sub], up)

    def hand(hop, sub):
        view = key_rows(hop, sub)
        return remote(view, view, kc_s.at[hop, sub], kc_r.at[hop, sub], mate)

    def pass_keys(hop, sub):
        @pl.when(z >= hop)
        def _():
            climb(hop - 1, sub).wait_recv()
            if hop < last:
                @pl.when(z < last)
                def _():
                    climb(hop, sub).start()
            hand(hop, sub).start()

    def keys_held(hop):
        @pl.when(z >= hop)
        def _():
            each_sub(lambda sub: hand(hop, sub).wait_recv())

    each_sub(lambda sub: swap(sub).start())

    @pl.loop(0, q_tiles)
    def _(index):
        hid[0, :, pl.ds(pl.multiple_of(index * tile, tile), tile)] = finish(index)

    def attend_to(head, start, count, masked):
        at_keys = pl.ds(pl.multiple_of(start, count), count)
        keys_here = kv[at_keys, pl.ds(pl.multiple_of(head * HEAD_DIM, HEAD_DIM), HEAD_DIM)]
        values_here = kv[at_keys, pl.ds(pl.multiple_of(kv_width + head * HEAD_DIM, HEAD_DIM), HEAD_DIM)]
        if masked:
            allowed = lax.broadcasted_iota(jnp.int32, (count, frames), 0) <= lax.broadcasted_iota(
                jnp.int32, (count, frames), 1
            )

        def scored(r):
            q = hid[0, :, pl.ds(pl.multiple_of((head * repeat + r) * HEAD_DIM, HEAD_DIM), HEAD_DIM)]
            return lax.dot_general(
                keys_here, q, (((1,), (1,)), ((), ())), preferred_element_type=jnp.float32
            )

        following = scored(0)
        for r in range(repeat):
            index = head * repeat + r
            scores = following
            if r + 1 < repeat:
                following = scored(r + 1)
            if masked:
                scores = jnp.where(allowed, scores, -1e30)
            top = jnp.max(scores, axis=0, keepdims=True) * scale
            before = m_ref[index]
            fresh = jnp.maximum(before, top)
            m_ref[index] = fresh
            alpha = jnp.exp2(before - fresh)
            p = jnp.exp2(scores * scale - fresh)
            l_ref[index] = alpha * l_ref[index] + jnp.sum(p, axis=0, keepdims=True)
            acc_ref[index] = alpha * acc_ref[index] + lax.dot_general(
                values_here, p.astype(jnp.bfloat16), (((0,), (0,)), ((), ())), preferred_element_type=jnp.float32
            )

    def attend_own(head):
        attend_to(head, s * frames, frames, True)

        @pl.when(k == 1)
        def _():
            attend_to(head, (s - 1) * frames, frames, False)

    def attend_hop(hop, head):
        @pl.when(z >= hop)
        def _():
            attend_to(head, (z - hop) * 2 * frames, 2 * frames, False)

    m_ref[...] = jnp.full_like(m_ref, -1e30)
    l_ref[...] = jnp.zeros_like(l_ref)
    acc_ref[...] = jnp.zeros_like(acc_ref)

    def first(sub):
        swap(sub).wait_recv()

        @pl.when(z < last)
        def _():
            climb(0, sub).start()

        hand(0, sub).start()
        o_on(1, 1, sub)

    each_sub(first)
    keys_held(0)

    for hop in range(1, last + 1):
        def phase(sub):
            pass_keys(hop, sub)
            if hop < last:
                o_on(1, hop + 1, sub)
            o_in(1, hop, sub)
            if hop > 1:
                attend_hop(hop - 1, sub)
            else:
                attend_own(sub)

        each_sub(phase)
        keys_held(hop)

    def climbed(number):
        return number // SUBS + 1, number % SUBS

    def fourth(sub):
        o_on(0, 1, sub)

        @pl.when(sub > 0)
        def _():
            o_in(0, 1, sub - 1)

        attend_hop(last, sub)

    each_sub(fourth)

    w_whole.wait_send()
    each_sub(w_settle)
    attended = w.at[pl.ds(0, frames), pl.ds(0, q_width)]
    stage = w.at[pl.ds(4 * frames, out_depth), pl.ds(0, 2 * wide)]

    def slot_in(place, slot):
        return w.at[pl.ds(place * frames, frames), pl.ds(pl.multiple_of(slot * 2 * wide, 2 * wide), 2 * wide)]

    def kept(slot):
        return slot_in(1, slot)

    def leaving(slot):
        return slot_in(2, slot)

    def carry(slot):
        return remote(leaving(slot), came.at[slot], x_s.at[slot], x_r.at[slot], across)

    @pl.loop(0, heads)
    def _(head):
        for r in range(repeat):
            index = head * repeat + r
            out = (acc_ref[index] / l_ref[index]).T.astype(jnp.bfloat16)
            attended[:, pl.ds(pl.multiple_of(index * HEAD_DIM, HEAD_DIM), HEAD_DIM)] = out

    def shares(group, sub):
        loads = [
            pltpu.make_async_copy(
                wo.at[2 * group + core, sub],
                w.at[pl.ds(4 * frames, out_depth), pl.ds(core * wide, wide)],
                stage_sem.at[core],
            )
            for core in range(2)
        ]
        for load in loads:
            load.start()
        for load in loads:
            load.wait()
        share = jnp.dot(attended[...], stage[...], preferred_element_type=jnp.float32).astype(jnp.bfloat16)
        slot = (group % 2) * SUBS + sub

        @pl.when(group // 2 == t)
        def _():
            kept(slot)[...] = share

        @pl.when(group // 2 != t)
        def _():
            leaving(slot)[...] = share
            carry(slot).start()

    def work(number):
        hop, sub = climbed(number)

        @pl.when(arrives(0, hop))
        def _():
            o_inward(0, 0, hop, sub).wait_recv()
            o_inward(0, 1, hop, sub).wait_recv()
            shares(z - hop, sub)

    o_whole.wait_recv()
    each_sub(lambda sub: shares(z, sub))
    for hop in range(1, last + 1):
        o_gathered(1, hop)

        @pl.when(arrives(1, hop))
        def _():
            each_sub(lambda sub: shares(z + hop, sub))

    @pl.loop(0, SUBS - 2)
    def _(number):
        work(number)

    @pl.loop(SUBS, last * SUBS)
    def _(number):
        o_on(0, *climbed(number))
        o_in(0, *climbed(number - 1))
        work(number - 2)

    o_in(0, last, SUBS - 1)
    work(last * SUBS - 2)
    work(last * SUBS - 1)

    high_first = z // 2

    @pl.loop(0, 2 * SUBS)
    def _(number):
        side, sub = number // SUBS, number % SUBS
        side = side + high_first * (1 - 2 * side)
        slot = side * SUBS + sub
        carry(slot).wait_recv()
        total = (kept(slot)[...].astype(jnp.float32) + came[slot].astype(jnp.float32)).astype(jnp.bfloat16)
        for core in range(2):
            start = pl.multiple_of((side * 2 + core) * block + sub * wide, wide)
            out_ref[:, pl.ds(start, wide)] = total[:, core * wide:(core + 1) * wide]

    o_whole.wait_send()

    @pl.loop(0, 2 * SUBS)
    def _(slot):
        carry(slot).wait_send()

    def settle(sub):
        crossing(sub).wait_send()
        swap(sub).wait_send()
        for hop in range(last + 1):
            @pl.when(z >= hop)
            def _():
                hand(hop, sub).wait_send()
                if hop < last:
                    @pl.when(z < last)
                    def _():
                        climb(hop, sub).wait_send()
        o_settle(sub)

    each_sub(settle)


def crossed(hidden, norm_gain, query_weight, key_weight, value_weight, out_weight):
    frames, features = hidden.shape
    depth, q_width = query_weight.shape
    kv_width = key_weight.shape[1]
    repeat = q_width // kv_width
    total = q_width + 2 * kv_width
    out_depth, block = out_weight.shape
    wide = block // SUBS
    count = q_width // HEAD_DIM
    dma = pltpu.SemaphoreType.DMA
    anywhere = pl.BlockSpec(memory_space=pl.ANY)
    vmem = pl.BlockSpec(memory_space=pltpu.VMEM)
    bf16, f32 = jnp.bfloat16, jnp.float32
    line = [dma((2, 3, SUBS))] * 4 + [dma((2, 2, 3, SUBS))] * 2 + [dma] * 2
    out, _ = pl.pallas_call(
        functools.partial(cross_kernel, repeat),
        out_shape=(
            jax.ShapeDtypeStruct((frames, 4 * block), bf16),
            jax.ShapeDtypeStruct((8, SUBS, out_depth, wide), bf16),
        ),
        in_specs=[vmem] + [anywhere] * 5,
        out_specs=(vmem, anywhere),
        scratch_shapes=[
            pltpu.VMEM((8 * depth, total), bf16),
            pltpu.VMEM((2, frames, features), bf16),
            pltpu.VMEM((4, frames, features // 2), bf16),
            pltpu.VMEM((total // HEAD_DIM, HEAD_DIM, frames), f32),
            pltpu.VMEM((8 * frames, 2 * kv_width), bf16),
            pltpu.VMEM((count, 1, frames), f32),
            pltpu.VMEM((count, 1, frames), f32),
            pltpu.VMEM((2 * SUBS, frames, 2 * wide), bf16),
            dma((4,)), dma((SUBS,)), dma((2,)),
            dma((SUBS,)), dma((SUBS,)), dma((SUBS,)), dma((SUBS,)),
            dma((3, SUBS)), dma((3, SUBS)), dma((4, SUBS)), dma((4, SUBS)),
            *line, *line,
            dma((2 * SUBS,)), dma((2 * SUBS,)),
        ],
        compiler_params=pltpu.CompilerParams(
            collective_id=0, has_side_effects=True, vmem_limit_bytes=60 * 1024 * 1024
        ),
        cost_estimate=pl.CostEstimate(
            flops=16 * frames * depth * total + 16 * frames * out_depth * block,
            bytes_accessed=4 * hidden.size,
            transcendentals=4 * frames * frames * count,
        ),
    )(norm_gain.reshape(1, -1), hidden, query_weight, key_weight, value_weight, out_weight)
    return out


def y_share(mine, core, after=None):
    depth = mine.shape[0] // 2
    part = lax.dynamic_slice_in_dim(mine, core * depth, depth, 0)
    near = lax.ppermute(part, "stream", [(0, 1), (1, 0)])
    if after is None:
        return near, swap_pairs(near, "seq")
    near, after = lax.optimization_barrier((near, after))
    return near, swap_pairs(near, "seq"), after


def fits(hidden, query_weight, key_weight):
    meshes = (lax.axis_size("stream"), lax.axis_size("seq"), lax.axis_size("tensor"))
    return (
        meshes == (2, 8, 2)
        and hidden.shape[1:] == (1, 512, 2048)
        and query_weight.shape == (512, 2048)
        and key_weight.shape == (512, 512)
    )


def body(hidden, norm_gain, query_weight, key_weight, value_projection_weight, out_weight):
    if not fits(hidden, query_weight, key_weight):
        return general_body(hidden, norm_gain, query_weight, key_weight, value_projection_weight, out_weight)
    out = crossed(
        hidden.reshape(hidden.shape[2:]), norm_gain, query_weight, key_weight, value_projection_weight, out_weight
    )
    return out.reshape(hidden.shape)


def general_body(hidden, norm_gain, query_weight, key_weight, value_projection_weight, out_weight):
    windows, frame_count = hidden.shape[1], hidden.shape[2]
    n_tensor = lax.axis_size("tensor")
    n_seq = lax.axis_size("seq")
    stream = lax.axis_index("stream")
    tensor = lax.axis_index("tensor")
    seq = lax.axis_index("seq")
    core = seq % 2
    rows = windows * frame_count
    depth = query_weight.shape[0] // 2
    out_half = out_weight.shape[1] // 2

    kv_weight = jnp.concatenate([key_weight, value_projection_weight], axis=1)
    kv_mine = lax.all_gather(
        lax.dynamic_slice_in_dim(kv_weight, stream * depth, depth, 0), "seq", axis=0, tiled=True
    )
    query_mine = lax.all_gather(
        lax.dynamic_slice_in_dim(query_weight, stream * depth, depth, 0), "seq", axis=0, tiled=True
    )
    out_mine = lax.all_gather(
        lax.dynamic_slice_in_dim(out_weight, stream * out_half, out_half, 1), "seq", axis=1, tiled=True
    )

    local = hidden.reshape(rows, hidden.shape[3])
    if n_tensor == 2:
        other = lax.ppermute(local, "tensor", [(0, 1), (1, 0)])
        gathered = jnp.where(
            tensor == 0,
            jnp.concatenate([local, other], axis=1),
            jnp.concatenate([other, local], axis=1),
        )
    else:
        gathered = lax.all_gather(local, "tensor", axis=1, tiled=True)
    flat = gathered.astype(jnp.float32)
    inverse_rms = lax.rsqrt(jnp.mean(flat * flat, axis=1, keepdims=True) + 1e-05)
    normed = (flat * inverse_rms * norm_gain).astype(jnp.bfloat16)
    split = normed.reshape(rows, n_seq, 2, depth)

    def features(half):
        return lax.dynamic_index_in_dim(split, half, 2, keepdims=False).reshape(rows, n_seq * depth)

    normed_mine = features(stream)
    normed_other = features(1 - stream)
    span = n_seq * depth // 2
    normed_near = lax.dynamic_slice_in_dim(normed_other, core * span, span, 1)
    normed_far = lax.dynamic_slice_in_dim(normed_other, (1 - core) * span, span, 1)

    def project(mine, near, far):
        total = jnp.dot(normed_mine, mine, preferred_element_type=jnp.float32)
        total += jnp.dot(normed_near, near, preferred_element_type=jnp.float32)
        total += jnp.dot(normed_far, far, preferred_element_type=jnp.float32)
        return total.astype(jnp.bfloat16)

    keys_values = project(kv_mine, *y_share(kv_mine, core))
    partner = lax.ppermute(keys_values, "stream", [(0, 1), (1, 0)])
    kv_width = key_weight.shape[1]
    parts = 2 if kv_width % (2 * HEAD_DIM) == 0 else 1
    step = kv_width // parts
    pieces = []
    for part in range(parts):
        columns = jnp.concatenate(
            [partner[:, part * step:(part + 1) * step],
             partner[:, kv_width + part * step:kv_width + (part + 1) * step]],
            axis=1,
        )
        pieces.append(
            lax.all_gather(columns.reshape(windows, frame_count, 2 * step), "seq", axis=1, tiled=True)
        )
    queries = project(query_mine, *y_share(query_mine, core)).reshape(windows, frame_count, -1)
    out_near = out_far = None
    width = out_weight.shape[0] // 2

    repeat = query_weight.shape[1] // key_weight.shape[1]
    chunk = frame_count // ROW_CHUNKS

    def scattered(share):
        if n_tensor == 2:
            wide = share.shape[1] // 2
            away = lax.dynamic_slice_in_dim(share, (1 - tensor) * wide, wide, 1)
            kept = lax.dynamic_slice_in_dim(share, tensor * wide, wide, 1)
            came = lax.ppermute(away, "tensor", [(0, 1), (1, 0)])
            return (kept.astype(jnp.float32) + came.astype(jnp.float32)).astype(jnp.bfloat16)
        return lax.psum_scatter(share, "tensor", scatter_dimension=1, tiled=True)

    outs = []
    q_step = step * repeat
    for window in range(windows):
        early = [
            attend(
                seq * frame_count,
                queries[window][:, part * q_step:(part + 1) * q_step],
                pieces[part][window],
                repeat,
            )
            for part in range(parts - 1)
        ]
        for index in range(ROW_CHUNKS):
            low, high = index * chunk, (index + 1) * chunk
            final = attend(
                seq * frame_count + low,
                queries[window][low:high, (parts - 1) * q_step:],
                pieces[-1][window],
                repeat,
            )
            attended = jnp.concatenate([done[low:high] for done in early] + [final], axis=1)
            share_mine = jnp.dot(attended, out_mine, preferred_element_type=jnp.float32)
            if out_near is None:
                out_near, out_far, attended = y_share(out_mine, core, attended)
            attended_near = lax.dynamic_slice_in_dim(attended, core * width, width, 1)
            attended_far = lax.dynamic_slice_in_dim(attended, (1 - core) * width, width, 1)
            share_other = jnp.dot(attended_near, out_near, preferred_element_type=jnp.float32)
            share_other += jnp.dot(attended_far, out_far, preferred_element_type=jnp.float32)
            mine = scattered(share_mine.astype(jnp.bfloat16)).reshape(chunk, -1, out_half)
            other = scattered(share_other.astype(jnp.bfloat16)).reshape(chunk, -1, out_half)
            outs.append(
                jnp.where(
                    stream == 0, jnp.stack([mine, other], axis=2), jnp.stack([other, mine], axis=2)
                ).reshape(chunk, -1)
            )
    return jnp.concatenate(outs, axis=0).reshape(1, windows, frame_count, -1)


def solution(mesh):
    in_specs = (
        P("stream", None, "seq", "tensor"),
        P(),
        P("seq", "tensor"),
        P("seq", "tensor"),
        P("seq", "tensor"),
        P("tensor", "seq"),
    )
    out_specs = P("stream", None, "seq", "tensor")
    return jax.shard_map(body, mesh=mesh, in_specs=in_specs, out_specs=out_specs, check_vma=False)
```

```python
import functools

import jax
import jax.numpy as jnp
from jax import lax
from jax.experimental import pallas as pl
from jax.experimental.pallas import tpu as pltpu
from jax.sharding import PartitionSpec as P

HEAD_DIM = 128
ROW_CHUNKS = 2
KEY_BLOCK = 1024
SUBS = 4
LOG2E = 1.4426950408889634


def swap_pairs(block, axis):
    count = lax.axis_size(axis)
    return lax.ppermute(block, axis, [(i, i ^ 1) for i in range(count)])


def attend_kernel(repeat, start_ref, q_ref, k_ref, v_ref, o_ref, m_ref, l_ref, acc_ref):
    step = pl.program_id(1)
    rows = q_ref.shape[0]
    keys = k_ref.shape[0]
    start = start_ref[0]
    last = (start + rows - 1) // keys
    scale = LOG2E * HEAD_DIM ** (-0.5)

    @pl.when(step == 0)
    def _():
        m_ref[...] = jnp.full_like(m_ref, -1e30)
        l_ref[...] = jnp.zeros_like(l_ref)
        acc_ref[...] = jnp.zeros_like(acc_ref)

    def update(masked):
        k = k_ref[...]
        v = v_ref[...]
        if masked:
            frame = start + lax.broadcasted_iota(jnp.int32, (keys, rows), 1)
            key = step * keys + lax.broadcasted_iota(jnp.int32, (keys, rows), 0)
            allowed = key <= frame

        def scored(r):
            q = q_ref[:, r * HEAD_DIM:(r + 1) * HEAD_DIM]
            return lax.dot_general(k, q, (((1,), (1,)), ((), ())), preferred_element_type=jnp.float32)

        following = scored(0)
        for r in range(repeat):
            s = following
            if r + 1 < repeat:
                following = scored(r + 1)
            if masked:
                s = jnp.where(allowed, s, -1e30)
            top = jnp.max(s, axis=0, keepdims=True) * scale
            before = m_ref[r]
            fresh = jnp.maximum(before, top)
            m_ref[r] = fresh
            alpha = jnp.exp2(before - fresh)
            p = jnp.exp2(s * scale - fresh)
            l_ref[r] = alpha * l_ref[r] + jnp.sum(p, axis=0, keepdims=True)
            acc_ref[r] = alpha * acc_ref[r] + lax.dot_general(
                v, p.astype(jnp.bfloat16), (((0,), (0,)), ((), ())), preferred_element_type=jnp.float32
            )

    @pl.when(step < last)
    def _():
        update(False)

    @pl.when(step == last)
    def _():
        update(True)
        for r in range(repeat):
            attended = (acc_ref[r] / l_ref[r]).T
            o_ref[:, r * HEAD_DIM:(r + 1) * HEAD_DIM] = attended.astype(o_ref.dtype)


def attend(start, queries, keys_values, repeat):
    rows, width = queries.shape
    count = keys_values.shape[0]
    groups = width // (repeat * HEAD_DIM)
    block = min(KEY_BLOCK, count)

    def at(step, start_ref):
        return jnp.minimum(step, (start_ref[0] + rows - 1) // block)

    return pl.pallas_call(
        functools.partial(attend_kernel, repeat),
        out_shape=jax.ShapeDtypeStruct((rows, width), jnp.bfloat16),
        grid_spec=pltpu.PrefetchScalarGridSpec(
            num_scalar_prefetch=1,
            grid=(groups, count // block),
            in_specs=[
                pl.BlockSpec((rows, repeat * HEAD_DIM), lambda g, i, s: (0, g)),
                pl.BlockSpec((block, HEAD_DIM), lambda g, i, s: (at(i, s), g)),
                pl.BlockSpec((block, HEAD_DIM), lambda g, i, s: (at(i, s), groups + g)),
            ],
            out_specs=pl.BlockSpec((rows, repeat * HEAD_DIM), lambda g, i, s: (0, g)),
            scratch_shapes=[
                pltpu.VMEM((repeat, 1, rows), jnp.float32),
                pltpu.VMEM((repeat, 1, rows), jnp.float32),
                pltpu.VMEM((repeat, HEAD_DIM, rows), jnp.float32),
            ],
        ),
        compiler_params=pltpu.CompilerParams(
            dimension_semantics=("arbitrary", "arbitrary"), vmem_limit_bytes=32 * 1024 * 1024
        ),
        cost_estimate=pl.CostEstimate(
            flops=8 * rows * count * width,
            bytes_accessed=2 * (2 * rows * width + keys_values.size),
            transcendentals=rows * count * width // HEAD_DIM,
        ),
    )(start.reshape(1), queries, keys_values, keys_values)


def line_order(z):
    first = z - 1 + 2 * ((3 - z) // 3)
    third = 3 * (1 - z // 2)
    return (z, first, 6 - z - first - third, third)


def remote(src, dst, send, recv, device):
    return pltpu.make_async_remote_copy(
        src_ref=src, dst_ref=dst, send_sem=send, recv_sem=recv, device_id=device, device_id_type=pl.DeviceIdType.MESH
    )


def greet(z, last, devices, up, down):
    barrier = pltpu.get_barrier_semaphore()

    def hello(device):
        pl.semaphore_signal(barrier, inc=1, device_id=device, device_id_type=pl.DeviceIdType.MESH)

    for device in devices:
        hello(device)

    @pl.when(z < last)
    def _():
        hello(up)

    @pl.when(z > 0)
    def _():
        hello(down)

    inner = jnp.where((z > 0) & (z < last), 1, 0)
    pl.semaphore_wait(barrier, len(devices) + 1 + inner)


def cross_kernel(
    repeat, gain_ref, hidden_ref, wq_ref, wk_ref, wv_ref, wo_ref, out_ref, wo,
    w, hid, normed, acc_ref, kv, m_ref, l_ref, came,
    fill_sem, wo_sem, stage_sem, cross_s, cross_r, swap_s, swap_r, k_s, k_r, kc_s, kc_r,
    wz_s, wz_r, wy_s, wy_r, wc_s, wc_r, w_own_s, w_own_r,
    oz_s, oz_r, oy_s, oy_r, oc_s, oc_r, o_own_s, o_own_r, x_s, x_r,
):
    last = 3
    c = lax.axis_index("stream")
    s = lax.axis_index("seq")
    t = lax.axis_index("tensor")
    z, k = s // 2, s % 2
    depth, q_width = wq_ref.shape
    half = depth // 2
    rows = half // SUBS
    kv_width = wk_ref.shape[1]
    frames = hid.shape[1]
    step = frames // SUBS
    out_depth, block = wo_ref.shape
    out_half = out_depth // 2
    wide = block // SUBS
    heads = kv_width // HEAD_DIM
    scale = LOG2E * HEAD_DIM ** (-0.5)
    at = {"stream": c, "seq": s, "tensor": t}
    up, down = {**at, "seq": s + 2}, {**at, "seq": s - 2}
    beside, mate, across = {**at, "stream": 1 - c}, {**at, "seq": 2 * z + 1 - k}, {**at, "tensor": 1 - t}
    greet(z, last, (beside, mate, across), up, down)
    sends = (z < last, z > 0)

    def each_sub(action):
        @pl.loop(0, SUBS)
        def _(sub):
            action(sub)

    def source(way, hop):
        return z - hop if way == 0 else z + hop

    def arrives(way, hop):
        return z >= hop if way == 0 else z + hop <= last

    def w_part(origin, core, side, sub):
        start = pl.multiple_of(origin * (2 * depth) + core * depth + side * half + sub * rows, rows)
        return w.at[pl.ds(start, rows)]

    def o_part(origin, core, side, sub):
        return wo.at[2 * origin + core, sub, pl.ds(pl.multiple_of(side * out_half, out_half), out_half)]

    def routes(part, z_s, z_r, y_s, y_r, c_s, c_r):
        def along(way, hop, sub):
            view = part(source(way, hop), k, c, sub)
            return remote(view, view, z_s.at[way, hop, sub], z_r.at[way, hop, sub], up if way == 0 else down)

        def sideways(way, hop, sub):
            view = part(source(way, hop), k, c, sub)
            return remote(view, view, y_s.at[way, hop - 1, sub], y_r.at[way, hop - 1, sub], beside)

        def inward(way, kind, hop, sub):
            view = part(source(way, hop), k, c if kind == 0 else 1 - c, sub)
            return remote(view, view, c_s.at[way, kind, hop - 1, sub], c_r.at[way, kind, hop - 1, sub], mate)

        def leave(way):
            @pl.when(sends[way])
            def _():
                each_sub(lambda sub: along(way, 0, sub).start())

        def pass_on(way, hop, sub):
            @pl.when(arrives(way, hop))
            def _():
                along(way, hop - 1, sub).wait_recv()

                @pl.when(sends[way] & (hop < last))
                def _():
                    along(way, hop, sub).start()

                sideways(way, hop, sub).start()
                inward(way, 0, hop, sub).start()

        def take(way, hop, sub):
            @pl.when(arrives(way, hop))
            def _():
                along(way, hop - 1, sub).wait_recv()
                inward(way, 0, hop, sub).start()

        def forward(way, hop, sub):
            @pl.when(arrives(way, hop) & sends[way])
            def _():
                along(way, hop, sub).start()

        def share_out(way, hop, sub):
            @pl.when(arrives(way, hop))
            def _():
                sideways(way, hop, sub).start()

        def pass_in(way, hop, sub):
            @pl.when(arrives(way, hop))
            def _():
                sideways(way, hop, sub).wait_recv()
                inward(way, 1, hop, sub).start()

        def gathered(way, hop):
            @pl.when(arrives(way, hop))
            def _():
                def action(sub):
                    inward(way, 0, hop, sub).wait_recv()
                    inward(way, 1, hop, sub).wait_recv()

                each_sub(action)

        def settle(sub):
            for way in range(2):
                for hop in range(last):
                    @pl.when(sends[way] & arrives(way, hop))
                    def _():
                        along(way, hop, sub).wait_send()
                for hop in range(1, last + 1):
                    @pl.when(arrives(way, hop))
                    def _():
                        sideways(way, hop, sub).wait_send()
                        inward(way, 0, hop, sub).wait_send()
                        inward(way, 1, hop, sub).wait_send()

        return leave, pass_on, pass_in, gathered, settle, inward, (take, forward, share_out)

    w_leave, w_on, w_in, w_gathered, w_settle, *_ = routes(w_part, wz_s, wz_r, wy_s, wy_r, wc_s, wc_r)
    o_leave, o_on, o_in, _, o_settle, o_inward, (o_take, o_forward, o_out) = routes(o_part, oz_s, oz_r, oy_s, oy_r, oc_s, oc_r)

    own = pl.multiple_of(s * depth, depth)
    fills = [
        pltpu.make_async_copy(wq_ref, w.at[pl.ds(own, depth), pl.ds(0, q_width)], fill_sem.at[0]),
        pltpu.make_async_copy(wk_ref, w.at[pl.ds(own, depth), pl.ds(q_width, kv_width)], fill_sem.at[1]),
        pltpu.make_async_copy(wv_ref, w.at[pl.ds(own, depth), pl.ds(q_width + kv_width, kv_width)], fill_sem.at[2]),
    ]
    mine = pltpu.make_async_copy(hidden_ref, hid.at[t], fill_sem.at[3])
    wo_fills = [
        pltpu.make_async_copy(wo_ref.at[:, pl.ds(sub * wide, wide)], wo.at[s, sub], wo_sem.at[sub])
        for sub in range(SUBS)
    ]

    def crossing(piece):
        start = pl.multiple_of(piece * step, step)
        return remote(
            hidden_ref.at[pl.ds(start, step)], hid.at[t, pl.ds(start, step)],
            cross_s.at[piece], cross_r.at[piece], across,
        )

    for copy in fills:
        copy.start()
    mine.start()
    each_sub(lambda piece: crossing(piece).start())
    for copy in fills:
        copy.wait()
    for way in range(2):
        w_leave(way)
    w_block = w.at[pl.ds(own, depth)]
    w_whole = remote(w_block, w_block, w_own_s, w_own_r, mate)
    w_whole.start()
    for copy in wo_fills:
        copy.start()

    tall = 16

    def norm(sub):
        crossing(sub).wait_recv()

        @pl.loop(0, step // tall)
        def _(i):
            at_rows = pl.ds(pl.multiple_of(sub * step + i * tall, tall), tall)
            low = hid[0, at_rows, :].astype(jnp.float32)
            high = hid[1, at_rows, :].astype(jnp.float32)
            total = jnp.sum(low * low, axis=1, keepdims=True) + jnp.sum(high * high, axis=1, keepdims=True)
            inverse_rms = lax.rsqrt(total / (2 * low.shape[1]) + 1e-05)
            part = normed.shape[2]
            for group in range(4):
                x = (low if group < 2 else high)[:, (group % 2) * part:(group % 2 + 1) * part]
                gain = gain_ref[:, group * part:(group + 1) * part]
                normed[group, at_rows, :] = (x * inverse_rms * gain).astype(jnp.bfloat16)

    order = line_order(z)
    tile = 512
    tiles = (q_width + 2 * kv_width) // tile
    q_tiles = q_width // tile
    folds = frames // HEAD_DIM

    def dot(place, index):
        group = order[place]
        columns = pl.ds(pl.multiple_of(index * tile, tile), tile)
        return jnp.dot(
            normed[group],
            w[pl.ds(pl.multiple_of(group * 2 * depth, 2 * depth), 2 * depth), columns],
            preferred_element_type=jnp.float32,
        )

    def held(index):
        return pl.ds(index * folds, folds)

    def project(place, low, high):
        @pl.loop(low, high)
        def _(index):
            value = dot(place, index).reshape(folds, HEAD_DIM, tile)
            if place == 0:
                acc_ref[held(index)] = value
            else:
                acc_ref[held(index)] += value

    def finish(index):
        total = acc_ref[held(index)].reshape(frames, tile) + dot(3, index)
        return total.astype(jnp.bfloat16)

    def first_hop(sub):
        for way in range(2):
            w_on(way, 1, sub)

    def second_hop(sub):
        for way in range(2):
            w_on(way, 2, sub)
            w_in(way, 1, sub)
        norm(sub)

    each_sub(first_hop)
    mine.wait()
    each_sub(second_hop)
    w_whole.wait_recv()
    for way in range(2):
        w_gathered(way, 1)
    for copy in wo_fills:
        copy.wait()
    for sub in range(SUBS):
        for way in range(2):
            w_on(way, 3, sub)
            w_in(way, 2, sub)
        if sub == SUBS - 1:
            for way in range(2):
                o_leave(way)
            o_whole = remote(wo.at[s], wo.at[s], o_own_s, o_own_r, mate)
            o_whole.start()
        low, high = sub * 2 * tiles // SUBS, (sub + 1) * 2 * tiles // SUBS
        for place in range(2):
            begin, end = max(low - place * tiles, 0), min(high - place * tiles, tiles)
            if begin < end:
                project(place, begin, end)
    for way in range(2):
        w_gathered(way, 2)
    project(2, 0, tiles)
    for way in range(2):
        each_sub(lambda sub: w_in(way, 3, sub))
        w_gathered(way, 3)

    for index in range(2 * kv_width // tile):
        piece = finish(q_tiles + index)
        for head in range(heads):
            start = (2 * head + index) * HEAD_DIM
            hid[1, :, start:start + HEAD_DIM] = piece[:, head * HEAD_DIM:(head + 1) * HEAD_DIM]

    def key_rows(hop, head):
        start = pl.multiple_of((2 * (z - hop) + k) * frames, frames)
        return kv.at[head, pl.ds(start, frames)]

    def swap(head):
        start = pl.multiple_of(head * 2 * HEAD_DIM, 2 * HEAD_DIM)
        return remote(
            hid.at[1, pl.ds(0, frames), pl.ds(start, 2 * HEAD_DIM)], key_rows(0, head),
            swap_s.at[head], swap_r.at[head], beside,
        )

    def climb(hop, sub):
        view = key_rows(hop, sub)
        return remote(view, view, k_s.at[hop, sub], k_r.at[hop, sub], up)

    def hand(hop, sub):
        view = key_rows(hop, sub)
        return remote(view, view, kc_s.at[hop, sub], kc_r.at[hop, sub], mate)

    def pass_keys(hop, sub):
        @pl.when(z >= hop)
        def _():
            climb(hop - 1, sub).wait_recv()
            if hop < last:
                @pl.when(z < last)
                def _():
                    climb(hop, sub).start()
            hand(hop, sub).start()

    each_sub(lambda sub: swap(sub).start())

    @pl.loop(0, q_tiles)
    def _(index):
        hid[0, :, pl.ds(pl.multiple_of(index * tile, tile), tile)] = finish(index)

    def attend_to(head, start, count, masked):
        at_keys = pl.ds(pl.multiple_of(start, count), count)
        keys_here = kv[head, at_keys, 0:HEAD_DIM]
        values_here = kv[head, at_keys, HEAD_DIM:2 * HEAD_DIM]
        if masked:
            allowed = lax.broadcasted_iota(jnp.int32, (count, frames), 0) <= lax.broadcasted_iota(
                jnp.int32, (count, frames), 1
            )

        def scored(r):
            q = hid[0, :, pl.ds(pl.multiple_of((head * repeat + r) * HEAD_DIM, HEAD_DIM), HEAD_DIM)]
            return lax.dot_general(
                keys_here, q, (((1,), (1,)), ((), ())), preferred_element_type=jnp.float32
            )

        following = scored(0)
        for r in range(repeat):
            index = head * repeat + r
            scores = following
            if r + 1 < repeat:
                following = scored(r + 1)
            if masked:
                scores = jnp.where(allowed, scores, -1e30)
            top = jnp.max(scores, axis=0, keepdims=True) * scale
            before = m_ref[index]
            fresh = jnp.maximum(before, top)
            m_ref[index] = fresh
            alpha = jnp.exp2(before - fresh)
            p = jnp.exp2(scores * scale - fresh)
            l_ref[index] = alpha * l_ref[index] + jnp.sum(p, axis=0, keepdims=True)
            acc_ref[index] = alpha * acc_ref[index] + lax.dot_general(
                values_here, p.astype(jnp.bfloat16), (((0,), (0,)), ((), ())), preferred_element_type=jnp.float32
            )

    def attend_own(head):
        hand(0, head).wait_recv()
        attend_to(head, s * frames, frames, True)

        @pl.when(k == 1)
        def _():
            attend_to(head, (s - 1) * frames, frames, False)

    def attend_hop(hop, head):
        @pl.when(z >= hop)
        def _():
            hand(hop, head).wait_recv()
            attend_to(head, (z - hop) * 2 * frames, 2 * frames, False)

    m_ref[...] = jnp.full_like(m_ref, -1e30)
    l_ref[...] = jnp.zeros_like(l_ref)
    acc_ref[...] = jnp.zeros_like(acc_ref)

    def first(sub):
        swap(sub).wait_recv()

        @pl.when(z < last)
        def _():
            climb(0, sub).start()

        hand(0, sub).start()
        o_take(1, 1, sub)
        o_forward(1, 1, sub)

        @pl.when(sub > 0)
        def _():
            attend_own(sub - 1)

    each_sub(first)

    def catch_up(hop, sub):
        @pl.when(sub > 0)
        def _():
            attend_hop(hop, sub - 1)

        @pl.when(sub == 0)
        def _():
            if hop == 1:
                attend_own(heads - 1)
            else:
                attend_hop(hop - 1, heads - 1)

    def phase_1(sub):
        pass_keys(1, sub)
        o_take(1, 2, sub)
        o_forward(1, 2, sub)
        o_take(0, 1, sub)
        o_out(1, 1, sub)
        o_out(0, 1, sub)
        catch_up(1, sub)

    def phase_2(sub):
        pass_keys(2, sub)
        o_take(1, 3, sub)
        o_out(1, 2, sub)
        catch_up(2, sub)

    def phase_3(sub):
        o_forward(0, 1, sub)
        pass_keys(3, sub)
        o_out(1, 3, sub)
        o_in(1, 1, sub)
        o_in(0, 1, sub)
        catch_up(3, sub)

    each_sub(phase_1)
    each_sub(phase_2)
    each_sub(phase_3)
    attend_hop(3, heads - 1)
    each_sub(lambda sub: o_in(1, 2, sub))
    each_sub(lambda sub: o_in(1, 3, sub))

    def climbed(number):
        return number // SUBS + 1, number % SUBS

    w_whole.wait_send()
    each_sub(w_settle)
    attended = w.at[pl.ds(0, frames), pl.ds(0, q_width)]

    def slot_in(place, slot):
        return w.at[pl.ds(place * frames, frames), pl.ds(pl.multiple_of(slot * 2 * wide, 2 * wide), 2 * wide)]

    def kept(slot):
        return slot_in(1, slot)

    def leaving(slot):
        return slot_in(2, slot)

    def carry(slot):
        return remote(leaving(slot), came.at[slot], x_s.at[slot], x_r.at[slot], across)

    @pl.loop(0, heads)
    def _(head):
        for r in range(repeat):
            index = head * repeat + r
            out = (acc_ref[index] / l_ref[index]).T.astype(jnp.bfloat16)
            attended[:, pl.ds(pl.multiple_of(index * HEAD_DIM, HEAD_DIM), HEAD_DIM)] = out

    def which(task):
        place, sub = task // SUBS, task % SUBS
        return place, sub, place <= last - z

    def ready(task):
        place, sub, above = which(task)

        @pl.when(above & (place > 0))
        def _():
            for kind in range(2):
                o_inward(1, kind, place, sub).wait_recv()

        @pl.when(place > last - z)
        def _():
            for kind in range(2):
                o_inward(0, kind, place - (last - z), sub).wait_recv()

    def load(task, buffer, core):
        place, sub, above = which(task)
        group = jnp.where(above, z + place, last - place)
        return pltpu.make_async_copy(
            wo.at[2 * group + core, sub],
            w.at[pl.ds(4 * frames, out_depth), pl.ds((2 * buffer + core) * wide, wide)],
            stage_sem.at[buffer, core],
        )

    def shares(task, buffer):
        place, sub, above = which(task)
        group = jnp.where(above, z + place, last - place)
        for core in range(2):
            load(task, buffer, core).wait()
        weights = w[4 * frames:4 * frames + out_depth, 2 * buffer * wide:2 * (buffer + 1) * wide]
        share = jnp.dot(attended[...], weights, preferred_element_type=jnp.float32).astype(jnp.bfloat16)
        slot = (group % 2) * SUBS + sub

        @pl.when(group // 2 == t)
        def _():
            kept(slot)[...] = share

        @pl.when(group // 2 != t)
        def _():
            leaving(slot)[...] = share
            carry(slot).start()

    def work(*tasks):
        for buffer, task in enumerate(tasks):
            ready(task)
            for core in range(2):
                load(task, buffer, core).start()
        for buffer, task in enumerate(tasks):
            shares(task, buffer)

    o_whole.wait_recv()

    @pl.loop(0, 2 * SUBS - 1)
    def _(pair):
        number = pair + SUBS
        o_on(0, *climbed(number))

        @pl.when(pair > 0)
        def _():
            o_in(0, *climbed(number - 1))

        work(2 * pair, 2 * pair + 1)

    o_on(0, last, SUBS - 1)
    o_in(0, last, SUBS - 2)
    work(4 * SUBS - 2)
    o_in(0, last, SUBS - 1)
    work(4 * SUBS - 1)

    high_first = z // 2

    @pl.loop(0, 2 * SUBS)
    def _(number):
        side, sub = number // SUBS, number % SUBS
        side = side + high_first * (1 - 2 * side)
        slot = side * SUBS + sub
        carry(slot).wait_recv()
        total = (kept(slot)[...].astype(jnp.float32) + came[slot].astype(jnp.float32)).astype(jnp.bfloat16)
        for core in range(2):
            start = pl.multiple_of((side * 2 + core) * block + sub * wide, wide)
            out_ref[:, pl.ds(start, wide)] = total[:, core * wide:(core + 1) * wide]

    o_whole.wait_send()

    @pl.loop(0, 2 * SUBS)
    def _(slot):
        carry(slot).wait_send()

    def settle(sub):
        crossing(sub).wait_send()
        swap(sub).wait_send()
        for hop in range(last + 1):
            @pl.when(z >= hop)
            def _():
                hand(hop, sub).wait_send()
                if hop < last:
                    @pl.when(z < last)
                    def _():
                        climb(hop, sub).wait_send()
        o_settle(sub)

    each_sub(settle)


def crossed(hidden, norm_gain, query_weight, key_weight, value_weight, out_weight):
    frames, features = hidden.shape
    depth, q_width = query_weight.shape
    kv_width = key_weight.shape[1]
    repeat = q_width // kv_width
    total = q_width + 2 * kv_width
    out_depth, block = out_weight.shape
    wide = block // SUBS
    count = q_width // HEAD_DIM
    dma = pltpu.SemaphoreType.DMA
    anywhere = pl.BlockSpec(memory_space=pl.ANY)
    vmem = pl.BlockSpec(memory_space=pltpu.VMEM)
    bf16, f32 = jnp.bfloat16, jnp.float32
    line = [dma((2, 3, SUBS))] * 4 + [dma((2, 2, 3, SUBS))] * 2 + [dma] * 2
    out, _ = pl.pallas_call(
        functools.partial(cross_kernel, repeat),
        out_shape=(
            jax.ShapeDtypeStruct((frames, 4 * block), bf16),
            jax.ShapeDtypeStruct((8, SUBS, out_depth, wide), bf16),
        ),
        in_specs=[vmem] + [anywhere] * 5,
        out_specs=(vmem, anywhere),
        scratch_shapes=[
            pltpu.VMEM((8 * depth, total), bf16),
            pltpu.VMEM((2, frames, features), bf16),
            pltpu.VMEM((4, frames, features // 2), bf16),
            pltpu.VMEM((total // HEAD_DIM, HEAD_DIM, frames), f32),
            pltpu.VMEM((kv_width // HEAD_DIM, 8 * frames, 2 * HEAD_DIM), bf16),
            pltpu.VMEM((count, 1, frames), f32),
            pltpu.VMEM((count, 1, frames), f32),
            pltpu.VMEM((2 * SUBS, frames, 2 * wide), bf16),
            dma((4,)), dma((SUBS,)), dma((2, 2)),
            dma((SUBS,)), dma((SUBS,)), dma((SUBS,)), dma((SUBS,)),
            dma((3, SUBS)), dma((3, SUBS)), dma((4, SUBS)), dma((4, SUBS)),
            *line, *line,
            dma((2 * SUBS,)), dma((2 * SUBS,)),
        ],
        compiler_params=pltpu.CompilerParams(
            collective_id=0, has_side_effects=True, vmem_limit_bytes=60 * 1024 * 1024
        ),
        cost_estimate=pl.CostEstimate(
            flops=16 * frames * depth * total + 16 * frames * out_depth * block,
            bytes_accessed=4 * hidden.size,
            transcendentals=4 * frames * frames * count,
        ),
    )(norm_gain.reshape(1, -1), hidden, query_weight, key_weight, value_weight, out_weight)
    return out


def y_share(mine, core, after=None):
    depth = mine.shape[0] // 2
    part = lax.dynamic_slice_in_dim(mine, core * depth, depth, 0)
    near = lax.ppermute(part, "stream", [(0, 1), (1, 0)])
    if after is None:
        return near, swap_pairs(near, "seq")
    near, after = lax.optimization_barrier((near, after))
    return near, swap_pairs(near, "seq"), after


def fits(hidden, query_weight, key_weight):
    meshes = (lax.axis_size("stream"), lax.axis_size("seq"), lax.axis_size("tensor"))
    return (
        meshes == (2, 8, 2)
        and hidden.shape[1:] == (1, 512, 2048)
        and query_weight.shape == (512, 2048)
        and key_weight.shape == (512, 512)
    )


def body(hidden, norm_gain, query_weight, key_weight, value_projection_weight, out_weight):
    if not fits(hidden, query_weight, key_weight):
        return general_body(hidden, norm_gain, query_weight, key_weight, value_projection_weight, out_weight)
    out = crossed(
        hidden.reshape(hidden.shape[2:]), norm_gain, query_weight, key_weight, value_projection_weight, out_weight
    )
    return out.reshape(hidden.shape)


def general_body(hidden, norm_gain, query_weight, key_weight, value_projection_weight, out_weight):
    windows, frame_count = hidden.shape[1], hidden.shape[2]
    n_tensor = lax.axis_size("tensor")
    n_seq = lax.axis_size("seq")
    stream = lax.axis_index("stream")
    tensor = lax.axis_index("tensor")
    seq = lax.axis_index("seq")
    core = seq % 2
    rows = windows * frame_count
    depth = query_weight.shape[0] // 2
    out_half = out_weight.shape[1] // 2

    kv_weight = jnp.concatenate([key_weight, value_projection_weight], axis=1)
    kv_mine = lax.all_gather(
        lax.dynamic_slice_in_dim(kv_weight, stream * depth, depth, 0), "seq", axis=0, tiled=True
    )
    query_mine = lax.all_gather(
        lax.dynamic_slice_in_dim(query_weight, stream * depth, depth, 0), "seq", axis=0, tiled=True
    )
    out_mine = lax.all_gather(
        lax.dynamic_slice_in_dim(out_weight, stream * out_half, out_half, 1), "seq", axis=1, tiled=True
    )

    local = hidden.reshape(rows, hidden.shape[3])
    if n_tensor == 2:
        other = lax.ppermute(local, "tensor", [(0, 1), (1, 0)])
        gathered = jnp.where(
            tensor == 0,
            jnp.concatenate([local, other], axis=1),
            jnp.concatenate([other, local], axis=1),
        )
    else:
        gathered = lax.all_gather(local, "tensor", axis=1, tiled=True)
    flat = gathered.astype(jnp.float32)
    inverse_rms = lax.rsqrt(jnp.mean(flat * flat, axis=1, keepdims=True) + 1e-05)
    normed = (flat * inverse_rms * norm_gain).astype(jnp.bfloat16)
    split = normed.reshape(rows, n_seq, 2, depth)

    def features(half):
        return lax.dynamic_index_in_dim(split, half, 2, keepdims=False).reshape(rows, n_seq * depth)

    normed_mine = features(stream)
    normed_other = features(1 - stream)
    span = n_seq * depth // 2
    normed_near = lax.dynamic_slice_in_dim(normed_other, core * span, span, 1)
    normed_far = lax.dynamic_slice_in_dim(normed_other, (1 - core) * span, span, 1)

    def project(mine, near, far):
        total = jnp.dot(normed_mine, mine, preferred_element_type=jnp.float32)
        total += jnp.dot(normed_near, near, preferred_element_type=jnp.float32)
        total += jnp.dot(normed_far, far, preferred_element_type=jnp.float32)
        return total.astype(jnp.bfloat16)

    keys_values = project(kv_mine, *y_share(kv_mine, core))
    partner = lax.ppermute(keys_values, "stream", [(0, 1), (1, 0)])
    kv_width = key_weight.shape[1]
    parts = 2 if kv_width % (2 * HEAD_DIM) == 0 else 1
    step = kv_width // parts
    pieces = []
    for part in range(parts):
        columns = jnp.concatenate(
            [partner[:, part * step:(part + 1) * step],
             partner[:, kv_width + part * step:kv_width + (part + 1) * step]],
            axis=1,
        )
        pieces.append(
            lax.all_gather(columns.reshape(windows, frame_count, 2 * step), "seq", axis=1, tiled=True)
        )
    queries = project(query_mine, *y_share(query_mine, core)).reshape(windows, frame_count, -1)
    out_near = out_far = None
    width = out_weight.shape[0] // 2

    repeat = query_weight.shape[1] // key_weight.shape[1]
    chunk = frame_count // ROW_CHUNKS

    def scattered(share):
        if n_tensor == 2:
            wide = share.shape[1] // 2
            away = lax.dynamic_slice_in_dim(share, (1 - tensor) * wide, wide, 1)
            kept = lax.dynamic_slice_in_dim(share, tensor * wide, wide, 1)
            came = lax.ppermute(away, "tensor", [(0, 1), (1, 0)])
            return (kept.astype(jnp.float32) + came.astype(jnp.float32)).astype(jnp.bfloat16)
        return lax.psum_scatter(share, "tensor", scatter_dimension=1, tiled=True)

    outs = []
    q_step = step * repeat
    for window in range(windows):
        early = [
            attend(
                seq * frame_count,
                queries[window][:, part * q_step:(part + 1) * q_step],
                pieces[part][window],
                repeat,
            )
            for part in range(parts - 1)
        ]
        for index in range(ROW_CHUNKS):
            low, high = index * chunk, (index + 1) * chunk
            final = attend(
                seq * frame_count + low,
                queries[window][low:high, (parts - 1) * q_step:],
                pieces[-1][window],
                repeat,
            )
            attended = jnp.concatenate([done[low:high] for done in early] + [final], axis=1)
            share_mine = jnp.dot(attended, out_mine, preferred_element_type=jnp.float32)
            if out_near is None:
                out_near, out_far, attended = y_share(out_mine, core, attended)
            attended_near = lax.dynamic_slice_in_dim(attended, core * width, width, 1)
            attended_far = lax.dynamic_slice_in_dim(attended, (1 - core) * width, width, 1)
            share_other = jnp.dot(attended_near, out_near, preferred_element_type=jnp.float32)
            share_other += jnp.dot(attended_far, out_far, preferred_element_type=jnp.float32)
            mine = scattered(share_mine.astype(jnp.bfloat16)).reshape(chunk, -1, out_half)
            other = scattered(share_other.astype(jnp.bfloat16)).reshape(chunk, -1, out_half)
            outs.append(
                jnp.where(
                    stream == 0, jnp.stack([mine, other], axis=2), jnp.stack([other, mine], axis=2)
                ).reshape(chunk, -1)
            )
    return jnp.concatenate(outs, axis=0).reshape(1, windows, frame_count, -1)


def solution(mesh):
    in_specs = (
        P("stream", None, "seq", "tensor"),
        P(),
        P("seq", "tensor"),
        P("seq", "tensor"),
        P("seq", "tensor"),
        P("tensor", "seq"),
    )
    out_specs = P("stream", None, "seq", "tensor")
    return jax.shard_map(body, mesh=mesh, in_specs=in_specs, out_specs=out_specs, check_vma=False)
```

```python
import functools

import jax
import jax.numpy as jnp
from jax import lax
from jax.experimental import pallas as pl
from jax.experimental.pallas import tpu as pltpu
from jax.sharding import PartitionSpec as P

HEAD_DIM = 128
ROW_CHUNKS = 2
KEY_BLOCK = 1024
SUBS = 4
LOG2E = 1.4426950408889634


def swap_pairs(block, axis):
    count = lax.axis_size(axis)
    return lax.ppermute(block, axis, [(i, i ^ 1) for i in range(count)])


def attend_kernel(repeat, start_ref, q_ref, k_ref, v_ref, o_ref, m_ref, l_ref, acc_ref):
    step = pl.program_id(1)
    rows = q_ref.shape[0]
    keys = k_ref.shape[0]
    start = start_ref[0]
    last = (start + rows - 1) // keys
    scale = LOG2E * HEAD_DIM ** (-0.5)

    @pl.when(step == 0)
    def _():
        m_ref[...] = jnp.full_like(m_ref, -1e30)
        l_ref[...] = jnp.zeros_like(l_ref)
        acc_ref[...] = jnp.zeros_like(acc_ref)

    def update(masked):
        k = k_ref[...]
        v = v_ref[...]
        if masked:
            frame = start + lax.broadcasted_iota(jnp.int32, (keys, rows), 1)
            key = step * keys + lax.broadcasted_iota(jnp.int32, (keys, rows), 0)
            allowed = key <= frame

        def scored(r):
            q = q_ref[:, r * HEAD_DIM:(r + 1) * HEAD_DIM]
            return lax.dot_general(k, q, (((1,), (1,)), ((), ())), preferred_element_type=jnp.float32)

        following = scored(0)
        for r in range(repeat):
            s = following
            if r + 1 < repeat:
                following = scored(r + 1)
            if masked:
                s = jnp.where(allowed, s, -1e30)
            top = jnp.max(s, axis=0, keepdims=True) * scale
            before = m_ref[r]
            fresh = jnp.maximum(before, top)
            m_ref[r] = fresh
            alpha = jnp.exp2(before - fresh)
            p = jnp.exp2(s * scale - fresh)
            l_ref[r] = alpha * l_ref[r] + jnp.sum(p, axis=0, keepdims=True)
            acc_ref[r] = alpha * acc_ref[r] + lax.dot_general(
                v, p.astype(jnp.bfloat16), (((0,), (0,)), ((), ())), preferred_element_type=jnp.float32
            )

    @pl.when(step < last)
    def _():
        update(False)

    @pl.when(step == last)
    def _():
        update(True)
        for r in range(repeat):
            attended = (acc_ref[r] / l_ref[r]).T
            o_ref[:, r * HEAD_DIM:(r + 1) * HEAD_DIM] = attended.astype(o_ref.dtype)


def attend(start, queries, keys_values, repeat):
    rows, width = queries.shape
    count = keys_values.shape[0]
    groups = width // (repeat * HEAD_DIM)
    block = min(KEY_BLOCK, count)

    def at(step, start_ref):
        return jnp.minimum(step, (start_ref[0] + rows - 1) // block)

    return pl.pallas_call(
        functools.partial(attend_kernel, repeat),
        out_shape=jax.ShapeDtypeStruct((rows, width), jnp.bfloat16),
        grid_spec=pltpu.PrefetchScalarGridSpec(
            num_scalar_prefetch=1,
            grid=(groups, count // block),
            in_specs=[
                pl.BlockSpec((rows, repeat * HEAD_DIM), lambda g, i, s: (0, g)),
                pl.BlockSpec((block, HEAD_DIM), lambda g, i, s: (at(i, s), g)),
                pl.BlockSpec((block, HEAD_DIM), lambda g, i, s: (at(i, s), groups + g)),
            ],
            out_specs=pl.BlockSpec((rows, repeat * HEAD_DIM), lambda g, i, s: (0, g)),
            scratch_shapes=[
                pltpu.VMEM((repeat, 1, rows), jnp.float32),
                pltpu.VMEM((repeat, 1, rows), jnp.float32),
                pltpu.VMEM((repeat, HEAD_DIM, rows), jnp.float32),
            ],
        ),
        compiler_params=pltpu.CompilerParams(
            dimension_semantics=("arbitrary", "arbitrary"), vmem_limit_bytes=32 * 1024 * 1024
        ),
        cost_estimate=pl.CostEstimate(
            flops=8 * rows * count * width,
            bytes_accessed=2 * (2 * rows * width + keys_values.size),
            transcendentals=rows * count * width // HEAD_DIM,
        ),
    )(start.reshape(1), queries, keys_values, keys_values)


def line_order(z):
    first = z - 1 + 2 * ((3 - z) // 3)
    third = 3 * (1 - z // 2)
    return (z, first, 6 - z - first - third, third)


def remote(src, dst, send, recv, device):
    return pltpu.make_async_remote_copy(
        src_ref=src, dst_ref=dst, send_sem=send, recv_sem=recv, device_id=device, device_id_type=pl.DeviceIdType.MESH
    )


def greet(z, last, devices, up, down):
    barrier = pltpu.get_barrier_semaphore()

    def hello(device):
        pl.semaphore_signal(barrier, inc=1, device_id=device, device_id_type=pl.DeviceIdType.MESH)

    for device in devices:
        hello(device)

    @pl.when(z < last)
    def _():
        hello(up)

    @pl.when(z > 0)
    def _():
        hello(down)

    inner = jnp.where((z > 0) & (z < last), 1, 0)
    pl.semaphore_wait(barrier, len(devices) + 1 + inner)


def cross_kernel(
    repeat, gain_ref, hidden_ref, wq_ref, wk_ref, wv_ref, wo_ref, out_ref, wo,
    w, hid, normed, acc_ref, kv, m_ref, l_ref, came,
    fill_sem, wo_sem, stage_sem, cross_s, cross_r, swap_s, swap_r, k_s, k_r, kc_s, kc_r,
    wz_s, wz_r, wy_s, wy_r, wc_s, wc_r, w_own_s, w_own_r,
    oz_s, oz_r, oy_s, oy_r, oc_s, oc_r, o_own_s, o_own_r, x_s, x_r,
):
    last = 3
    c = lax.axis_index("stream")
    s = lax.axis_index("seq")
    t = lax.axis_index("tensor")
    z, k = s // 2, s % 2
    depth, q_width = wq_ref.shape
    half = depth // 2
    rows = half // SUBS
    kv_width = wk_ref.shape[1]
    frames = hid.shape[1]
    step = frames // SUBS
    out_depth, block = wo_ref.shape
    out_half = out_depth // 2
    wide = block // SUBS
    heads = kv_width // HEAD_DIM
    scale = LOG2E * HEAD_DIM ** (-0.5)
    at = {"stream": c, "seq": s, "tensor": t}
    up, down = {**at, "seq": s + 2}, {**at, "seq": s - 2}
    beside, mate, across = {**at, "stream": 1 - c}, {**at, "seq": 2 * z + 1 - k}, {**at, "tensor": 1 - t}
    greet(z, last, (beside, mate, across), up, down)
    sends = (z < last, z > 0)

    def each_sub(action):
        @pl.loop(0, SUBS)
        def _(sub):
            action(sub)

    def source(way, hop):
        return z - hop if way == 0 else z + hop

    def arrives(way, hop):
        return z >= hop if way == 0 else z + hop <= last

    def w_part(origin, core, side, sub):
        start = pl.multiple_of(origin * (2 * depth) + core * depth + side * half + sub * rows, rows)
        return w.at[pl.ds(start, rows)]

    def o_part(origin, core, side, sub):
        return wo.at[2 * origin + core, sub, pl.ds(pl.multiple_of(side * out_half, out_half), out_half)]

    def routes(part, z_s, z_r, y_s, y_r, c_s, c_r):
        def along(way, hop, sub):
            view = part(source(way, hop), k, c, sub)
            return remote(view, view, z_s.at[way, hop, sub], z_r.at[way, hop, sub], up if way == 0 else down)

        def sideways(way, hop, sub):
            view = part(source(way, hop), k, c, sub)
            return remote(view, view, y_s.at[way, hop - 1, sub], y_r.at[way, hop - 1, sub], beside)

        def inward(way, kind, hop, sub):
            view = part(source(way, hop), k, c if kind == 0 else 1 - c, sub)
            return remote(view, view, c_s.at[way, kind, hop - 1, sub], c_r.at[way, kind, hop - 1, sub], mate)

        def leave(way):
            @pl.when(sends[way])
            def _():
                each_sub(lambda sub: along(way, 0, sub).start())

        def pass_on(way, hop, sub):
            @pl.when(arrives(way, hop))
            def _():
                along(way, hop - 1, sub).wait_recv()

                @pl.when(sends[way] & (hop < last))
                def _():
                    along(way, hop, sub).start()

                sideways(way, hop, sub).start()
                inward(way, 0, hop, sub).start()

        def take(way, hop, sub):
            @pl.when(arrives(way, hop))
            def _():
                along(way, hop - 1, sub).wait_recv()
                inward(way, 0, hop, sub).start()

        def forward(way, hop, sub):
            @pl.when(arrives(way, hop) & sends[way])
            def _():
                along(way, hop, sub).start()

        def share_out(way, hop, sub):
            @pl.when(arrives(way, hop))
            def _():
                sideways(way, hop, sub).start()

        def pass_in(way, hop, sub):
            @pl.when(arrives(way, hop))
            def _():
                sideways(way, hop, sub).wait_recv()
                inward(way, 1, hop, sub).start()

        def gathered(way, hop):
            @pl.when(arrives(way, hop))
            def _():
                def action(sub):
                    inward(way, 0, hop, sub).wait_recv()
                    inward(way, 1, hop, sub).wait_recv()

                each_sub(action)

        def final_hop(way):
            return z if way == 0 else last - z

        def drained(way):
            @pl.when(sends[way])
            def _():
                along(way, final_hop(way), SUBS - 1).wait_send()

        def settle(sub, seen=False):
            for way in range(2):
                for hop in range(last):
                    unseen = jnp.logical_not((final_hop(way) == hop) & (sub == SUBS - 1)) if seen else True

                    @pl.when(sends[way] & arrives(way, hop) & unseen)
                    def _():
                        along(way, hop, sub).wait_send()
                for hop in range(1, last + 1):
                    @pl.when(arrives(way, hop))
                    def _():
                        sideways(way, hop, sub).wait_send()
                        inward(way, 0, hop, sub).wait_send()
                        inward(way, 1, hop, sub).wait_send()

        return leave, pass_on, pass_in, gathered, settle, inward, (take, forward, share_out), drained

    w_leave, w_on, w_in, w_gathered, w_settle, _, _, w_drained = routes(w_part, wz_s, wz_r, wy_s, wy_r, wc_s, wc_r)
    o_leave, o_on, o_in, _, o_settle, o_inward, (o_take, o_forward, o_out), _ = routes(o_part, oz_s, oz_r, oy_s, oy_r, oc_s, oc_r)

    own = pl.multiple_of(s * depth, depth)
    fills = [
        pltpu.make_async_copy(wq_ref, w.at[pl.ds(own, depth), pl.ds(0, q_width)], fill_sem.at[0]),
        pltpu.make_async_copy(wk_ref, w.at[pl.ds(own, depth), pl.ds(q_width, kv_width)], fill_sem.at[1]),
        pltpu.make_async_copy(wv_ref, w.at[pl.ds(own, depth), pl.ds(q_width + kv_width, kv_width)], fill_sem.at[2]),
    ]
    mine = pltpu.make_async_copy(hidden_ref, hid.at[t], fill_sem.at[3])
    wo_fills = [
        pltpu.make_async_copy(wo_ref.at[:, pl.ds(sub * wide, wide)], wo.at[s, sub], wo_sem.at[sub])
        for sub in range(SUBS)
    ]

    def crossing(piece):
        start = pl.multiple_of(piece * step, step)
        return remote(
            hidden_ref.at[pl.ds(start, step)], hid.at[t, pl.ds(start, step)],
            cross_s.at[piece], cross_r.at[piece], across,
        )

    for copy in fills:
        copy.start()
    mine.start()
    each_sub(lambda piece: crossing(piece).start())
    for copy in fills:
        copy.wait()
    for way in range(2):
        w_leave(way)
    w_block = w.at[pl.ds(own, depth)]
    w_whole = remote(w_block, w_block, w_own_s, w_own_r, mate)
    w_whole.start()
    for copy in wo_fills:
        copy.start()

    tall = 16

    def norm(sub):
        crossing(sub).wait_recv()

        @pl.loop(0, step // tall)
        def _(i):
            at_rows = pl.ds(pl.multiple_of(sub * step + i * tall, tall), tall)
            low = hid[0, at_rows, :].astype(jnp.float32)
            high = hid[1, at_rows, :].astype(jnp.float32)
            total = jnp.sum(low * low, axis=1, keepdims=True) + jnp.sum(high * high, axis=1, keepdims=True)
            inverse_rms = lax.rsqrt(total / (2 * low.shape[1]) + 1e-05)
            part = normed.shape[2]
            for group in range(4):
                x = (low if group < 2 else high)[:, (group % 2) * part:(group % 2 + 1) * part]
                gain = gain_ref[:, group * part:(group + 1) * part]
                normed[group, at_rows, :] = (x * inverse_rms * gain).astype(jnp.bfloat16)

    order = line_order(z)
    tile = 512
    tiles = (q_width + 2 * kv_width) // tile
    q_tiles = q_width // tile
    folds = frames // HEAD_DIM

    def dot(place, index):
        group = order[place]
        columns = pl.ds(pl.multiple_of(index * tile, tile), tile)
        return jnp.dot(
            normed[group],
            w[pl.ds(pl.multiple_of(group * 2 * depth, 2 * depth), 2 * depth), columns],
            preferred_element_type=jnp.float32,
        )

    def held(index):
        return pl.ds(index * folds, folds)

    def project(place, low, high):
        @pl.loop(low, high)
        def _(index):
            value = dot(place, index).reshape(folds, HEAD_DIM, tile)
            if place == 0:
                acc_ref[held(index)] = value
            else:
                acc_ref[held(index)] += value

    def finish(index):
        total = acc_ref[held(index)].reshape(frames, tile) + dot(3, index)
        return total.astype(jnp.bfloat16)

    def first_hop(sub):
        for way in range(2):
            w_on(way, 1, sub)

    def second_hop(sub):
        for way in range(2):
            w_on(way, 2, sub)
            w_in(way, 1, sub)
        norm(sub)

    each_sub(first_hop)
    mine.wait()
    each_sub(second_hop)
    w_whole.wait_recv()
    for way in range(2):
        w_gathered(way, 1)
    for copy in wo_fills:
        copy.wait()
    for sub in range(SUBS):
        for way in range(2):
            w_on(way, 3, sub)
            if sub == SUBS - 1:
                w_drained(way)
                o_leave(way)
            w_in(way, 2, sub)
        low, high = sub * 2 * tiles // SUBS, (sub + 1) * 2 * tiles // SUBS
        for place in range(2):
            begin, end = max(low - place * tiles, 0), min(high - place * tiles, tiles)
            if begin < end:
                project(place, begin, end)
    for way in range(2):
        w_gathered(way, 2)
    o_whole = remote(wo.at[s], wo.at[s], o_own_s, o_own_r, mate)
    o_whole.start()
    project(2, 0, tiles)
    for way in range(2):
        each_sub(lambda sub: w_in(way, 3, sub))
        w_gathered(way, 3)

    for index in range(2 * kv_width // tile):
        piece = finish(q_tiles + index)
        for head in range(heads):
            start = (2 * head + index) * HEAD_DIM
            hid[1, :, start:start + HEAD_DIM] = piece[:, head * HEAD_DIM:(head + 1) * HEAD_DIM]

    def key_rows(hop, head):
        start = pl.multiple_of((2 * (z - hop) + k) * frames, frames)
        return kv.at[head, pl.ds(start, frames)]

    def swap(head):
        start = pl.multiple_of(head * 2 * HEAD_DIM, 2 * HEAD_DIM)
        return remote(
            hid.at[1, pl.ds(0, frames), pl.ds(start, 2 * HEAD_DIM)], key_rows(0, head),
            swap_s.at[head], swap_r.at[head], beside,
        )

    def climb(hop, sub):
        view = key_rows(hop, sub)
        return remote(view, view, k_s.at[hop, sub], k_r.at[hop, sub], up)

    def hand(hop, sub):
        view = key_rows(hop, sub)
        return remote(view, view, kc_s.at[hop, sub], kc_r.at[hop, sub], mate)

    def pass_keys(hop, sub):
        @pl.when(z >= hop)
        def _():
            climb(hop - 1, sub).wait_recv()
            if hop < last:
                @pl.when(z < last)
                def _():
                    climb(hop, sub).start()
            hand(hop, sub).start()

    each_sub(lambda sub: swap(sub).start())

    @pl.loop(0, q_tiles)
    def _(index):
        hid[0, :, pl.ds(pl.multiple_of(index * tile, tile), tile)] = finish(index)

    def attend_to(head, start, count, masked):
        at_keys = pl.ds(pl.multiple_of(start, count), count)
        keys_here = kv[head, at_keys, 0:HEAD_DIM]
        values_here = kv[head, at_keys, HEAD_DIM:2 * HEAD_DIM]
        if masked:
            allowed = lax.broadcasted_iota(jnp.int32, (count, frames), 0) <= lax.broadcasted_iota(
                jnp.int32, (count, frames), 1
            )

        def scored(r):
            q = hid[0, :, pl.ds(pl.multiple_of((head * repeat + r) * HEAD_DIM, HEAD_DIM), HEAD_DIM)]
            return lax.dot_general(
                keys_here, q, (((1,), (1,)), ((), ())), preferred_element_type=jnp.float32
            )

        following = scored(0)
        for r in range(repeat):
            index = head * repeat + r
            scores = following
            if r + 1 < repeat:
                following = scored(r + 1)
            if masked:
                scores = jnp.where(allowed, scores, -1e30)
            top = jnp.max(scores, axis=0, keepdims=True) * scale
            before = m_ref[index]
            fresh = jnp.maximum(before, top)
            m_ref[index] = fresh
            alpha = jnp.exp2(before - fresh)
            p = jnp.exp2(scores * scale - fresh)
            l_ref[index] = alpha * l_ref[index] + jnp.sum(p, axis=0, keepdims=True)
            acc_ref[index] = alpha * acc_ref[index] + lax.dot_general(
                values_here, p.astype(jnp.bfloat16), (((0,), (0,)), ((), ())), preferred_element_type=jnp.float32
            )

    def attend_own(head):
        hand(0, head).wait_recv()
        attend_to(head, s * frames, frames, True)

        @pl.when(k == 1)
        def _():
            attend_to(head, (s - 1) * frames, frames, False)

    def attend_hop(hop, head):
        @pl.when(z >= hop)
        def _():
            hand(hop, head).wait_recv()
            attend_to(head, (z - hop) * 2 * frames, 2 * frames, False)

    m_ref[...] = jnp.full_like(m_ref, -1e30)
    l_ref[...] = jnp.zeros_like(l_ref)
    acc_ref[...] = jnp.zeros_like(acc_ref)

    def first(sub):
        swap(sub).wait_recv()

        @pl.when(z < last)
        def _():
            climb(0, sub).start()

        hand(0, sub).start()
        o_take(1, 1, sub)
        o_forward(1, 1, sub)

        @pl.when(sub > 0)
        def _():
            attend_own(sub - 1)

    each_sub(first)

    def catch_up(hop, sub):
        @pl.when(sub > 0)
        def _():
            attend_hop(hop, sub - 1)

        @pl.when(sub == 0)
        def _():
            if hop == 1:
                attend_own(heads - 1)
            else:
                attend_hop(hop - 1, heads - 1)

    def phase_1(sub):
        pass_keys(1, sub)
        o_take(1, 2, sub)
        o_forward(1, 2, sub)
        o_take(0, 1, sub)
        o_out(1, 1, sub)
        o_out(0, 1, sub)
        catch_up(1, sub)

    def phase_2(sub):
        pass_keys(2, sub)
        o_take(1, 3, sub)
        o_out(1, 2, sub)
        catch_up(2, sub)

    def phase_3(sub):
        o_forward(0, 1, sub)
        pass_keys(3, sub)
        o_out(1, 3, sub)
        o_in(1, 1, sub)
        o_in(0, 1, sub)
        catch_up(3, sub)

    each_sub(phase_1)
    each_sub(phase_2)
    each_sub(phase_3)
    attend_hop(3, heads - 1)
    each_sub(lambda sub: o_in(1, 2, sub))
    each_sub(lambda sub: o_in(1, 3, sub))

    def climbed(number):
        return number // SUBS + 1, number % SUBS

    w_whole.wait_send()
    each_sub(lambda sub: w_settle(sub, True))
    attended = w.at[pl.ds(0, frames), pl.ds(0, q_width)]

    def slot_in(place, slot):
        return w.at[pl.ds(place * frames, frames), pl.ds(pl.multiple_of(slot * 2 * wide, 2 * wide), 2 * wide)]

    def kept(slot):
        return slot_in(1, slot)

    def leaving(slot):
        return slot_in(2, slot)

    def carry(slot):
        return remote(leaving(slot), came.at[slot], x_s.at[slot], x_r.at[slot], across)

    @pl.loop(0, heads)
    def _(head):
        for r in range(repeat):
            index = head * repeat + r
            out = (acc_ref[index] / l_ref[index]).T.astype(jnp.bfloat16)
            attended[:, pl.ds(pl.multiple_of(index * HEAD_DIM, HEAD_DIM), HEAD_DIM)] = out

    orders = [
        [[2, 3, 0, 1], [0, 1, 2, 3]],
        [[2, 3, 1, 0], [1, 0, 2, 3]],
        [[2, 3, 1, 0], [1, 2, 0, 3]],
        [[3, 2, 1, 0], [3, 2, 1, 0]],
    ]
    turns = []
    for place in range(4):
        group = 0
        for plane in range(4):
            for side in range(2):
                group = jnp.where((z == plane) & (t == side), orders[plane][side][place], group)
        turns.append(group)

    def which(task):
        place, sub = task // SUBS, task % SUBS
        group = turns[3]
        for index in range(3):
            group = jnp.where(place == index, turns[index], group)
        return group, sub

    def ready(task):
        group, sub = which(task)

        @pl.when(group > z)
        def _():
            for kind in range(2):
                o_inward(1, kind, group - z, sub).wait_recv()

        @pl.when(group < z)
        def _():
            for kind in range(2):
                o_inward(0, kind, z - group, sub).wait_recv()

    def load(task, buffer, core):
        group, sub = which(task)
        return pltpu.make_async_copy(
            wo.at[2 * group + core, sub],
            w.at[pl.ds(4 * frames, out_depth), pl.ds((2 * buffer + core) * wide, wide)],
            stage_sem.at[buffer, core],
        )

    def shares(task, buffer):
        group, sub = which(task)
        for core in range(2):
            load(task, buffer, core).wait()
        weights = w[4 * frames:4 * frames + out_depth, 2 * buffer * wide:2 * (buffer + 1) * wide]
        share = jnp.dot(attended[...], weights, preferred_element_type=jnp.float32).astype(jnp.bfloat16)
        slot = (group % 2) * SUBS + sub

        @pl.when(group // 2 == t)
        def _():
            kept(slot)[...] = share

        @pl.when(group // 2 != t)
        def _():
            leaving(slot)[...] = share
            carry(slot).start()

    def work(*tasks):
        for buffer, task in enumerate(tasks):
            ready(task)
            for core in range(2):
                load(task, buffer, core).start()
        for buffer, task in enumerate(tasks):
            shares(task, buffer)

    o_whole.wait_recv()

    relay = z == 2

    @pl.when(jnp.logical_not(relay))
    def _():
        @pl.loop(0, SUBS - 1)
        def _(pair):
            work(2 * pair, 2 * pair + 1)

    @pl.loop(0, 2 * SUBS - 1)
    def _(pair):
        number = pair + SUBS
        o_on(0, *climbed(number))

        @pl.when(pair > 0)
        def _():
            o_in(0, *climbed(number - 1))

        @pl.when(relay)
        def _():
            work(2 * pair, 2 * pair + 1)

        @pl.when(jnp.logical_not(relay))
        def _():
            work(2 * SUBS - 2 + pair)

    o_on(0, last, SUBS - 1)
    o_in(0, last, SUBS - 2)

    @pl.when(jnp.logical_not(relay))
    def _():
        work(4 * SUBS - 3)

    work(4 * SUBS - 2)
    o_in(0, last, SUBS - 1)
    work(4 * SUBS - 1)

    high_first = jnp.where(z > 2 * t, 1, 0)

    @pl.loop(0, 2 * SUBS)
    def _(number):
        side, sub = number // SUBS, number % SUBS
        side = side + high_first * (1 - 2 * side)
        slot = side * SUBS + sub
        carry(slot).wait_recv()
        total = (kept(slot)[...].astype(jnp.float32) + came[slot].astype(jnp.float32)).astype(jnp.bfloat16)
        for core in range(2):
            start = pl.multiple_of((side * 2 + core) * block + sub * wide, wide)
            out_ref[:, pl.ds(start, wide)] = total[:, core * wide:(core + 1) * wide]

    o_whole.wait_send()

    @pl.loop(0, 2 * SUBS)
    def _(slot):
        carry(slot).wait_send()

    def settle(sub):
        crossing(sub).wait_send()
        swap(sub).wait_send()
        for hop in range(last + 1):
            @pl.when(z >= hop)
            def _():
                hand(hop, sub).wait_send()
                if hop < last:
                    @pl.when(z < last)
                    def _():
                        climb(hop, sub).wait_send()
        o_settle(sub)

    each_sub(settle)


def crossed(hidden, norm_gain, query_weight, key_weight, value_weight, out_weight):
    frames, features = hidden.shape
    depth, q_width = query_weight.shape
    kv_width = key_weight.shape[1]
    repeat = q_width // kv_width
    total = q_width + 2 * kv_width
    out_depth, block = out_weight.shape
    wide = block // SUBS
    count = q_width // HEAD_DIM
    dma = pltpu.SemaphoreType.DMA
    anywhere = pl.BlockSpec(memory_space=pl.ANY)
    vmem = pl.BlockSpec(memory_space=pltpu.VMEM)
    bf16, f32 = jnp.bfloat16, jnp.float32
    line = [dma((2, 3, SUBS))] * 4 + [dma((2, 2, 3, SUBS))] * 2 + [dma] * 2
    out, _ = pl.pallas_call(
        functools.partial(cross_kernel, repeat),
        out_shape=(
            jax.ShapeDtypeStruct((frames, 4 * block), bf16),
            jax.ShapeDtypeStruct((8, SUBS, out_depth, wide), bf16),
        ),
        in_specs=[vmem] + [anywhere] * 5,
        out_specs=(vmem, anywhere),
        scratch_shapes=[
            pltpu.VMEM((8 * depth, total), bf16),
            pltpu.VMEM((2, frames, features), bf16),
            pltpu.VMEM((4, frames, features // 2), bf16),
            pltpu.VMEM((total // HEAD_DIM, HEAD_DIM, frames), f32),
            pltpu.VMEM((kv_width // HEAD_DIM, 8 * frames, 2 * HEAD_DIM), bf16),
            pltpu.VMEM((count, 1, frames), f32),
            pltpu.VMEM((count, 1, frames), f32),
            pltpu.VMEM((2 * SUBS, frames, 2 * wide), bf16),
            dma((4,)), dma((SUBS,)), dma((2, 2)),
            dma((SUBS,)), dma((SUBS,)), dma((SUBS,)), dma((SUBS,)),
            dma((3, SUBS)), dma((3, SUBS)), dma((4, SUBS)), dma((4, SUBS)),
            *line, *line,
            dma((2 * SUBS,)), dma((2 * SUBS,)),
        ],
        compiler_params=pltpu.CompilerParams(
            collective_id=0, has_side_effects=True, vmem_limit_bytes=60 * 1024 * 1024
        ),
        cost_estimate=pl.CostEstimate(
            flops=16 * frames * depth * total + 16 * frames * out_depth * block,
            bytes_accessed=4 * hidden.size,
            transcendentals=4 * frames * frames * count,
        ),
    )(norm_gain.reshape(1, -1), hidden, query_weight, key_weight, value_weight, out_weight)
    return out


def y_share(mine, core, after=None):
    depth = mine.shape[0] // 2
    part = lax.dynamic_slice_in_dim(mine, core * depth, depth, 0)
    near = lax.ppermute(part, "stream", [(0, 1), (1, 0)])
    if after is None:
        return near, swap_pairs(near, "seq")
    near, after = lax.optimization_barrier((near, after))
    return near, swap_pairs(near, "seq"), after


def fits(hidden, query_weight, key_weight):
    meshes = (lax.axis_size("stream"), lax.axis_size("seq"), lax.axis_size("tensor"))
    return (
        meshes == (2, 8, 2)
        and hidden.shape[1:] == (1, 512, 2048)
        and query_weight.shape == (512, 2048)
        and key_weight.shape == (512, 512)
    )


def body(hidden, norm_gain, query_weight, key_weight, value_projection_weight, out_weight):
    if not fits(hidden, query_weight, key_weight):
        return general_body(hidden, norm_gain, query_weight, key_weight, value_projection_weight, out_weight)
    out = crossed(
        hidden.reshape(hidden.shape[2:]), norm_gain, query_weight, key_weight, value_projection_weight, out_weight
    )
    return out.reshape(hidden.shape)


def general_body(hidden, norm_gain, query_weight, key_weight, value_projection_weight, out_weight):
    windows, frame_count = hidden.shape[1], hidden.shape[2]
    n_tensor = lax.axis_size("tensor")
    n_seq = lax.axis_size("seq")
    stream = lax.axis_index("stream")
    tensor = lax.axis_index("tensor")
    seq = lax.axis_index("seq")
    core = seq % 2
    rows = windows * frame_count
    depth = query_weight.shape[0] // 2
    out_half = out_weight.shape[1] // 2

    kv_weight = jnp.concatenate([key_weight, value_projection_weight], axis=1)
    kv_mine = lax.all_gather(
        lax.dynamic_slice_in_dim(kv_weight, stream * depth, depth, 0), "seq", axis=0, tiled=True
    )
    query_mine = lax.all_gather(
        lax.dynamic_slice_in_dim(query_weight, stream * depth, depth, 0), "seq", axis=0, tiled=True
    )
    out_mine = lax.all_gather(
        lax.dynamic_slice_in_dim(out_weight, stream * out_half, out_half, 1), "seq", axis=1, tiled=True
    )

    local = hidden.reshape(rows, hidden.shape[3])
    if n_tensor == 2:
        other = lax.ppermute(local, "tensor", [(0, 1), (1, 0)])
        gathered = jnp.where(
            tensor == 0,
            jnp.concatenate([local, other], axis=1),
            jnp.concatenate([other, local], axis=1),
        )
    else:
        gathered = lax.all_gather(local, "tensor", axis=1, tiled=True)
    flat = gathered.astype(jnp.float32)
    inverse_rms = lax.rsqrt(jnp.mean(flat * flat, axis=1, keepdims=True) + 1e-05)
    normed = (flat * inverse_rms * norm_gain).astype(jnp.bfloat16)
    split = normed.reshape(rows, n_seq, 2, depth)

    def features(half):
        return lax.dynamic_index_in_dim(split, half, 2, keepdims=False).reshape(rows, n_seq * depth)

    normed_mine = features(stream)
    normed_other = features(1 - stream)
    span = n_seq * depth // 2
    normed_near = lax.dynamic_slice_in_dim(normed_other, core * span, span, 1)
    normed_far = lax.dynamic_slice_in_dim(normed_other, (1 - core) * span, span, 1)

    def project(mine, near, far):
        total = jnp.dot(normed_mine, mine, preferred_element_type=jnp.float32)
        total += jnp.dot(normed_near, near, preferred_element_type=jnp.float32)
        total += jnp.dot(normed_far, far, preferred_element_type=jnp.float32)
        return total.astype(jnp.bfloat16)

    keys_values = project(kv_mine, *y_share(kv_mine, core))
    partner = lax.ppermute(keys_values, "stream", [(0, 1), (1, 0)])
    kv_width = key_weight.shape[1]
    parts = 2 if kv_width % (2 * HEAD_DIM) == 0 else 1
    step = kv_width // parts
    pieces = []
    for part in range(parts):
        columns = jnp.concatenate(
            [partner[:, part * step:(part + 1) * step],
             partner[:, kv_width + part * step:kv_width + (part + 1) * step]],
            axis=1,
        )
        pieces.append(
            lax.all_gather(columns.reshape(windows, frame_count, 2 * step), "seq", axis=1, tiled=True)
        )
    queries = project(query_mine, *y_share(query_mine, core)).reshape(windows, frame_count, -1)
    out_near = out_far = None
    width = out_weight.shape[0] // 2

    repeat = query_weight.shape[1] // key_weight.shape[1]
    chunk = frame_count // ROW_CHUNKS

    def scattered(share):
        if n_tensor == 2:
            wide = share.shape[1] // 2
            away = lax.dynamic_slice_in_dim(share, (1 - tensor) * wide, wide, 1)
            kept = lax.dynamic_slice_in_dim(share, tensor * wide, wide, 1)
            came = lax.ppermute(away, "tensor", [(0, 1), (1, 0)])
            return (kept.astype(jnp.float32) + came.astype(jnp.float32)).astype(jnp.bfloat16)
        return lax.psum_scatter(share, "tensor", scatter_dimension=1, tiled=True)

    outs = []
    q_step = step * repeat
    for window in range(windows):
        early = [
            attend(
                seq * frame_count,
                queries[window][:, part * q_step:(part + 1) * q_step],
                pieces[part][window],
                repeat,
            )
            for part in range(parts - 1)
        ]
        for index in range(ROW_CHUNKS):
            low, high = index * chunk, (index + 1) * chunk
            final = attend(
                seq * frame_count + low,
                queries[window][low:high, (parts - 1) * q_step:],
                pieces[-1][window],
                repeat,
            )
            attended = jnp.concatenate([done[low:high] for done in early] + [final], axis=1)
            share_mine = jnp.dot(attended, out_mine, preferred_element_type=jnp.float32)
            if out_near is None:
                out_near, out_far, attended = y_share(out_mine, core, attended)
            attended_near = lax.dynamic_slice_in_dim(attended, core * width, width, 1)
            attended_far = lax.dynamic_slice_in_dim(attended, (1 - core) * width, width, 1)
            share_other = jnp.dot(attended_near, out_near, preferred_element_type=jnp.float32)
            share_other += jnp.dot(attended_far, out_far, preferred_element_type=jnp.float32)
            mine = scattered(share_mine.astype(jnp.bfloat16)).reshape(chunk, -1, out_half)
            other = scattered(share_other.astype(jnp.bfloat16)).reshape(chunk, -1, out_half)
            outs.append(
                jnp.where(
                    stream == 0, jnp.stack([mine, other], axis=2), jnp.stack([other, mine], axis=2)
                ).reshape(chunk, -1)
            )
    return jnp.concatenate(outs, axis=0).reshape(1, windows, frame_count, -1)


def solution(mesh):
    in_specs = (
        P("stream", None, "seq", "tensor"),
        P(),
        P("seq", "tensor"),
        P("seq", "tensor"),
        P("seq", "tensor"),
        P("tensor", "seq"),
    )
    out_specs = P("stream", None, "seq", "tensor")
    return jax.shard_map(body, mesh=mesh, in_specs=in_specs, out_specs=out_specs, check_vma=False)
```

```python
import functools

import jax
import jax.numpy as jnp
from jax import lax
from jax.experimental import pallas as pl
from jax.experimental.pallas import tpu as pltpu
from jax.sharding import PartitionSpec as P

HEAD_DIM = 128
ROW_CHUNKS = 2
KEY_BLOCK = 1024
SUBS = 4
LOG2E = 1.4426950408889634


def swap_pairs(block, axis):
    count = lax.axis_size(axis)
    return lax.ppermute(block, axis, [(i, i ^ 1) for i in range(count)])


def attend_kernel(repeat, start_ref, q_ref, k_ref, v_ref, o_ref, m_ref, l_ref, acc_ref):
    step = pl.program_id(1)
    rows = q_ref.shape[0]
    keys = k_ref.shape[0]
    start = start_ref[0]
    last = (start + rows - 1) // keys
    scale = LOG2E * HEAD_DIM ** (-0.5)

    @pl.when(step == 0)
    def _():
        m_ref[...] = jnp.full_like(m_ref, -1e30)
        l_ref[...] = jnp.zeros_like(l_ref)
        acc_ref[...] = jnp.zeros_like(acc_ref)

    def update(masked):
        k = k_ref[...]
        v = v_ref[...]
        if masked:
            frame = start + lax.broadcasted_iota(jnp.int32, (keys, rows), 1)
            key = step * keys + lax.broadcasted_iota(jnp.int32, (keys, rows), 0)
            allowed = key <= frame

        def scored(r):
            q = q_ref[:, r * HEAD_DIM:(r + 1) * HEAD_DIM]
            return lax.dot_general(k, q, (((1,), (1,)), ((), ())), preferred_element_type=jnp.float32)

        following = scored(0)
        for r in range(repeat):
            s = following
            if r + 1 < repeat:
                following = scored(r + 1)
            if masked:
                s = jnp.where(allowed, s, -1e30)
            top = jnp.max(s, axis=0, keepdims=True) * scale
            before = m_ref[r]
            fresh = jnp.maximum(before, top)
            m_ref[r] = fresh
            alpha = jnp.exp2(before - fresh)
            p = jnp.exp2(s * scale - fresh)
            l_ref[r] = alpha * l_ref[r] + jnp.sum(p, axis=0, keepdims=True)
            acc_ref[r] = alpha * acc_ref[r] + lax.dot_general(
                v, p.astype(jnp.bfloat16), (((0,), (0,)), ((), ())), preferred_element_type=jnp.float32
            )

    @pl.when(step < last)
    def _():
        update(False)

    @pl.when(step == last)
    def _():
        update(True)
        for r in range(repeat):
            attended = (acc_ref[r] / l_ref[r]).T
            o_ref[:, r * HEAD_DIM:(r + 1) * HEAD_DIM] = attended.astype(o_ref.dtype)


def attend(start, queries, keys_values, repeat):
    rows, width = queries.shape
    count = keys_values.shape[0]
    groups = width // (repeat * HEAD_DIM)
    block = min(KEY_BLOCK, count)

    def at(step, start_ref):
        return jnp.minimum(step, (start_ref[0] + rows - 1) // block)

    return pl.pallas_call(
        functools.partial(attend_kernel, repeat),
        out_shape=jax.ShapeDtypeStruct((rows, width), jnp.bfloat16),
        grid_spec=pltpu.PrefetchScalarGridSpec(
            num_scalar_prefetch=1,
            grid=(groups, count // block),
            in_specs=[
                pl.BlockSpec((rows, repeat * HEAD_DIM), lambda g, i, s: (0, g)),
                pl.BlockSpec((block, HEAD_DIM), lambda g, i, s: (at(i, s), g)),
                pl.BlockSpec((block, HEAD_DIM), lambda g, i, s: (at(i, s), groups + g)),
            ],
            out_specs=pl.BlockSpec((rows, repeat * HEAD_DIM), lambda g, i, s: (0, g)),
            scratch_shapes=[
                pltpu.VMEM((repeat, 1, rows), jnp.float32),
                pltpu.VMEM((repeat, 1, rows), jnp.float32),
                pltpu.VMEM((repeat, HEAD_DIM, rows), jnp.float32),
            ],
        ),
        compiler_params=pltpu.CompilerParams(
            dimension_semantics=("arbitrary", "arbitrary"), vmem_limit_bytes=32 * 1024 * 1024
        ),
        cost_estimate=pl.CostEstimate(
            flops=8 * rows * count * width,
            bytes_accessed=2 * (2 * rows * width + keys_values.size),
            transcendentals=rows * count * width // HEAD_DIM,
        ),
    )(start.reshape(1), queries, keys_values, keys_values)


def line_order(z):
    first = z - 1 + 2 * ((3 - z) // 3)
    third = 3 * (1 - z // 2)
    return (z, first, 6 - z - first - third, third)


def remote(src, dst, send, recv, device):
    return pltpu.make_async_remote_copy(
        src_ref=src, dst_ref=dst, send_sem=send, recv_sem=recv, device_id=device, device_id_type=pl.DeviceIdType.MESH
    )


def greet(z, last, devices, up, down):
    barrier = pltpu.get_barrier_semaphore()

    def hello(device):
        pl.semaphore_signal(barrier, inc=1, device_id=device, device_id_type=pl.DeviceIdType.MESH)

    for device in devices:
        hello(device)

    @pl.when(z < last)
    def _():
        hello(up)

    @pl.when(z > 0)
    def _():
        hello(down)

    inner = jnp.where((z > 0) & (z < last), 1, 0)
    pl.semaphore_wait(barrier, len(devices) + 1 + inner)


def cross_kernel(
    repeat, gain_ref, hidden_ref, wq_ref, wk_ref, wv_ref, wo_ref, out_ref, wo,
    w, hid, normed, acc_ref, kv, m_ref, l_ref, came,
    fill_sem, wo_sem, stage_sem, cross_s, cross_r, swap_s, swap_r, k_s, k_r, kc_s, kc_r,
    wz_s, wz_r, wy_s, wy_r, wc_s, wc_r, w_own_s, w_own_r,
    oz_s, oz_r, oy_s, oy_r, oc_s, oc_r, o_own_s, o_own_r, x_s, x_r,
):
    last = 3
    c = lax.axis_index("stream")
    s = lax.axis_index("seq")
    t = lax.axis_index("tensor")
    z, k = s // 2, s % 2
    depth, q_width = wq_ref.shape
    half = depth // 2
    rows = half // SUBS
    kv_width = wk_ref.shape[1]
    frames = hid.shape[1]
    step = frames // SUBS
    out_depth, block = wo_ref.shape
    out_half = out_depth // 2
    wide = block // SUBS
    heads = kv_width // HEAD_DIM
    scale = LOG2E * HEAD_DIM ** (-0.5)
    at = {"stream": c, "seq": s, "tensor": t}
    up, down = {**at, "seq": s + 2}, {**at, "seq": s - 2}
    beside, mate, across = {**at, "stream": 1 - c}, {**at, "seq": 2 * z + 1 - k}, {**at, "tensor": 1 - t}
    greet(z, last, (beside, mate, across), up, down)
    sends = (z < last, z > 0)

    def each_sub(action):
        @pl.loop(0, SUBS)
        def _(sub):
            action(sub)

    def source(way, hop):
        return z - hop if way == 0 else z + hop

    def arrives(way, hop):
        return z >= hop if way == 0 else z + hop <= last

    def w_part(origin, core, side, sub):
        start = pl.multiple_of(origin * (2 * depth) + core * depth + side * half + sub * rows, rows)
        return w.at[pl.ds(start, rows)]

    def o_part(origin, core, side, sub):
        return wo.at[2 * origin + core, sub, pl.ds(pl.multiple_of(side * out_half, out_half), out_half)]

    def routes(part, z_s, z_r, y_s, y_r, c_s, c_r):
        def along(way, hop, sub):
            view = part(source(way, hop), k, c, sub)
            return remote(view, view, z_s.at[way, hop, sub], z_r.at[way, hop, sub], up if way == 0 else down)

        def sideways(way, hop, sub):
            view = part(source(way, hop), k, c, sub)
            return remote(view, view, y_s.at[way, hop - 1, sub], y_r.at[way, hop - 1, sub], beside)

        def inward(way, kind, hop, sub):
            view = part(source(way, hop), k, c if kind == 0 else 1 - c, sub)
            return remote(view, view, c_s.at[way, kind, hop - 1, sub], c_r.at[way, kind, hop - 1, sub], mate)

        def leave(way):
            @pl.when(sends[way])
            def _():
                each_sub(lambda sub: along(way, 0, sub).start())

        def pass_on(way, hop, sub):
            @pl.when(arrives(way, hop))
            def _():
                along(way, hop - 1, sub).wait_recv()

                @pl.when(sends[way] & (hop < last))
                def _():
                    along(way, hop, sub).start()

                sideways(way, hop, sub).start()
                inward(way, 0, hop, sub).start()

        def take(way, hop, sub):
            @pl.when(arrives(way, hop))
            def _():
                along(way, hop - 1, sub).wait_recv()
                inward(way, 0, hop, sub).start()

        def forward(way, hop, sub):
            @pl.when(arrives(way, hop) & sends[way])
            def _():
                along(way, hop, sub).start()

        def share_out(way, hop, sub):
            @pl.when(arrives(way, hop))
            def _():
                sideways(way, hop, sub).start()

        def pass_in(way, hop, sub):
            @pl.when(arrives(way, hop))
            def _():
                sideways(way, hop, sub).wait_recv()
                inward(way, 1, hop, sub).start()

        def gathered(way, hop):
            @pl.when(arrives(way, hop))
            def _():
                def action(sub):
                    inward(way, 0, hop, sub).wait_recv()
                    inward(way, 1, hop, sub).wait_recv()

                each_sub(action)

        def final_hop(way):
            return z if way == 0 else last - z

        def drained(way):
            @pl.when(sends[way])
            def _():
                along(way, final_hop(way), SUBS - 1).wait_send()

        def settle(sub, seen=False):
            for way in range(2):
                for hop in range(last):
                    unseen = jnp.logical_not((final_hop(way) == hop) & (sub == SUBS - 1)) if seen else True

                    @pl.when(sends[way] & arrives(way, hop) & unseen)
                    def _():
                        along(way, hop, sub).wait_send()
                for hop in range(1, last + 1):
                    @pl.when(arrives(way, hop))
                    def _():
                        sideways(way, hop, sub).wait_send()
                        inward(way, 0, hop, sub).wait_send()
                        inward(way, 1, hop, sub).wait_send()

        return leave, pass_on, pass_in, gathered, settle, inward, (take, forward, share_out), drained

    w_leave, w_on, w_in, w_gathered, w_settle, _, _, w_drained = routes(w_part, wz_s, wz_r, wy_s, wy_r, wc_s, wc_r)
    o_leave, o_on, o_in, _, o_settle, o_inward, (o_take, o_forward, o_out), _ = routes(o_part, oz_s, oz_r, oy_s, oy_r, oc_s, oc_r)

    own = pl.multiple_of(s * depth, depth)
    fills = [
        pltpu.make_async_copy(wq_ref, w.at[pl.ds(own, depth), pl.ds(0, q_width)], fill_sem.at[0]),
        pltpu.make_async_copy(wk_ref, w.at[pl.ds(own, depth), pl.ds(q_width, kv_width)], fill_sem.at[1]),
        pltpu.make_async_copy(wv_ref, w.at[pl.ds(own, depth), pl.ds(q_width + kv_width, kv_width)], fill_sem.at[2]),
    ]
    mine = pltpu.make_async_copy(hidden_ref, hid.at[t], fill_sem.at[3])
    wo_fills = [
        pltpu.make_async_copy(wo_ref.at[:, pl.ds(sub * wide, wide)], wo.at[s, sub], wo_sem.at[sub])
        for sub in range(SUBS)
    ]

    def crossing(piece):
        start = pl.multiple_of(piece * step, step)
        return remote(
            hidden_ref.at[pl.ds(start, step)], hid.at[t, pl.ds(start, step)],
            cross_s.at[piece], cross_r.at[piece], across,
        )

    for copy in fills:
        copy.start()
    mine.start()
    each_sub(lambda piece: crossing(piece).start())
    for copy in fills:
        copy.wait()
    for way in range(2):
        w_leave(way)
    w_block = w.at[pl.ds(own, depth)]
    w_whole = remote(w_block, w_block, w_own_s, w_own_r, mate)
    w_whole.start()
    for copy in wo_fills:
        copy.start()

    tall = 16

    def norm(sub):
        crossing(sub).wait_recv()

        @pl.loop(0, step // tall)
        def _(i):
            at_rows = pl.ds(pl.multiple_of(sub * step + i * tall, tall), tall)
            low = hid[0, at_rows, :].astype(jnp.float32)
            high = hid[1, at_rows, :].astype(jnp.float32)
            total = jnp.sum(low * low, axis=1, keepdims=True) + jnp.sum(high * high, axis=1, keepdims=True)
            inverse_rms = lax.rsqrt(total / (2 * low.shape[1]) + 1e-05)
            part = normed.shape[2]
            for group in range(4):
                x = (low if group < 2 else high)[:, (group % 2) * part:(group % 2 + 1) * part]
                gain = gain_ref[:, group * part:(group + 1) * part]
                normed[group, at_rows, :] = (x * inverse_rms * gain).astype(jnp.bfloat16)

    order = line_order(z)
    tile = 512
    tiles = (q_width + 2 * kv_width) // tile
    q_tiles = q_width // tile
    folds = frames // HEAD_DIM

    def dot(place, index):
        group = order[place]
        columns = pl.ds(pl.multiple_of(index * tile, tile), tile)
        return jnp.dot(
            normed[group],
            w[pl.ds(pl.multiple_of(group * 2 * depth, 2 * depth), 2 * depth), columns],
            preferred_element_type=jnp.float32,
        )

    def held(index):
        return pl.ds(index * folds, folds)

    def project(place, low, high):
        @pl.loop(low, high)
        def _(index):
            value = dot(place, index).reshape(folds, HEAD_DIM, tile)
            if place == 0:
                acc_ref[held(index)] = value
            else:
                acc_ref[held(index)] += value

    def finish(index):
        total = acc_ref[held(index)].reshape(frames, tile) + dot(3, index)
        return total.astype(jnp.bfloat16)

    def first_hop(sub):
        for way in range(2):
            w_on(way, 1, sub)

    def second_hop(sub):
        for way in range(2):
            w_on(way, 2, sub)
            w_in(way, 1, sub)
        norm(sub)

    each_sub(first_hop)
    mine.wait()
    each_sub(second_hop)
    w_whole.wait_recv()
    for way in range(2):
        w_gathered(way, 1)
    for copy in wo_fills:
        copy.wait()
    for sub in range(SUBS):
        for way in range(2):
            w_on(way, 3, sub)
            if sub == SUBS - 1:
                w_drained(way)
                o_leave(way)
            w_in(way, 2, sub)
        low, high = sub * 2 * tiles // SUBS, (sub + 1) * 2 * tiles // SUBS
        for place in range(2):
            begin, end = max(low - place * tiles, 0), min(high - place * tiles, tiles)
            if begin < end:
                project(place, begin, end)
    for way in range(2):
        w_gathered(way, 2)
    o_whole = remote(wo.at[s], wo.at[s], o_own_s, o_own_r, mate)
    o_whole.start()
    project(2, 0, tiles)
    for way in range(2):
        each_sub(lambda sub: w_in(way, 3, sub))
        w_gathered(way, 3)

    for index in range(2 * kv_width // tile):
        piece = finish(q_tiles + index)
        for head in range(heads):
            start = (2 * head + index) * HEAD_DIM
            hid[1, :, start:start + HEAD_DIM] = piece[:, head * HEAD_DIM:(head + 1) * HEAD_DIM]

    def key_rows(hop, head):
        start = pl.multiple_of((2 * (z - hop) + k) * frames, frames)
        return kv.at[head, pl.ds(start, frames)]

    def swap(head):
        start = pl.multiple_of(head * 2 * HEAD_DIM, 2 * HEAD_DIM)
        return remote(
            hid.at[1, pl.ds(0, frames), pl.ds(start, 2 * HEAD_DIM)], key_rows(0, head),
            swap_s.at[head], swap_r.at[head], beside,
        )

    def climb(hop, sub):
        view = key_rows(hop, sub)
        return remote(view, view, k_s.at[hop, sub], k_r.at[hop, sub], up)

    def hand(hop, sub):
        view = key_rows(hop, sub)
        return remote(view, view, kc_s.at[hop, sub], kc_r.at[hop, sub], mate)

    def pass_keys(hop, sub):
        @pl.when(z >= hop)
        def _():
            climb(hop - 1, sub).wait_recv()
            if hop < last:
                @pl.when(z < last)
                def _():
                    climb(hop, sub).start()
            hand(hop, sub).start()

    each_sub(lambda sub: swap(sub).start())

    @pl.loop(0, q_tiles)
    def _(index):
        hid[0, :, pl.ds(pl.multiple_of(index * tile, tile), tile)] = finish(index)

    def attend_to(head, start, count, masked):
        at_keys = pl.ds(pl.multiple_of(start, count), count)
        keys_here = kv[head, at_keys, 0:HEAD_DIM]
        values_here = kv[head, at_keys, HEAD_DIM:2 * HEAD_DIM]
        if masked:
            allowed = lax.broadcasted_iota(jnp.int32, (count, frames), 0) <= lax.broadcasted_iota(
                jnp.int32, (count, frames), 1
            )

        def scored(r):
            q = hid[0, :, pl.ds(pl.multiple_of((head * repeat + r) * HEAD_DIM, HEAD_DIM), HEAD_DIM)]
            return lax.dot_general(
                keys_here, q, (((1,), (1,)), ((), ())), preferred_element_type=jnp.float32
            )

        following = scored(0)
        for r in range(repeat):
            index = head * repeat + r
            scores = following
            if r + 1 < repeat:
                following = scored(r + 1)
            if masked:
                scores = jnp.where(allowed, scores, -1e30)
            top = jnp.max(scores, axis=0, keepdims=True) * scale
            before = m_ref[index]
            fresh = jnp.maximum(before, top)
            m_ref[index] = fresh
            alpha = jnp.exp2(before - fresh)
            p = jnp.exp2(scores * scale - fresh)
            l_ref[index] = alpha * l_ref[index] + jnp.sum(p, axis=0, keepdims=True)
            acc_ref[index] = alpha * acc_ref[index] + lax.dot_general(
                values_here, p.astype(jnp.bfloat16), (((0,), (0,)), ((), ())), preferred_element_type=jnp.float32
            )

    def attend_own(head):
        hand(0, head).wait_recv()
        attend_to(head, s * frames, frames, True)

        @pl.when(k == 1)
        def _():
            attend_to(head, (s - 1) * frames, frames, False)

    def attend_hop(hop, head):
        @pl.when(z >= hop)
        def _():
            hand(hop, head).wait_recv()
            attend_to(head, (z - hop) * 2 * frames, 2 * frames, False)

    m_ref[...] = jnp.full_like(m_ref, -1e30)
    l_ref[...] = jnp.zeros_like(l_ref)
    acc_ref[...] = jnp.zeros_like(acc_ref)

    def first(sub):
        swap(sub).wait_recv()

        @pl.when(z < last)
        def _():
            climb(0, sub).start()

        hand(0, sub).start()
        o_take(1, 1, sub)
        o_forward(1, 1, sub)

        @pl.when(sub > 0)
        def _():
            attend_own(sub - 1)

    each_sub(first)

    def catch_up(hop, sub):
        @pl.when(sub > 0)
        def _():
            attend_hop(hop, sub - 1)

        @pl.when(sub == 0)
        def _():
            if hop == 1:
                attend_own(heads - 1)
            else:
                attend_hop(hop - 1, heads - 1)

    def phase_1(sub):
        pass_keys(1, sub)
        o_take(1, 2, sub)
        o_forward(1, 2, sub)
        o_take(0, 1, sub)
        o_out(1, 1, sub)
        o_out(0, 1, sub)
        catch_up(1, sub)

    def phase_2(sub):
        pass_keys(2, sub)
        o_take(1, 3, sub)
        o_out(1, 2, sub)
        catch_up(2, sub)

    def phase_3(sub):
        o_forward(0, 1, sub)
        pass_keys(3, sub)
        o_out(1, 3, sub)
        o_in(1, 1, sub)
        o_in(0, 1, sub)
        catch_up(3, sub)

    each_sub(phase_1)
    each_sub(phase_2)
    each_sub(phase_3)
    attend_hop(3, heads - 1)

    def climbed(number):
        return number // SUBS + 1, number % SUBS

    o_on(0, 2, 0)
    o_on(0, 2, 1)
    w_whole.wait_send()
    each_sub(lambda sub: w_settle(sub, True))
    attended = w.at[pl.ds(0, frames), pl.ds(0, q_width)]

    def slot_in(place, slot):
        return w.at[pl.ds(place * frames, frames), pl.ds(pl.multiple_of(slot * 2 * wide, 2 * wide), 2 * wide)]

    def kept(slot):
        return slot_in(1, slot)

    def leaving(slot):
        return slot_in(2, slot)

    def carry(slot):
        return remote(leaving(slot), came.at[slot], x_s.at[slot], x_r.at[slot], across)

    @pl.loop(0, heads)
    def _(head):
        for r in range(repeat):
            index = head * repeat + r
            out = (acc_ref[index] / l_ref[index]).T.astype(jnp.bfloat16)
            attended[:, pl.ds(pl.multiple_of(index * HEAD_DIM, HEAD_DIM), HEAD_DIM)] = out

    orders = [
        [[2, 3, 0, 1], [0, 1, 2, 3]],
        [[2, 3, 1, 0], [1, 0, 2, 3]],
        [[2, 3, 1, 0], [1, 2, 0, 3]],
        [[3, 2, 1, 0], [3, 2, 1, 0]],
    ]
    blend = [
        (3, 0), (3, 1), (1, 0), (1, 1), (3, 2), (1, 2), (1, 3), (3, 3),
        (2, 0), (0, 0), (0, 1), (2, 1), (0, 2), (2, 2), (2, 3), (0, 3),
    ]
    turns = []
    for place in range(4):
        group = 0
        for plane in range(4):
            for side in range(2):
                group = jnp.where((z == plane) & (t == side), orders[plane][side][place], group)
        turns.append(group)

    def which(task):
        place, sub = task // SUBS, task % SUBS
        group = turns[3]
        for index in range(3):
            group = jnp.where(place == index, turns[index], group)
        mixed = (z == last) & (t == 1)
        for index, (plane, piece) in enumerate(blend):
            here = mixed & (task == index)
            group = jnp.where(here, plane, group)
            sub = jnp.where(here, piece, sub)
        return group, sub

    def ready(task):
        group, sub = which(task)

        @pl.when(group > z)
        def _():
            for kind in range(2):
                o_inward(1, kind, group - z, sub).wait_recv()

        @pl.when(group < z)
        def _():
            for kind in range(2):
                o_inward(0, kind, z - group, sub).wait_recv()

    def load(task, buffer, core):
        group, sub = which(task)
        return pltpu.make_async_copy(
            wo.at[2 * group + core, sub],
            w.at[pl.ds(4 * frames, out_depth), pl.ds((2 * buffer + core) * wide, wide)],
            stage_sem.at[buffer, core],
        )

    def shares(task, buffer):
        group, sub = which(task)
        for core in range(2):
            load(task, buffer, core).wait()
        weights = w[4 * frames:4 * frames + out_depth, 2 * buffer * wide:2 * (buffer + 1) * wide]
        share = jnp.dot(attended[...], weights, preferred_element_type=jnp.float32).astype(jnp.bfloat16)
        slot = (group % 2) * SUBS + sub

        @pl.when(group // 2 == t)
        def _():
            kept(slot)[...] = share

        @pl.when(group // 2 != t)
        def _():
            leaving(slot)[...] = share
            carry(slot).start()

    def work(*tasks):
        for buffer, task in enumerate(tasks):
            ready(task)
            for core in range(2):
                load(task, buffer, core).start()
        for buffer, task in enumerate(tasks):
            shares(task, buffer)

    o_whole.wait_recv()

    o_on(0, 2, 2)
    o_in(1, 2, 0)
    o_in(1, 2, 1)
    work(0, 1)
    o_on(0, 2, 3)
    o_in(0, 2, 0)
    o_in(0, 2, 1)
    o_in(1, 2, 2)
    o_in(1, 2, 3)
    work(2, 3)
    o_in(0, 2, 2)
    each_sub(lambda sub: o_in(1, 3, sub))
    work(4, 5)

    @pl.loop(0, SUBS)
    def _(sub):
        o_on(0, last, sub)
        o_in(0, *climbed(2 * SUBS - 1 + sub))
        work(6 + 2 * sub, 7 + 2 * sub)

    work(4 * SUBS - 2)
    o_in(0, last, SUBS - 1)
    work(4 * SUBS - 1)

    high_first = jnp.where(z > 2 * t, 1, 0)

    @pl.loop(0, 2 * SUBS)
    def _(number):
        side, sub = number // SUBS, number % SUBS
        side = side + high_first * (1 - 2 * side)
        slot = side * SUBS + sub
        carry(slot).wait_recv()
        total = (kept(slot)[...].astype(jnp.float32) + came[slot].astype(jnp.float32)).astype(jnp.bfloat16)
        for core in range(2):
            start = pl.multiple_of((side * 2 + core) * block + sub * wide, wide)
            out_ref[:, pl.ds(start, wide)] = total[:, core * wide:(core + 1) * wide]

    o_whole.wait_send()

    @pl.loop(0, 2 * SUBS)
    def _(slot):
        carry(slot).wait_send()

    def settle(sub):
        crossing(sub).wait_send()
        swap(sub).wait_send()
        for hop in range(last + 1):
            @pl.when(z >= hop)
            def _():
                hand(hop, sub).wait_send()
                if hop < last:
                    @pl.when(z < last)
                    def _():
                        climb(hop, sub).wait_send()
        o_settle(sub)

    each_sub(settle)


def crossed(hidden, norm_gain, query_weight, key_weight, value_weight, out_weight):
    frames, features = hidden.shape
    depth, q_width = query_weight.shape
    kv_width = key_weight.shape[1]
    repeat = q_width // kv_width
    total = q_width + 2 * kv_width
    out_depth, block = out_weight.shape
    wide = block // SUBS
    count = q_width // HEAD_DIM
    dma = pltpu.SemaphoreType.DMA
    anywhere = pl.BlockSpec(memory_space=pl.ANY)
    vmem = pl.BlockSpec(memory_space=pltpu.VMEM)
    bf16, f32 = jnp.bfloat16, jnp.float32
    line = [dma((2, 3, SUBS))] * 4 + [dma((2, 2, 3, SUBS))] * 2 + [dma] * 2
    out, _ = pl.pallas_call(
        functools.partial(cross_kernel, repeat),
        out_shape=(
            jax.ShapeDtypeStruct((frames, 4 * block), bf16),
            jax.ShapeDtypeStruct((8, SUBS, out_depth, wide), bf16),
        ),
        in_specs=[vmem] + [anywhere] * 5,
        out_specs=(vmem, anywhere),
        scratch_shapes=[
            pltpu.VMEM((8 * depth, total), bf16),
            pltpu.VMEM((2, frames, features), bf16),
            pltpu.VMEM((4, frames, features // 2), bf16),
            pltpu.VMEM((total // HEAD_DIM, HEAD_DIM, frames), f32),
            pltpu.VMEM((kv_width // HEAD_DIM, 8 * frames, 2 * HEAD_DIM), bf16),
            pltpu.VMEM((count, 1, frames), f32),
            pltpu.VMEM((count, 1, frames), f32),
            pltpu.VMEM((2 * SUBS, frames, 2 * wide), bf16),
            dma((4,)), dma((SUBS,)), dma((2, 2)),
            dma((SUBS,)), dma((SUBS,)), dma((SUBS,)), dma((SUBS,)),
            dma((3, SUBS)), dma((3, SUBS)), dma((4, SUBS)), dma((4, SUBS)),
            *line, *line,
            dma((2 * SUBS,)), dma((2 * SUBS,)),
        ],
        compiler_params=pltpu.CompilerParams(
            collective_id=0, has_side_effects=True, vmem_limit_bytes=60 * 1024 * 1024
        ),
        cost_estimate=pl.CostEstimate(
            flops=16 * frames * depth * total + 16 * frames * out_depth * block,
            bytes_accessed=4 * hidden.size,
            transcendentals=4 * frames * frames * count,
        ),
    )(norm_gain.reshape(1, -1), hidden, query_weight, key_weight, value_weight, out_weight)
    return out


def y_share(mine, core, after=None):
    depth = mine.shape[0] // 2
    part = lax.dynamic_slice_in_dim(mine, core * depth, depth, 0)
    near = lax.ppermute(part, "stream", [(0, 1), (1, 0)])
    if after is None:
        return near, swap_pairs(near, "seq")
    near, after = lax.optimization_barrier((near, after))
    return near, swap_pairs(near, "seq"), after


def fits(hidden, query_weight, key_weight):
    meshes = (lax.axis_size("stream"), lax.axis_size("seq"), lax.axis_size("tensor"))
    return (
        meshes == (2, 8, 2)
        and hidden.shape[1:] == (1, 512, 2048)
        and query_weight.shape == (512, 2048)
        and key_weight.shape == (512, 512)
    )


def body(hidden, norm_gain, query_weight, key_weight, value_projection_weight, out_weight):
    if not fits(hidden, query_weight, key_weight):
        return general_body(hidden, norm_gain, query_weight, key_weight, value_projection_weight, out_weight)
    out = crossed(
        hidden.reshape(hidden.shape[2:]), norm_gain, query_weight, key_weight, value_projection_weight, out_weight
    )
    return out.reshape(hidden.shape)


def general_body(hidden, norm_gain, query_weight, key_weight, value_projection_weight, out_weight):
    windows, frame_count = hidden.shape[1], hidden.shape[2]
    n_tensor = lax.axis_size("tensor")
    n_seq = lax.axis_size("seq")
    stream = lax.axis_index("stream")
    tensor = lax.axis_index("tensor")
    seq = lax.axis_index("seq")
    core = seq % 2
    rows = windows * frame_count
    depth = query_weight.shape[0] // 2
    out_half = out_weight.shape[1] // 2

    kv_weight = jnp.concatenate([key_weight, value_projection_weight], axis=1)
    kv_mine = lax.all_gather(
        lax.dynamic_slice_in_dim(kv_weight, stream * depth, depth, 0), "seq", axis=0, tiled=True
    )
    query_mine = lax.all_gather(
        lax.dynamic_slice_in_dim(query_weight, stream * depth, depth, 0), "seq", axis=0, tiled=True
    )
    out_mine = lax.all_gather(
        lax.dynamic_slice_in_dim(out_weight, stream * out_half, out_half, 1), "seq", axis=1, tiled=True
    )

    local = hidden.reshape(rows, hidden.shape[3])
    if n_tensor == 2:
        other = lax.ppermute(local, "tensor", [(0, 1), (1, 0)])
        gathered = jnp.where(
            tensor == 0,
            jnp.concatenate([local, other], axis=1),
            jnp.concatenate([other, local], axis=1),
        )
    else:
        gathered = lax.all_gather(local, "tensor", axis=1, tiled=True)
    flat = gathered.astype(jnp.float32)
    inverse_rms = lax.rsqrt(jnp.mean(flat * flat, axis=1, keepdims=True) + 1e-05)
    normed = (flat * inverse_rms * norm_gain).astype(jnp.bfloat16)
    split = normed.reshape(rows, n_seq, 2, depth)

    def features(half):
        return lax.dynamic_index_in_dim(split, half, 2, keepdims=False).reshape(rows, n_seq * depth)

    normed_mine = features(stream)
    normed_other = features(1 - stream)
    span = n_seq * depth // 2
    normed_near = lax.dynamic_slice_in_dim(normed_other, core * span, span, 1)
    normed_far = lax.dynamic_slice_in_dim(normed_other, (1 - core) * span, span, 1)

    def project(mine, near, far):
        total = jnp.dot(normed_mine, mine, preferred_element_type=jnp.float32)
        total += jnp.dot(normed_near, near, preferred_element_type=jnp.float32)
        total += jnp.dot(normed_far, far, preferred_element_type=jnp.float32)
        return total.astype(jnp.bfloat16)

    keys_values = project(kv_mine, *y_share(kv_mine, core))
    partner = lax.ppermute(keys_values, "stream", [(0, 1), (1, 0)])
    kv_width = key_weight.shape[1]
    parts = 2 if kv_width % (2 * HEAD_DIM) == 0 else 1
    step = kv_width // parts
    pieces = []
    for part in range(parts):
        columns = jnp.concatenate(
            [partner[:, part * step:(part + 1) * step],
             partner[:, kv_width + part * step:kv_width + (part + 1) * step]],
            axis=1,
        )
        pieces.append(
            lax.all_gather(columns.reshape(windows, frame_count, 2 * step), "seq", axis=1, tiled=True)
        )
    queries = project(query_mine, *y_share(query_mine, core)).reshape(windows, frame_count, -1)
    out_near = out_far = None
    width = out_weight.shape[0] // 2

    repeat = query_weight.shape[1] // key_weight.shape[1]
    chunk = frame_count // ROW_CHUNKS

    def scattered(share):
        if n_tensor == 2:
            wide = share.shape[1] // 2
            away = lax.dynamic_slice_in_dim(share, (1 - tensor) * wide, wide, 1)
            kept = lax.dynamic_slice_in_dim(share, tensor * wide, wide, 1)
            came = lax.ppermute(away, "tensor", [(0, 1), (1, 0)])
            return (kept.astype(jnp.float32) + came.astype(jnp.float32)).astype(jnp.bfloat16)
        return lax.psum_scatter(share, "tensor", scatter_dimension=1, tiled=True)

    outs = []
    q_step = step * repeat
    for window in range(windows):
        early = [
            attend(
                seq * frame_count,
                queries[window][:, part * q_step:(part + 1) * q_step],
                pieces[part][window],
                repeat,
            )
            for part in range(parts - 1)
        ]
        for index in range(ROW_CHUNKS):
            low, high = index * chunk, (index + 1) * chunk
            final = attend(
                seq * frame_count + low,
                queries[window][low:high, (parts - 1) * q_step:],
                pieces[-1][window],
                repeat,
            )
            attended = jnp.concatenate([done[low:high] for done in early] + [final], axis=1)
            share_mine = jnp.dot(attended, out_mine, preferred_element_type=jnp.float32)
            if out_near is None:
                out_near, out_far, attended = y_share(out_mine, core, attended)
            attended_near = lax.dynamic_slice_in_dim(attended, core * width, width, 1)
            attended_far = lax.dynamic_slice_in_dim(attended, (1 - core) * width, width, 1)
            share_other = jnp.dot(attended_near, out_near, preferred_element_type=jnp.float32)
            share_other += jnp.dot(attended_far, out_far, preferred_element_type=jnp.float32)
            mine = scattered(share_mine.astype(jnp.bfloat16)).reshape(chunk, -1, out_half)
            other = scattered(share_other.astype(jnp.bfloat16)).reshape(chunk, -1, out_half)
            outs.append(
                jnp.where(
                    stream == 0, jnp.stack([mine, other], axis=2), jnp.stack([other, mine], axis=2)
                ).reshape(chunk, -1)
            )
    return jnp.concatenate(outs, axis=0).reshape(1, windows, frame_count, -1)


def solution(mesh):
    in_specs = (
        P("stream", None, "seq", "tensor"),
        P(),
        P("seq", "tensor"),
        P("seq", "tensor"),
        P("seq", "tensor"),
        P("tensor", "seq"),
    )
    out_specs = P("stream", None, "seq", "tensor")
    return jax.shard_map(body, mesh=mesh, in_specs=in_specs, out_specs=out_specs, check_vma=False)
```
